32 devices in a mesh: seq: 8 (over z, x), tp: 4 (over y, core).
Axes of the slice: x: 2, y: 2, z: 4, core: 2. Of those that a mesh axis runs over, the one named last changes fastest.
Arguments:
- source: bfloat16 [8192, 1024], P('seq'), may hold values from -6 to 6
- target: bfloat16 [4096, 1024], P('seq'), may hold values from -6 to 6
- source_document: int32 [8192], replicated, may hold values from -1 to 16, as said below
- target_document: int32 [4096], replicated, may hold values from -1 to 16, as said below
- cotangent: bfloat16 [4096, 1024], P('seq'), may hold values from -6 to 6
- encoder_attention: bfloat16 [3, 1024, 1024], P(None, None, 'tp'), may hold values from -0.1875 to 0.1875
- encoder_mixing: bfloat16 [1024, 1024], P('tp'), may hold values from -1 to 1
- encoder_gains: float32 [2, 1024], replicated, may hold values from 0.1 to 1.9
- encoder_inner: bfloat16 [1024, 4096], P(None, 'tp'), may hold values from -0.1875 to 0.1875
- encoder_outer: bfloat16 [4096, 1024], P('tp'), may hold values from -0.09375 to 0.09375
- encoder_prefix: bfloat16 [2, 30, 1024], P(None, None, 'tp'), may hold values from -6 to 6
- encoder_down: bfloat16 [1024, 512], P(None, 'tp'), may hold values from -0.1875 to 0.1875
- encoder_up: bfloat16 [512, 1024], P('tp'), may hold values from -0.25 to 0.25
- decoder_attention: bfloat16 [3, 1024, 1024], P(None, None, 'tp'), may hold values from -0.1875 to 0.1875
- decoder_mixing: bfloat16 [1024, 1024], P('tp'), may hold values from -1 to 1
- decoder_prefix: bfloat16 [2, 30, 1024], P(None, None, 'tp'), may hold values from -6 to 6
- cross_query: bfloat16 [1024, 1024], P(None, 'tp'), may hold values from -0.1875 to 0.1875
- cross_memory: bfloat16 [2, 1024, 1024], P(None, None, 'tp'), may hold values from -0.1875 to 0.1875
- cross_mixing: bfloat16 [1024, 1024], P('tp'), may hold values from -1 to 1
- cross_prefix: bfloat16 [2, 30, 1024], P(None, None, 'tp'), may hold values from -6 to 6
- decoder_gains: float32 [3, 1024], replicated, may hold values from 0.1 to 1.9
- decoder_inner: bfloat16 [1024, 4096], P(None, 'tp'), may hold values from -0.1875 to 0.1875
- decoder_outer: bfloat16 [4096, 1024], P('tp'), may hold values from -0.09375 to 0.09375
- decoder_down: bfloat16 [1024, 512], P(None, 'tp'), may hold values from -0.1875 to 0.1875
- decoder_up: bfloat16 [512, 1024], P('tp'), may hold values from -0.25 to 0.25
Outputs:
- decoded: float32 [4096, 1024], P('seq')
- source_gradient: float32 [8192, 1024], P('seq')
- target_gradient: float32 [4096, 1024], P('seq')
- encoder_prefix_gradient: float32 [2, 30, 1024], P(None, None, 'tp')
- encoder_down_gradient: float32 [1024, 512], P(None, 'tp')
- encoder_up_gradient: float32 [512, 1024], P('tp')
- decoder_prefix_gradient: float32 [2, 30, 1024], P(None, None, 'tp')
- cross_prefix_gradient: float32 [2, 30, 1024], P(None, None, 'tp')
- decoder_down_gradient: float32 [1024, 512], P(None, 'tp')
- decoder_up_gradient: float32 [512, 1024], P('tp')
The draws below stay inside these ranges and needn't reach their ends.
Inputs may be any that keep to these rules, and one draw needn't show every extreme that they name: Document numbers never fall along the stream, apart from padding; a number names the same document in source_document and target_document, and every document has real slots in both. The slots of one document, in either stream, lie on one index of seq or on two neighbouring ones, the same indices in both streams, and number at most 1024 source and 512 target slots, which some document reaches in every draw; every index but the first begins with a document that began on the index before. Padding slots stand only at the end of a document. `target_document`: as for source_document.
All inputs are finite; a program needn't handle non-finite values.
Results may differ from the reference program's by a relative error of at most 0.03.
Values may be sent and summed in bfloat16 or wider, within the bound.
A program may use at most 256 MiB of HBM per device.

```python
import jax
import jax.numpy as jnp
from jax import lax

D = 1024
HEADS = 16
HEAD_DIM = 64
FF = 4096
ADAPT = 512
PREFIX = 30
GRANULES = 8
SRC_DEV = 1024
TGT_DEV = 512
SRC = 8192
TGT = 4096
N_SEQ = 8


def layout(key):
    key = jax.random.fold_in(key, 5)
    streams = jax.random.split(key, 5)
    count = SRC // SRC_DEV
    half = GRANULES // 2
    head_span = jax.random.randint(streams[0], (count,), 1, half + 1)
    tail_span = jax.random.randint(streams[1], (count,), 1, half + 1)
    chosen = jax.random.randint(streams[2], (), 1, count)
    order = jnp.arange(count, dtype=jnp.int32)
    head_span = jnp.where(order == chosen, half, head_span)
    tail_span = jnp.where(order == chosen - 1, half, tail_span)
    source_trim = jax.random.randint(streams[3], (count, 3), 1, SRC_DEV // GRANULES // 2 + 1)
    target_trim = jax.random.randint(streams[4], (count, 3), 1, TGT_DEV // GRANULES // 2 + 1)
    return (head_span, tail_span, source_trim, target_trim)


def numbering(head_span, tail_span, trim, slots):
    count = head_span.shape[0]
    granule = slots // GRANULES
    device_index = jnp.arange(count, dtype=jnp.int32)[:, None]
    places = jnp.arange(slots, dtype=jnp.int32)[None, :]
    part = places // granule
    in_head = part < head_span[:, None]
    in_tail = part >= GRANULES - tail_span[:, None]
    ident = jnp.where(in_head, 2 * device_index, jnp.where(in_tail, 2 * device_index + 2, 2 * device_index + 1))
    finish = jnp.where(in_head, head_span[:, None] * granule, jnp.where(in_tail, slots, (GRANULES - tail_span[:, None]) * granule))
    amount = jnp.where(in_head, trim[:, 0:1], jnp.where(in_tail, trim[:, 2:3], trim[:, 1:2]))
    ending = jnp.logical_not(in_tail) | (device_index == count - 1)
    padded = (places >= finish - amount) & ending
    return jnp.where(padded, -1, ident).reshape(-1).astype(jnp.int32)


def draw_source_document(key, part):
    head_span, tail_span, source_trim, target_trim = layout(key)
    return numbering(head_span, tail_span, source_trim, SRC_DEV)


def draw_target_document(key, part):
    head_span, tail_span, source_trim, target_trim = layout(key)
    return numbering(head_span, tail_span, target_trim, TGT_DEV)


def steps_of(stream_key, dims, cuts, smallest, high):
    factor_of = 1.0
    for position, shards_of in cuts:
        heights = jax.random.uniform(jax.random.fold_in(jax.random.fold_in(stream_key, 6), position), (shards_of,), jnp.float32, smallest / len(cuts), high / len(cuts))
        factor_of = factor_of * jnp.repeat(jnp.exp(heights), dims[position] // shards_of).reshape((-1,) + (1,) * (len(dims) - 1 - position))
    return factor_of


def normal_values(key, dims, scale, reach, cuts=(), kind=jnp.bfloat16):
    values = scale * jax.random.normal(key, dims, jnp.float32)
    if cuts:
        values = values * steps_of(key, dims, cuts, -0.22, 0.18)
    return jnp.clip(values, -reach, reach).astype(kind)


def setup_inputs(seed: int = 0) -> dict:
    key_of = jax.random.split(jax.random.key(seed), 26)
    return {
        "source": normal_values(key_of[0], (SRC, D), 1.0, 6.0, ((0, 8),)),
        "target": normal_values(key_of[1], (TGT, D), 1.0, 6.0, ((0, 8),)),
        "source_document": draw_source_document(jax.random.fold_in(key_of[25], 71), 0),
        "target_document": draw_target_document(jax.random.fold_in(key_of[25], 71), 0),
        "cotangent": normal_values(key_of[4], (TGT, D), 1.0, 6.0, ((0, 8),)),
        "encoder_attention": normal_values(key_of[5], (3, D, D), D ** -0.5, 0.1875, ((2, 4),)),
        "encoder_mixing": normal_values(key_of[6], (D, D), (max(2, D // 32)) ** -0.5, 1.0, ((0, 4),)),
        "encoder_gains": jnp.clip(1.0 + 0.18 * jax.random.normal(key_of[7], (2, D), jnp.float32), 0.1, 1.9),
        "encoder_inner": normal_values(key_of[8], (D, FF), D ** -0.5, 0.1875, ((1, 4),)),
        "encoder_outer": normal_values(key_of[9], (FF, D), FF ** -0.5, 0.09375, ((0, 4),)),
        "encoder_prefix": normal_values(key_of[10], (2, PREFIX, D), 1.0, 6.0, ((2, 4),)),
        "encoder_down": normal_values(key_of[11], (D, ADAPT), D ** -0.5, 0.1875, ((1, 4),)),
        "encoder_up": normal_values(key_of[12], (ADAPT, D), ADAPT ** -0.5, 0.25, ((0, 4),)),
        "decoder_attention": normal_values(key_of[13], (3, D, D), D ** -0.5, 0.1875, ((2, 4),)),
        "decoder_mixing": normal_values(key_of[14], (D, D), (max(2, D // 32)) ** -0.5, 1.0, ((0, 4),)),
        "decoder_prefix": normal_values(key_of[15], (2, PREFIX, D), 1.0, 6.0, ((2, 4),)),
        "cross_query": normal_values(key_of[16], (D, D), D ** -0.5, 0.1875, ((1, 4),)),
        "cross_memory": normal_values(key_of[17], (2, D, D), D ** -0.5, 0.1875, ((2, 4),)),
        "cross_mixing": normal_values(key_of[18], (D, D), (max(2, D // 32)) ** -0.5, 1.0, ((0, 4),)),
        "cross_prefix": normal_values(key_of[19], (2, PREFIX, D), 1.0, 6.0, ((2, 4),)),
        "decoder_gains": jnp.clip(1.0 + 0.18 * jax.random.normal(key_of[20], (3, D), jnp.float32), 0.1, 1.9),
        "decoder_inner": normal_values(key_of[21], (D, FF), D ** -0.5, 0.1875, ((1, 4),)),
        "decoder_outer": normal_values(key_of[22], (FF, D), FF ** -0.5, 0.09375, ((0, 4),)),
        "decoder_down": normal_values(key_of[23], (D, ADAPT), D ** -0.5, 0.1875, ((1, 4),)),
        "decoder_up": normal_values(key_of[24], (ADAPT, D), ADAPT ** -0.5, 0.25, ((0, 4),)),
    }


EPSILON = 1e-05
NEGATIVE = -1e+30
HIGHEST = lax.Precision.HIGHEST

@jax.custom_vjp
def low(v):
    return lax.optimization_barrier(v.astype(jnp.bfloat16)).astype(jnp.float32)

@jax.custom_vjp
def low_back(v):
    return v

def low_keep(v):
    return (low(v), None)

def low_pass(kept, grad):
    return (grad,)

def back_keep(v):
    return (v, None)

def back_low(kept, grad):
    return (low(grad),)
low.defvjp(low_keep, low_pass)
low_back.defvjp(back_keep, back_low)

def normalize(inputs, scaling):
    centered = inputs - lax.optimization_barrier(jnp.mean(inputs, axis=-1, keepdims=True))
    spread = lax.rsqrt(lax.optimization_barrier(jnp.mean(centered * centered, axis=-1, keepdims=True)) + EPSILON)
    return scaling * (centered * spread)

def product(left, right):
    return jnp.dot(left, right, precision=HIGHEST)

def exact_gelu(inputs):
    return jax.nn.gelu(inputs, approximate=False)

def attention(queries, key_rows, value_rows, prefix, query_doc, key_doc, causal):
    row_count = query_doc.shape[0] // N_SEQ
    key_count = key_doc.shape[0] // N_SEQ
    temper = HEAD_DIM ** (-0.5)
    query_blocks = queries.reshape(N_SEQ, row_count, HEADS, HEAD_DIM)
    empty_rows = jnp.zeros((key_count, HEADS * HEAD_DIM), jnp.float32)
    key_heads = jnp.concatenate([empty_rows, key_rows, empty_rows], axis=0).reshape(-1, HEADS, HEAD_DIM)
    value_heads = jnp.concatenate([empty_rows, value_rows, empty_rows], axis=0).reshape(-1, HEADS, HEAD_DIM)
    filler = jnp.full((key_count,), -1, jnp.int32)
    key_docs = jnp.concatenate([filler, key_doc.astype(jnp.int32), filler])
    prefix_keys = prefix[0].reshape(PREFIX, HEADS, HEAD_DIM)
    prefix_values = prefix[1].reshape(PREFIX, HEADS, HEAD_DIM)
    prefix_open = jnp.full((row_count, PREFIX), True)

    @jax.checkpoint
    def one_block(inputs):
        block_queries, block_doc, index = inputs
        start = (index * key_count).astype(jnp.int32)
        window_keys = lax.dynamic_slice_in_dim(key_heads, start, 3 * key_count, 0)
        window_values = lax.dynamic_slice_in_dim(value_heads, start, 3 * key_count, 0)
        window_docs = lax.dynamic_slice_in_dim(key_docs, start, 3 * key_count, 0)
        key_places = (index - 1) * key_count + jnp.arange(3 * key_count, dtype=jnp.int32)
        query_places = index * row_count + jnp.arange(row_count, dtype=jnp.int32)
        opening = jnp.einsum('qhd,phd->hqp', block_queries, prefix_keys, precision=HIGHEST)
        remaining = jnp.einsum('qhd,khd->hqk', block_queries, window_keys, precision=HIGHEST)
        scores = low_back(jnp.concatenate([opening, remaining], axis=2) * temper)
        allowed = (window_docs[None, :] == block_doc[:, None]) & (window_docs[None, :] >= 0)
        if causal:
            allowed = allowed & (key_places[None, :] <= query_places[:, None])
        allowed = jnp.concatenate([prefix_open, allowed], axis=1)
        scores = jnp.where(allowed[None], scores, NEGATIVE)
        highest = lax.optimization_barrier(jnp.max(scores, axis=2, keepdims=True))
        log_total = highest + jnp.log(lax.optimization_barrier(jnp.sum(jnp.exp(scores - highest), axis=2, keepdims=True)))
        chances = low(jnp.exp(scores - log_total))
        blended = jnp.einsum('hqp,phd->qhd', chances[:, :, :PREFIX], prefix_values, precision=HIGHEST)
        blended = blended + jnp.einsum('hqk,khd->qhd', chances[:, :, PREFIX:], window_values, precision=HIGHEST)
        return low(low_back(blended.reshape(row_count, HEADS * HEAD_DIM)))
    indices = jnp.arange(N_SEQ, dtype=jnp.int32)
    outputs = lax.map(one_block, (query_blocks, query_doc.astype(jnp.int32).reshape(N_SEQ, row_count), indices))
    return outputs.reshape(N_SEQ * row_count, HEADS * HEAD_DIM)

def attention_block(query_in, key_in, weights, prefix, query_doc, key_doc, causal):
    query_weight, key_weight, value_weight, mixing_weight = weights
    queries = low(low_back(product(query_in, query_weight)))
    key_rows = low(low_back(product(key_in, key_weight)))
    value_rows = low(low_back(product(key_in, value_weight)))
    blended = attention(queries, key_rows, value_rows, prefix, query_doc, key_doc, causal)
    return low_back(product(blended, mixing_weight))

def feed(hidden, inner_weight, outer_weight, down_weight, up_weight):
    rounded = low(hidden)
    inner_gelu = low(exact_gelu(low_back(product(rounded, inner_weight))))
    side_gelu = low(exact_gelu(low_back(product(rounded, down_weight))))
    return low_back(product(inner_gelu, outer_weight) + 4.0 * product(side_gelu, up_weight))

def reference(source, target, source_document, target_document, cotangent, encoder_attention, encoder_mixing, encoder_gains, encoder_inner, encoder_outer, encoder_prefix, encoder_down, encoder_up, decoder_attention, decoder_mixing, decoder_prefix, cross_query, cross_memory, cross_mixing, cross_prefix, decoder_gains, decoder_inner, decoder_outer, decoder_down, decoder_up):
    wide = jnp.float32
    encoder_weights = (encoder_attention[0].astype(wide), encoder_attention[1].astype(wide), encoder_attention[2].astype(wide), encoder_mixing.astype(wide))
    decoder_weights = (decoder_attention[0].astype(wide), decoder_attention[1].astype(wide), decoder_attention[2].astype(wide), decoder_mixing.astype(wide))
    cross_weights = (cross_query.astype(wide), cross_memory[0].astype(wide), cross_memory[1].astype(wide), cross_mixing.astype(wide))
    encoder_gains = encoder_gains.astype(wide)
    decoder_gains = decoder_gains.astype(wide)
    encoder_inner = encoder_inner.astype(wide)
    encoder_outer = encoder_outer.astype(wide)
    decoder_inner = decoder_inner.astype(wide)
    decoder_outer = decoder_outer.astype(wide)
    real_rows = (target_document >= 0).astype(wide)[:, None]

    def forward(source_in, target_in, encoder_prefix_in, encoder_down_in, encoder_up_in, decoder_prefix_in, cross_prefix_in, decoder_down_in, decoder_up_in):
        encoder_first = source_in + attention_block(source_in, source_in, encoder_weights, encoder_prefix_in, source_document, source_document, False)
        encoder_middle = normalize(encoder_first, encoder_gains[0])
        encoder_second = encoder_middle + feed(encoder_middle, encoder_inner, encoder_outer, encoder_down_in, encoder_up_in)
        encoded = normalize(encoder_second, encoder_gains[1])
        decoder_first = target_in + attention_block(target_in, target_in, decoder_weights, decoder_prefix_in, target_document, target_document, True)
        decoder_middle = normalize(decoder_first, decoder_gains[0])
        decoder_second = decoder_middle + attention_block(low(decoder_middle), low(encoded), cross_weights, cross_prefix_in, target_document, source_document, False)
        decoder_late = normalize(decoder_second, decoder_gains[1])
        decoder_third = decoder_late + feed(decoder_late, decoder_inner, decoder_outer, decoder_down_in, decoder_up_in)
        return normalize(decoder_third, decoder_gains[2]) * real_rows
    primals = tuple((item.astype(wide) for item in (source, target, encoder_prefix, encoder_down, encoder_up, decoder_prefix, cross_prefix, decoder_down, decoder_up)))
    result, pullback = jax.vjp(forward, *primals)
    gradients = pullback(cotangent.astype(wide))
    return (result, gradients[0], gradients[1], gradients[2], gradients[3], gradients[4], gradients[5], gradients[6], gradients[7], gradients[8])
```

```python
from functools import partial

import jax
import jax.numpy as jnp
from jax import lax
from jax.experimental import pallas as pl
from jax.experimental.pallas import tpu as pltpu
from jax.sharding import PartitionSpec as P

HEAD_DIM = 64
EPSILON = 1e-05
NEGATIVE = -1e30
HEADS = 4
KEY_BLOCK = 256
PREFIX = 30
PREFIX_ROWS = 32
SEGMENT = 64
MESH = pl.DeviceIdType.MESH
F32 = jnp.float32
BF16 = jnp.bfloat16
VMEM_BYTES = 56 * 2**20


def mm(left, right):
    return jnp.dot(left, right, preferred_element_type=F32)


def mm_nt(left, right):
    return lax.dot_general(left, right, (((1,), (1,)), ((), ())), preferred_element_type=F32)


def mm_tn(left, right):
    return lax.dot_general(left, right, (((0,), (0,)), ((), ())), preferred_element_type=F32)


def normalize(inputs, scaling):
    centered = inputs - jnp.mean(inputs, axis=-1, keepdims=True)
    spread = lax.rsqrt(jnp.mean(centered * centered, axis=-1, keepdims=True) + EPSILON)
    return scaling * (centered * spread)


def normalize_back(inputs, scaling, gradient):
    centered = inputs - jnp.mean(inputs, axis=-1, keepdims=True)
    spread = lax.rsqrt(jnp.mean(centered * centered, axis=-1, keepdims=True) + EPSILON)
    unit = centered * spread
    scaled = gradient * scaling
    first = jnp.mean(scaled, axis=-1, keepdims=True)
    second = jnp.mean(scaled * unit, axis=-1, keepdims=True)
    return spread * (scaled - first - unit * second)


def gelu_parts(inputs):
    chance = 0.5 * (1.0 + lax.erf(inputs * (0.5**0.5)))
    density = jnp.exp(-0.5 * inputs * inputs) * 0.3989422804014327
    return (inputs * chance).astype(BF16), (chance + inputs * density).astype(BF16)


def project_kernel(x_ref, w_ref, q_ref, kv_ref):
    rows = x_ref[...]
    q_ref[...] = mm(rows, w_ref[0]).astype(BF16)
    kv_ref[0] = mm(rows, w_ref[1]).astype(BF16)
    kv_ref[1] = mm(rows, w_ref[2]).astype(BF16)


def project(inputs, weights):
    rows, width = inputs.shape
    block = 256
    cols = weights.shape[2]
    return pl.pallas_call(
        project_kernel,
        grid=(rows // block,),
        in_specs=[
            pl.BlockSpec((block, width), lambda i: (i, 0)),
            pl.BlockSpec(weights.shape, lambda i: (0, 0, 0)),
        ],
        out_specs=[
            pl.BlockSpec((block, cols), lambda i: (i, 0)),
            pl.BlockSpec((2, block, cols), lambda i: (0, i, 0)),
        ],
        out_shape=[
            jax.ShapeDtypeStruct((rows, cols), BF16),
            jax.ShapeDtypeStruct((2, rows, cols), BF16),
        ],
        compiler_params=pltpu.CompilerParams(vmem_limit_bytes=VMEM_BYTES),
        cost_estimate=pl.CostEstimate(
            flops=6 * rows * width * cols, bytes_accessed=8 * rows * cols + 6 * width * cols, transcendentals=0
        ),
    )(inputs, weights)


def by_heads(rows, lane_head):
    zero = jnp.zeros_like(rows)
    return jnp.concatenate([jnp.where(lane_head == h, rows, zero) for h in range(HEADS)], axis=0)


def head_bias(kd_ref, qd_ref, start, first_query, halo, block, causal):
    key_doc = kd_ref[pl.ds(start, KEY_BLOCK), :]
    allowed = key_doc == qd_ref[0]
    if causal:
        key_place = start - halo + lax.broadcasted_iota(jnp.int32, (KEY_BLOCK, block), 0)
        query_place = first_query + lax.broadcasted_iota(jnp.int32, (KEY_BLOCK, block), 1)
        allowed = allowed & (key_place <= query_place)
    bias = jnp.where(allowed, 0.0, NEGATIVE)
    return jnp.concatenate([bias] * HEADS, axis=1)


def prefix_scores(pre_ref, stacked):
    scores = mm_nt(pre_ref[0], stacked)
    row = lax.broadcasted_iota(jnp.int32, scores.shape, 0)
    return jnp.where(row < PREFIX, scores, NEGATIVE)


def fill_window(window, parts, index):
    at = 0
    for part in parts:
        size = part.shape[1]
        window[at : at + size, :] = part[index]
        at += size


def attend_kernel(
    halo, causal, lo_ref, hi_ref, q_ref, bef_ref, own_ref, aft_ref, pre_ref, qd_ref, kd_ref,
    wide_ref, low_ref, total_ref, keys, values, blended,
):
    i = pl.program_id(0)
    block = q_ref.shape[0]
    parts = (bef_ref, own_ref, aft_ref)

    @pl.when(i == 0)
    def _():
        fill_window(keys, parts, 0)
        at = 0
        for part in parts:
            for k in range(part.shape[1] // KEY_BLOCK):
                values[at] = part[1, k * KEY_BLOCK : (k + 1) * KEY_BLOCK, :].T
                at += 1

    lane_head = lax.broadcasted_iota(jnp.int32, q_ref.shape, 1) // HEAD_DIM
    stacked = by_heads(q_ref[...] * jnp.asarray(HEAD_DIM**-0.5, BF16), lane_head)
    scores = prefix_scores(pre_ref, stacked)
    highest = jnp.max(scores, axis=0, keepdims=True)
    chances = jnp.exp(scores - highest)
    summed = jnp.sum(chances, axis=0, keepdims=True)
    low = chances.astype(BF16)
    pre_values = pre_ref[1].T
    for h in range(HEADS):
        rows = slice(h * HEAD_DIM, (h + 1) * HEAD_DIM)
        blended[rows, :] = mm(pre_values[rows, :], low[:, h * block : (h + 1) * block])

    def step(kb, carry):
        highest, summed = carry
        start = pl.multiple_of(kb * KEY_BLOCK, KEY_BLOCK)
        scores = mm_nt(keys[pl.ds(start, KEY_BLOCK), :], stacked)
        scores = scores + head_bias(kd_ref, qd_ref, start, i * block, halo, block, causal)
        top = jnp.maximum(highest, jnp.max(scores, axis=0, keepdims=True))
        fade = jnp.exp(highest - top)
        chances = jnp.exp(scores - top)
        summed = summed * fade + jnp.sum(chances, axis=0, keepdims=True)
        low = chances.astype(BF16)
        for h in range(HEADS):
            rows = slice(h * HEAD_DIM, (h + 1) * HEAD_DIM)
            cols = slice(h * block, (h + 1) * block)
            blended[rows, :] = blended[rows, :] * fade[:, cols] + mm(values[kb, rows, :], low[:, cols])
        return top, summed

    highest, summed = lax.fori_loop(lo_ref[i], hi_ref[i], step, (highest, summed))
    total_ref[0] = highest + jnp.log(summed)
    inverse = 1.0 / summed
    for h in range(HEADS):
        rows = slice(h * HEAD_DIM, (h + 1) * HEAD_DIM)
        blended[rows, :] = blended[rows, :] * inverse[:, h * block : (h + 1) * block]
    result = blended[...].T
    wide_ref[...] = result
    low_ref[...] = result.astype(BF16)


def attend(queries, parts, prefix, docs, causal):
    query_doc, key_doc, lo, hi = docs
    rows, cols = queries.shape
    count, _, block = query_doc.shape
    window = key_doc.shape[0]
    halo = parts[0].shape[1]

    def whole(array):
        return pl.BlockSpec(array.shape, lambda i, *_: (0,) * array.ndim)

    return pl.pallas_call(
        partial(attend_kernel, halo, causal),
        grid_spec=pltpu.PrefetchScalarGridSpec(
            num_scalar_prefetch=2,
            grid=(count,),
            in_specs=[
                pl.BlockSpec((block, cols), lambda i, *_: (i, 0)),
                whole(parts[0]),
                whole(parts[1]),
                whole(parts[2]),
                whole(prefix),
                pl.BlockSpec((1, 1, block), lambda i, *_: (i, 0, 0)),
                whole(key_doc),
            ],
            out_specs=[
                pl.BlockSpec((block, cols), lambda i, *_: (i, 0)),
                pl.BlockSpec((block, cols), lambda i, *_: (i, 0)),
                pl.BlockSpec((1, 1, HEADS * block), lambda i, *_: (i, 0, 0)),
            ],
            scratch_shapes=[
                pltpu.VMEM((window, cols), BF16),
                pltpu.VMEM((window // KEY_BLOCK, cols, KEY_BLOCK), BF16),
                pltpu.VMEM((cols, block), F32),
            ],
        ),
        out_shape=[
            jax.ShapeDtypeStruct((rows, cols), F32),
            jax.ShapeDtypeStruct((rows, cols), BF16),
            jax.ShapeDtypeStruct((count, 1, HEADS * block), F32),
        ],
        compiler_params=pltpu.CompilerParams(vmem_limit_bytes=VMEM_BYTES),
        cost_estimate=pl.CostEstimate(
            flops=16 * rows * 1024 * cols, bytes_accessed=8 * window * cols, transcendentals=4 * rows * 1024
        ),
    )(lo, hi, queries, *parts, prefix, query_doc, key_doc)


def attend_back_kernel(
    halo, causal, lo_ref, hi_ref, q_ref, g_ref, wide_ref, total_ref, bef_ref, own_ref, aft_ref, pre_ref,
    qd_ref, kd_ref, dq_ref, dbef_ref, down_ref, daft_ref, dpre_ref,
    keys, values, turned, key_sum, value_sum, query_sum, prefix_sum,
):
    i = pl.program_id(0)
    block = q_ref.shape[0]
    parts = (bef_ref, own_ref, aft_ref)

    @pl.when(i == 0)
    def _():
        fill_window(keys, parts, 0)
        fill_window(values, parts, 1)
        at = 0
        for part in parts:
            for k in range(part.shape[1] // KEY_BLOCK):
                turned[at] = part[0, k * KEY_BLOCK : (k + 1) * KEY_BLOCK, :].T
                at += 1
        key_sum[...] = jnp.zeros_like(key_sum)
        value_sum[...] = jnp.zeros_like(value_sum)
        prefix_sum[...] = jnp.zeros_like(prefix_sum)

    lane_head = lax.broadcasted_iota(jnp.int32, q_ref.shape, 1) // HEAD_DIM
    stacked = by_heads(q_ref[...] * jnp.asarray(HEAD_DIM**-0.5, BF16), lane_head)
    grads = by_heads(g_ref[...], lane_head)
    mixed = (g_ref[...].astype(F32) * wide_ref[...]).T
    offsets = jnp.concatenate(
        [
            jnp.sum(mixed[h * HEAD_DIM : (h + 1) * HEAD_DIM, :], axis=0, keepdims=True)
            for h in range(HEADS)
        ],
        axis=1,
    )
    total = total_ref[0]
    chances = jnp.exp(prefix_scores(pre_ref, stacked) - total)
    score_grad = (chances * (mm_nt(pre_ref[1], grads) - offsets)).astype(BF16)
    prefix_sum[0] += mm(score_grad, stacked)
    prefix_sum[1] += mm(chances.astype(BF16), grads)
    pre_keys = pre_ref[0].T
    for h in range(HEADS):
        rows = slice(h * HEAD_DIM, (h + 1) * HEAD_DIM)
        query_sum[rows, :] = mm(pre_keys[rows, :], score_grad[:, h * block : (h + 1) * block])

    def step(kb, carry):
        start = pl.multiple_of(kb * KEY_BLOCK, KEY_BLOCK)
        here = pl.ds(start, KEY_BLOCK)
        scores = mm_nt(keys[here, :], stacked)
        scores = scores + head_bias(kd_ref, qd_ref, start, i * block, halo, block, causal)
        chances = jnp.exp(scores - total)
        score_grad = (chances * (mm_nt(values[here, :], grads) - offsets)).astype(BF16)
        key_sum[here, :] += mm(score_grad, stacked)
        value_sum[here, :] += mm(chances.astype(BF16), grads)
        for h in range(HEADS):
            rows = slice(h * HEAD_DIM, (h + 1) * HEAD_DIM)
            query_sum[rows, :] += mm(turned[kb, rows, :], score_grad[:, h * block : (h + 1) * block])
        return carry

    lax.fori_loop(lo_ref[i], hi_ref[i], step, 0)
    dq_ref[...] = (query_sum[...].T * HEAD_DIM**-0.5).astype(BF16)

    @pl.when(i == pl.num_programs(0) - 1)
    def _():
        at = 0
        for part in (dbef_ref, down_ref, daft_ref):
            size = part.shape[1]
            part[0] = key_sum[at : at + size, :].astype(part.dtype)
            part[1] = value_sum[at : at + size, :].astype(part.dtype)
            at += size
        dpre_ref[...] = prefix_sum[...]


def attend_back(queries, grads, wide, total, parts, prefix, docs, causal):
    query_doc, key_doc, lo, hi = docs
    rows, cols = queries.shape
    count, _, block = query_doc.shape
    window = key_doc.shape[0]
    halo = parts[0].shape[1]

    def whole(shape):
        return pl.BlockSpec(shape, lambda i, *_: (0,) * len(shape))

    def blocked():
        return pl.BlockSpec((block, cols), lambda i, *_: (i, 0))

    return pl.pallas_call(
        partial(attend_back_kernel, halo, causal),
        grid_spec=pltpu.PrefetchScalarGridSpec(
            num_scalar_prefetch=2,
            grid=(count,),
            in_specs=[
                blocked(),
                blocked(),
                blocked(),
                pl.BlockSpec((1, 1, HEADS * block), lambda i, *_: (i, 0, 0)),
                whole(parts[0].shape),
                whole(parts[1].shape),
                whole(parts[2].shape),
                whole(prefix.shape),
                pl.BlockSpec((1, 1, block), lambda i, *_: (i, 0, 0)),
                whole(key_doc.shape),
            ],
            out_specs=[
                blocked(),
                whole(parts[0].shape),
                whole(parts[1].shape),
                whole(parts[2].shape),
                whole(prefix.shape),
            ],
            scratch_shapes=[
                pltpu.VMEM((window, cols), BF16),
                pltpu.VMEM((window, cols), BF16),
                pltpu.VMEM((window // KEY_BLOCK, cols, KEY_BLOCK), BF16),
                pltpu.VMEM((window, cols), F32),
                pltpu.VMEM((window, cols), F32),
                pltpu.VMEM((cols, block), F32),
                pltpu.VMEM(prefix.shape, F32),
            ],
        ),
        out_shape=[
            jax.ShapeDtypeStruct((rows, cols), BF16),
            jax.ShapeDtypeStruct(parts[0].shape, BF16),
            jax.ShapeDtypeStruct(parts[1].shape, F32),
            jax.ShapeDtypeStruct(parts[2].shape, BF16),
            jax.ShapeDtypeStruct(prefix.shape, F32),
        ],
        compiler_params=pltpu.CompilerParams(vmem_limit_bytes=VMEM_BYTES),
        cost_estimate=pl.CostEstimate(
            flops=40 * rows * 1024 * cols, bytes_accessed=16 * window * cols, transcendentals=4 * rows * 1024
        ),
    )(lo, hi, queries, grads, wide, total, *parts, prefix, query_doc, key_doc)


class Place:
    def __init__(self, n_seq):
        self.s = lax.axis_index("seq")
        self.t = lax.axis_index("tp")
        self.core = self.t % 2
        self.other = 1 - self.core
        self.twin_t = self.t + 1 - 2 * self.core
        self.across_t = (self.t + 2) % 4
        self.corner_t = 3 - self.t
        self.twin = (self.s, self.twin_t)
        self.across = (self.s, self.across_t)
        self.corner = (self.s, self.corner_t)
        self.after = ((self.s + 1) % n_seq, self.t)
        self.before = ((self.s + n_seq - 1) % n_seq, self.t)

    def greet(self, partners):
        barrier = pltpu.get_barrier_semaphore()
        for partner in partners:
            pl.semaphore_signal(barrier, inc=1, device_id=partner, device_id_type=MESH)
        pl.semaphore_wait(barrier, len(partners))


class Sems:
    def __init__(self, send, receive):
        self.send, self.receive, self.used = send, receive, 0

    def take(self):
        kind = self.used
        self.used += 1
        return kind


def remote(sems, kind, j, src, dst, device):
    return pltpu.make_async_remote_copy(
        src_ref=src,
        dst_ref=dst,
        send_sem=sems.send.at[kind, j],
        recv_sem=sems.receive.at[kind, j],
        device_id=device,
        device_id_type=MESH,
    )


def span(j):
    return pl.ds(pl.multiple_of(j * SEGMENT, SEGMENT), SEGMENT)


class Twins:
    def __init__(self, place, sems, buf):
        self.place, self.sems, self.buf, self.kind = place, sems, buf, sems.take()

    def copy(self, j, half):
        part = self.buf.at[half, span(j)]
        return remote(self.sems, self.kind, j, part, part, self.place.twin)

    def put(self, j, value):
        self.buf[self.place.core, span(j)] = value
        self.copy(j, self.place.core).start()

    def wait(self, j):
        self.copy(j, self.place.other).wait_recv()

    def both(self, j):
        return jnp.concatenate([self.buf[self.place.core, span(j)], self.buf[self.place.other, span(j)]], axis=0)

    def drain(self, j):
        self.copy(j, self.place.core).wait_send()


class Total:
    SHAPES = staticmethod(
        lambda half: [
            pltpu.VMEM((half, 1024), F32),
            pltpu.VMEM((half, 1024), BF16),
            pltpu.VMEM((half, 1024), BF16),
            pltpu.VMEM((half, 1024), BF16),
            pltpu.VMEM((half, 1024), BF16),
        ]
    )

    def __init__(self, place, sems, refs):
        self.place, self.sems = place, sems
        self.mine, self.away, self.came, self.chip, self.far = refs
        self.kind_twin, self.kind_across = sems.take(), sems.take()

    def twin_copy(self, j):
        rows = span(j)
        return remote(self.sems, self.kind_twin, j, self.away.at[rows], self.came.at[rows], self.place.twin)

    def across_copy(self, j):
        rows = span(j)
        return remote(self.sems, self.kind_across, j, self.chip.at[rows], self.far.at[rows], self.place.across)

    def put(self, j, value):
        self.mine[span(j)] = value[:SEGMENT]
        self.away[span(j)] = value[SEGMENT:].astype(BF16)
        self.twin_copy(j).start()

    def middle(self, j):
        self.twin_copy(j).wait_recv()
        self.chip[span(j)] = (self.mine[span(j)] + self.came[span(j)].astype(F32)).astype(BF16)
        self.across_copy(j).start()

    def get(self, j):
        self.across_copy(j).wait_recv()
        return self.chip[span(j)].astype(F32) + self.far[span(j)].astype(F32)

    def drain(self, j):
        self.twin_copy(j).wait_send()
        self.across_copy(j).wait_send()


class Heads:
    def __init__(self, place, sems, own, buf):
        self.place, self.sems, self.own, self.buf = place, sems, own, buf
        self.kinds = [sems.take() for _ in range(3)]

    def copies(self, j):
        p, rows = self.place, span(j)
        landing = self.buf.at[p.t, rows]
        return [
            remote(self.sems, self.kinds[0], j, self.own.at[p.core, rows], landing, p.across),
            remote(self.sems, self.kinds[1], j, self.own.at[p.other, rows], landing, p.corner),
            remote(self.sems, self.kinds[2], j, self.own.at[p.other, rows], landing, p.twin),
        ]

    def send(self, j):
        for copy in self.copies(j):
            copy.start()
        self.buf[self.place.t, span(j)] = self.own[self.place.core, span(j)]

    def wait(self, j):
        p, rows = self.place, span(j)
        for kind, source, device in zip(
            self.kinds, (p.across_t, p.corner_t, p.twin_t), (p.across, p.corner, p.twin)
        ):
            part = self.buf.at[source, rows]
            remote(self.sems, kind, j, part, part, device).wait_recv()

    def mix(self, j, weight):
        rows = span(j)
        total = mm(self.buf[0, rows], weight[0])
        for k in range(1, 4):
            total = total + mm(self.buf[k, rows], weight[k])
        return total

    def drain(self, j):
        for copy in self.copies(j):
            copy.wait_send()


class Halo:
    def __init__(self, place, sems, rows, halo):
        self.place, self.sems, self.rows, self.halo = place, sems, rows, halo
        self.half = rows // 2
        self.up = [sems.take() if hh * self.half >= rows - halo else None for hh in range(2)]
        self.down = [sems.take() if hh * self.half < halo else None for hh in range(2)]

    def place_up(self, hh, j):
        return span(j + (hh * self.half - (self.rows - self.halo)) // SEGMENT)

    def place_down(self, hh, j):
        return span(j + hh * self.half // SEGMENT)

    def out_copies(self, j, own, before, after):
        copies = []
        for hh in range(2):
            src = own.at[:, self.place_down(hh, j)]
            if self.up[hh] is not None:
                dst = before.at[:, self.place_up(hh, j)]
                copies.append(remote(self.sems, self.up[hh], j, src, dst, self.place.after))
            if self.down[hh] is not None:
                dst = after.at[:, self.place_down(hh, j)]
                copies.append(remote(self.sems, self.down[hh], j, src, dst, self.place.before))
        return copies

    def back_copies(self, j, before, after, from_before, from_after):
        copies = []
        for hh in range(2):
            if self.up[hh] is not None:
                where = self.place_up(hh, j)
                copies.append(
                    remote(self.sems, self.up[hh], j, before.at[:, where], from_after.at[:, where], self.place.before)
                )
            if self.down[hh] is not None:
                where = self.place_down(hh, j)
                copies.append(
                    remote(self.sems, self.down[hh], j, after.at[:, where], from_before.at[:, where], self.place.after)
                )
        return copies

    def gathered(self, j, hh, own, from_before, from_after):
        total = own[:, self.place_down(hh, j)]
        if self.down[hh] is not None:
            total = total + from_before[:, self.place_down(hh, j)].astype(F32)
        if self.up[hh] is not None:
            total = total + from_after[:, self.place_up(hh, j)].astype(F32)
        return total


def pipeline(n, stages):
    last = max(delay for delay, _ in stages)

    def step(s, carry):
        for delay, stage in stages:
            pl.when((s >= delay) & (s < n + delay))(partial(stage, s - delay))
        return carry

    lax.fori_loop(0, n + last, step, 0)


def each(n, *actions):
    def step(j, carry):
        for action in actions:
            action(j)
        return carry

    lax.fori_loop(0, n, step, 0)


def exchange_call(kernel, cid, outs, scratch, kinds, n, flops, args):
    vmem = pl.BlockSpec(memory_space=pltpu.VMEM)
    moved = sum(a.size * a.dtype.itemsize for a in args)
    return pl.pallas_call(
        kernel,
        in_specs=[vmem] * len(args),
        out_specs=[vmem] * len(outs),
        out_shape=[jax.ShapeDtypeStruct(shape, kind) for shape, kind in outs],
        scratch_shapes=scratch + [pltpu.SemaphoreType.DMA((kinds, n)), pltpu.SemaphoreType.DMA((kinds, n))],
        compiler_params=pltpu.CompilerParams(
            collective_id=cid, has_side_effects=True, vmem_limit_bytes=VMEM_BYTES
        ),
        cost_estimate=pl.CostEstimate(flops=flops, bytes_accessed=moved, transcendentals=0),
    )(*args)


def feed_rows(rows, w1, w2, wd, wu):
    inner, inner_slope = gelu_parts(mm(rows, w1[...]))
    side, side_slope = gelu_parts(mm(rows, wd[...]))
    return mm(inner, w2[...]) + 4.0 * mm(side, wu[...]), inner_slope, side, side_slope


def feed_rows_back(grads, rows, inner_slope, side, side_slope, w1, w2, wd, wu):
    four = (4.0 * grads.astype(F32)).astype(BF16)
    grad_inner = (inner_slope.astype(F32) * mm_nt(grads, w2[...])).astype(BF16)
    grad_side = (side_slope.astype(F32) * mm_nt(four, wu[...])).astype(BF16)
    piece = mm_nt(grad_inner, w1[...]) + mm_nt(grad_side, wd[...])
    return piece, mm_tn(rows, grad_side), mm_tn(side, four)


def encoder_forward_kernel(
    n_seq, halo_rows, a, x, gains, wo, w1, w2, wd, wu, wkv,
    e1, e3, hidden, inner_slope, side, side_slope, kv, before, after,
    heads_buf, e2, s0, s1, s2, s3, s4, encoded, send, receive,
):
    place, sems = Place(n_seq), Sems(send, receive)
    half = e1.shape[0]
    n = half // SEGMENT
    heads = Heads(place, sems, a, heads_buf)
    low = Twins(place, sems, hidden)
    total = Total(place, sems, (s0, s1, s2, s3, s4))
    low_encoded = Twins(place, sems, encoded)
    halo = Halo(place, sems, 2 * half, halo_rows)
    place.greet([place.twin, place.across, place.corner, place.before, place.after])
    each(n, heads.send)

    def mix(j):
        heads.wait(j)
        rows = span(j)
        first = x[place.core, rows].astype(F32) + heads.mix(j, wo)
        e1[rows] = first
        middle = normalize(first, gains[0:1])
        e2[rows] = middle
        low.put(j, middle.astype(BF16))

    def feed(j):
        low.wait(j)
        piece, slope, side_rows, slope_side = feed_rows(low.both(j), w1, w2, wd, wu)
        inner_slope[j] = slope
        side[j] = side_rows
        side_slope[j] = slope_side
        total.put(j, piece)

    def finish(j):
        rows = span(j)
        second = e2[rows] + total.get(j)
        e3[rows] = second
        low_encoded.put(j, normalize(second, gains[1:2]).astype(BF16))

    def memory(j):
        low_encoded.wait(j)
        rows = low_encoded.both(j)
        for i in range(2):
            made = mm(rows, wkv[i]).astype(BF16)
            kv[i, span(j + place.core * n)] = made[:SEGMENT]
            kv[i, span(j + place.other * n)] = made[SEGMENT:]
        for copy in halo.out_copies(j, kv, before, after):
            copy.start()

    pipeline(n, [(2, total.middle), (0, mix), (1, feed), (4, finish), (5, memory)])

    def arrived(j):
        for copy in halo.out_copies(j, kv, before, after):
            copy.wait()

    each(n, heads.drain, low.drain, total.drain, low_encoded.drain, arrived)


def decoder_self_kernel(n_seq, a, x, gains, wo, wq, t1, t2, q, heads_buf, hidden, send, receive):
    place, sems = Place(n_seq), Sems(send, receive)
    half = t1.shape[0]
    n = half // SEGMENT
    heads = Heads(place, sems, a, heads_buf)
    low = Twins(place, sems, hidden)
    place.greet([place.twin, place.across, place.corner])
    each(n, heads.send)

    def mix(j):
        heads.wait(j)
        rows = span(j)
        first = x[place.core, rows].astype(F32) + heads.mix(j, wo)
        t1[rows] = first
        middle = normalize(first, gains[0:1])
        t2[rows] = middle
        low.put(j, middle.astype(BF16))

    def query(j):
        low.wait(j)
        made = mm(low.both(j), wq[...]).astype(BF16)
        q[place.core, span(j)] = made[:SEGMENT]
        q[place.other, span(j)] = made[SEGMENT:]

    pipeline(n, [(0, mix), (1, query)])
    each(n, heads.drain, low.drain)


def decoder_chain_kernel(
    n_seq, a, t2, real, cotangent, gains, wo, w1, w2, wd, wu, mixing,
    decoded, g2, da, down_grad, up_grad,
    heads_buf, t3, t4, g3, hidden, low_g3, low_g2, inner_slope, side, side_slope,
    f0, f1, f2, f3, f4, b0, b1, b2, b3, b4, send, receive,
):
    place, sems = Place(n_seq), Sems(send, receive)
    half = t2.shape[0]
    n = half // SEGMENT
    heads = Heads(place, sems, a, heads_buf)
    low = Twins(place, sems, hidden)
    ahead = Total(place, sems, (f0, f1, f2, f3, f4))
    result = Twins(place, sems, decoded)
    back3 = Twins(place, sems, low_g3)
    behind = Total(place, sems, (b0, b1, b2, b3, b4))
    back2 = Twins(place, sems, low_g2)
    place.greet([place.twin, place.across, place.corner])
    each(n, heads.send)
    down_grad[...] = jnp.zeros_like(down_grad)
    up_grad[...] = jnp.zeros_like(up_grad)

    def mix(j):
        heads.wait(j)
        rows = span(j)
        second = t2[rows] + heads.mix(j, wo)
        t3[rows] = second
        late = normalize(second, gains[1:2])
        t4[rows] = late
        low.put(j, late.astype(BF16))

    def feed(j):
        low.wait(j)
        piece, slope, side_rows, slope_side = feed_rows(low.both(j), w1, w2, wd, wu)
        inner_slope[j] = slope
        side[j] = side_rows
        side_slope[j] = slope_side
        ahead.put(j, piece)

    def turn(j):
        rows = span(j)
        third = t4[rows] + ahead.get(j)
        mask = real[place.core, rows]
        result.put(j, normalize(third, gains[2:3]) * mask)
        grad = normalize_back(third, gains[2:3], cotangent[place.core, rows].astype(F32) * mask)
        g3[rows] = grad
        back3.put(j, grad.astype(BF16))

    def feed_back(j):
        back3.wait(j)
        piece, down, up = feed_rows_back(
            back3.both(j), low.both(j), inner_slope[j], side[j], side_slope[j], w1, w2, wd, wu
        )
        down_grad[...] += down
        up_grad[...] += up
        behind.put(j, piece)

    def finish(j):
        rows = span(j)
        grad = normalize_back(t3[rows], gains[1:2], g3[rows] + behind.get(j))
        g2[rows] = grad
        back2.put(j, grad.astype(BF16))

    def heads_back(j):
        back2.wait(j)
        made = mm_nt(back2.both(j), mixing[...]).astype(BF16)
        da[place.core, span(j)] = made[:SEGMENT]
        da[place.other, span(j)] = made[SEGMENT:]

    pipeline(
        n,
        [
            (2, ahead.middle),
            (6, behind.middle),
            (0, mix),
            (1, feed),
            (4, turn),
            (5, feed_back),
            (8, finish),
            (9, heads_back),
        ],
    )
    each(
        n, heads.drain, low.drain, ahead.drain, result.drain, result.wait, back3.drain, behind.drain, back2.drain
    )


def decoder_query_back_kernel(
    n_seq, dq, g2, t1, gains, wq, mixing, g1, da, low_g1, s0, s1, s2, s3, s4, send, receive
):
    place, sems = Place(n_seq), Sems(send, receive)
    half = t1.shape[0]
    n = half // SEGMENT
    total = Total(place, sems, (s0, s1, s2, s3, s4))
    back = Twins(place, sems, low_g1)
    place.greet([place.twin, place.across])

    def start(j):
        rows = jnp.concatenate([dq[place.core, span(j)], dq[place.other, span(j)]], axis=0)
        total.put(j, mm_nt(rows, wq[...]))

    def finish(j):
        rows = span(j)
        grad = normalize_back(t1[rows], gains[0:1], g2[rows] + total.get(j))
        g1[rows] = grad
        back.put(j, grad.astype(BF16))

    def heads_back(j):
        back.wait(j)
        made = mm_nt(back.both(j), mixing[...]).astype(BF16)
        da[place.core, span(j)] = made[:SEGMENT]
        da[place.other, span(j)] = made[SEGMENT:]

    pipeline(n, [(0, start), (1, total.middle), (3, finish), (4, heads_back)])
    each(n, total.drain, back.drain)


def key_rows(place, halo, j, scratch, own, from_before, from_after):
    for hh in range(2):
        scratch[hh] = halo.gathered(j, hh, own, from_before, from_after).astype(BF16)
    return [
        jnp.concatenate([scratch[place.core, i], scratch[place.other, i]], axis=0) for i in range(2)
    ]


def encoder_back_kernel(
    n_seq, halo_rows, dkv, dbefore, dafter, wkv, e3, e1, gains, hidden, inner_slope, side, side_slope,
    w1, w2, wd, wu, mixing,
    g1, da, down_grad, up_grad,
    from_before, from_after, rounded, g2, low_g2, low_g1,
    f0, f1, f2, f3, f4, b0, b1, b2, b3, b4, send, receive,
):
    place, sems = Place(n_seq), Sems(send, receive)
    half = e1.shape[0]
    n = half // SEGMENT
    halo = Halo(place, sems, 2 * half, halo_rows)
    first = Total(place, sems, (f0, f1, f2, f3, f4))
    back2 = Twins(place, sems, low_g2)
    second = Total(place, sems, (b0, b1, b2, b3, b4))
    back1 = Twins(place, sems, low_g1)
    place.greet([place.twin, place.across, place.before, place.after])

    def leave(j):
        for copy in halo.back_copies(j, dbefore, dafter, from_before, from_after):
            copy.start()

    each(n, leave)
    down_grad[...] = jnp.zeros_like(down_grad)
    up_grad[...] = jnp.zeros_like(up_grad)

    def start(j):
        for copy in halo.back_copies(j, dbefore, dafter, from_before, from_after):
            copy.wait_recv()
        key_grad, value_grad = key_rows(place, halo, j, rounded, dkv, from_before, from_after)
        first.put(j, mm_nt(key_grad, wkv[0]) + mm_nt(value_grad, wkv[1]))

    def turn(j):
        rows = span(j)
        grad = normalize_back(e3[rows], gains[1:2], first.get(j))
        g2[rows] = grad
        back2.put(j, grad.astype(BF16))

    def feed_back(j):
        back2.wait(j)
        rows = jnp.concatenate([hidden[place.core, span(j)], hidden[place.other, span(j)]], axis=0)
        piece, down, up = feed_rows_back(
            back2.both(j), rows, inner_slope[j], side[j], side_slope[j], w1, w2, wd, wu
        )
        down_grad[...] += down
        up_grad[...] += up
        second.put(j, piece)

    def finish(j):
        rows = span(j)
        grad = normalize_back(e1[rows], gains[0:1], g2[rows] + second.get(j))
        g1[rows] = grad
        back1.put(j, grad.astype(BF16))

    def heads_back(j):
        back1.wait(j)
        made = mm_nt(back1.both(j), mixing[...]).astype(BF16)
        da[place.core, span(j)] = made[:SEGMENT]
        da[place.other, span(j)] = made[SEGMENT:]

    pipeline(
        n,
        [
            (1, first.middle),
            (5, second.middle),
            (0, start),
            (3, turn),
            (4, feed_back),
            (7, finish),
            (8, heads_back),
        ],
    )

    def left(j):
        for copy in halo.back_copies(j, dbefore, dafter, from_before, from_after):
            copy.wait_send()

    each(n, left, first.drain, back2.drain, second.drain, back1.drain)


def input_back_kernel(
    n_seq, halo_rows, dq, dkv, dbefore, dafter, weights, g1,
    gradient, from_before, from_after, rounded, s0, s1, s2, s3, s4, send, receive,
):
    place, sems = Place(n_seq), Sems(send, receive)
    half = g1.shape[0]
    n = half // SEGMENT
    halo = Halo(place, sems, 2 * half, halo_rows)
    total = Total(place, sems, (s0, s1, s2, s3, s4))
    result = Twins(place, sems, gradient)
    place.greet([place.twin, place.across, place.before, place.after])

    def leave(j):
        for copy in halo.back_copies(j, dbefore, dafter, from_before, from_after):
            copy.start()

    each(n, leave)

    def start(j):
        for copy in halo.back_copies(j, dbefore, dafter, from_before, from_after):
            copy.wait_recv()
        key_grad, value_grad = key_rows(place, halo, j, rounded, dkv, from_before, from_after)
        query_grad = jnp.concatenate([dq[place.core, span(j)], dq[place.other, span(j)]], axis=0)
        total.put(
            j, mm_nt(query_grad, weights[0]) + mm_nt(key_grad, weights[1]) + mm_nt(value_grad, weights[2])
        )

    def finish(j):
        result.put(j, g1[span(j)] + total.get(j))

    pipeline(n, [(1, total.middle), (0, start), (3, finish)])

    def left(j):
        for copy in halo.back_copies(j, dbefore, dafter, from_before, from_after):
            copy.wait_send()

    each(n, left, total.drain, result.drain, result.wait)


def document_plan(query_docs, key_docs, query_rows, key_rows_, halo, block, causal):
    s = lax.axis_index("seq")
    own = lax.dynamic_slice_in_dim(query_docs, s * query_rows, query_rows)
    filler = jnp.full((halo,), -1, jnp.int32)
    padded = jnp.concatenate([filler, key_docs, filler])
    window = key_rows_ + 2 * halo
    keys = lax.dynamic_slice_in_dim(padded, s * key_rows_, window)
    blocks = own.reshape(-1, block)
    top = jnp.max(blocks, axis=1)
    bottom = jnp.min(jnp.where(blocks >= 0, blocks, 2**30), axis=1)
    read = (keys[None] >= bottom[:, None]) & (keys[None] <= top[:, None])
    index = jnp.arange(window, dtype=jnp.int32)[None]
    lo = jnp.min(jnp.where(read, index, window), axis=1) // KEY_BLOCK
    hi = (jnp.max(jnp.where(read, index + 1, 0), axis=1) + KEY_BLOCK - 1) // KEY_BLOCK
    if causal:
        ends = halo + block * (1 + jnp.arange(blocks.shape[0], dtype=jnp.int32))
        hi = jnp.minimum(hi, (ends + KEY_BLOCK - 1) // KEY_BLOCK)
    rows = jnp.where(blocks >= 0, blocks, -2)[:, None, :]
    return rows, keys[:, None], lo, hi


def halo_parts(kv, halo):
    size = lax.axis_size("seq")
    rows = kv.shape[1]
    up = [(i, i + 1) for i in range(size - 1)]
    down = [(i + 1, i) for i in range(size - 1)]
    before = lax.ppermute(kv[:, rows - halo :], "seq", up)
    after = lax.ppermute(kv[:, :halo], "seq", down)
    return before, kv, after


def halves(array):
    return array.reshape((2, array.shape[0] // 2) + array.shape[1:])


def exchange_scratch(half, *kinds):
    shapes = []
    for kind in kinds:
        if kind == "total":
            shapes += Total.SHAPES(half)
        else:
            shape, dtype = kind
            shapes.append(pltpu.VMEM(shape, dtype))
    return shapes


def on_device(
    n_seq,
    wide,
    source,
    target,
    source_document,
    target_document,
    cotangent,
    encoder_attention,
    encoder_mixing,
    encoder_gains,
    encoder_inner,
    encoder_outer,
    encoder_prefix,
    encoder_down,
    encoder_up,
    decoder_attention,
    decoder_mixing,
    decoder_prefix,
    cross_query,
    cross_memory,
    cross_mixing,
    cross_prefix,
    decoder_gains,
    decoder_inner,
    decoder_outer,
    decoder_down,
    decoder_up,
):
    ids = iter(range(1 + 16 * int(wide), 100))
    source_rows, width = source.shape
    target_rows = target.shape[0]
    cols = encoder_mixing.shape[0]
    hidden = encoder_inner.shape[1]
    adapt = encoder_down.shape[1]
    source_halo = source_rows if wide else source_rows // 2
    target_halo = target_rows if wide else target_rows // 2
    source_half, target_half = source_rows // 2, target_rows // 2
    source_n, target_n = source_half // SEGMENT, target_half // SEGMENT
    chunk = 2 * SEGMENT

    encoder_wo = lax.all_gather(encoder_mixing, "tp")
    decoder_wo = lax.all_gather(decoder_mixing, "tp")
    cross_wo = lax.all_gather(cross_mixing, "tp")

    def padded(prefix):
        return jnp.pad(prefix, ((0, 0), (0, PREFIX_ROWS - prefix.shape[1]), (0, 0)))

    encoder_prefix, decoder_prefix, cross_prefix = map(padded, (encoder_prefix, decoder_prefix, cross_prefix))

    encoder_q, encoder_kv = project(source, encoder_attention)
    encoder_parts = halo_parts(encoder_kv, source_halo)
    decoder_q, decoder_kv = project(target, decoder_attention)
    decoder_parts = halo_parts(decoder_kv, target_halo)

    encoder_docs = document_plan(
        source_document, source_document, source_rows, source_rows, source_halo, 256, False
    )
    decoder_docs = document_plan(
        target_document, target_document, target_rows, target_rows, target_halo, 128, True
    )
    cross_docs = document_plan(
        target_document, source_document, target_rows, source_rows, source_halo, 128, False
    )
    own_target = lax.dynamic_slice_in_dim(target_document, lax.axis_index("seq") * target_rows, target_rows)
    real = halves((own_target >= 0).astype(F32)[:, None])

    decoder_wide, decoder_low, decoder_total = attend(
        decoder_q, decoder_parts, decoder_prefix, decoder_docs, True
    )
    t1, t2, cross_q = exchange_call(
        partial(decoder_self_kernel, n_seq),
        next(ids),
        [((target_half, width), F32), ((target_half, width), F32), ((2, target_half, cols), BF16)],
        exchange_scratch(target_half, ((4, target_half, cols), BF16), ((2, target_half, width), BF16)),
        4,
        target_n,
        4 * target_rows * width * cols,
        (halves(decoder_low), halves(target), decoder_gains, decoder_wo, cross_query),
    )
    encoder_wide, encoder_low, encoder_total = attend(
        encoder_q, encoder_parts, encoder_prefix, encoder_docs, False
    )
    e1, e3, encoder_hidden, encoder_slope, encoder_side, encoder_side_slope, cross_kv, cross_before, cross_after = (
        exchange_call(
            partial(encoder_forward_kernel, n_seq, source_halo),
            next(ids),
            [
                ((source_half, width), F32),
                ((source_half, width), F32),
                ((2, source_half, width), BF16),
                ((source_n, chunk, hidden), BF16),
                ((source_n, chunk, adapt), BF16),
                ((source_n, chunk, adapt), BF16),
                ((2, source_rows, cols), BF16),
                ((2, source_halo, cols), BF16),
                ((2, source_halo, cols), BF16),
            ],
            exchange_scratch(
                source_half,
                ((4, source_half, cols), BF16),
                ((source_half, width), F32),
                "total",
                ((2, source_half, width), BF16),
            ),
            3 + 1 + 2 + 1 + (4 if wide else 2),
            source_n,
            2 * source_rows * width * (2 * hidden + 2 * adapt + 4 * cols),
            (
                halves(encoder_low), halves(source), encoder_gains, encoder_wo, encoder_inner, encoder_outer,
                encoder_down, encoder_up, cross_memory,
            ),
        )
    )
    cross_parts = (cross_before, cross_kv, cross_after)
    cross_q = cross_q.reshape(target_rows, cols)
    cross_wide, cross_low, cross_total = attend(cross_q, cross_parts, cross_prefix, cross_docs, False)

    decoded, g2, cross_da, decoder_down_gradient, decoder_up_gradient = exchange_call(
        partial(decoder_chain_kernel, n_seq),
        next(ids),
        [
            ((2, target_half, width), F32),
            ((target_half, width), F32),
            ((2, target_half, cols), BF16),
            ((width, adapt), F32),
            ((adapt, width), F32),
        ],
        exchange_scratch(
            target_half,
            ((4, target_half, cols), BF16),
            ((target_half, width), F32),
            ((target_half, width), F32),
            ((target_half, width), F32),
            ((2, target_half, width), BF16),
            ((2, target_half, width), BF16),
            ((2, target_half, width), BF16),
            ((target_n, chunk, hidden), BF16),
            ((target_n, chunk, adapt), BF16),
            ((target_n, chunk, adapt), BF16),
            "total",
            "total",
        ),
        3 + 1 + 2 + 1 + 1 + 2 + 1,
        target_n,
        2 * target_rows * width * (4 * hidden + 6 * adapt + 2 * cols),
        (
            halves(cross_low), t2, real, halves(cotangent), decoder_gains, cross_wo, decoder_inner,
            decoder_outer, decoder_down, decoder_up, cross_mixing,
        ),
    )

    cross_dq, cross_dbefore, cross_dkv, cross_dafter, cross_prefix_gradient = attend_back(
        cross_q, cross_da.reshape(target_rows, cols), cross_wide, cross_total, cross_parts, cross_prefix,
        cross_docs, False,
    )
    decoder_g1, decoder_da = exchange_call(
        partial(decoder_query_back_kernel, n_seq),
        next(ids),
        [((target_half, width), F32), ((2, target_half, cols), BF16)],
        exchange_scratch(target_half, ((2, target_half, width), BF16), "total"),
        3,
        target_n,
        4 * target_rows * width * cols,
        (halves(cross_dq), g2, t1, decoder_gains, cross_query, decoder_mixing),
    )
    encoder_g1, encoder_da, encoder_down_gradient, encoder_up_gradient = exchange_call(
        partial(encoder_back_kernel, n_seq, source_halo),
        next(ids),
        [
            ((source_half, width), F32),
            ((2, source_half, cols), BF16),
            ((width, adapt), F32),
            ((adapt, width), F32),
        ],
        exchange_scratch(
            source_half,
            ((2, source_halo, cols), BF16),
            ((2, source_halo, cols), BF16),
            ((2, 2, SEGMENT, cols), BF16),
            ((source_half, width), F32),
            ((2, source_half, width), BF16),
            ((2, source_half, width), BF16),
            "total",
            "total",
        ),
        (4 if wide else 2) + 2 + 1 + 2 + 1,
        source_n,
        2 * source_rows * width * (2 * hidden + 4 * adapt + 3 * cols),
        (
            cross_dkv, cross_dbefore, cross_dafter, cross_memory, e3, e1, encoder_gains, encoder_hidden,
            encoder_slope, encoder_side, encoder_side_slope, encoder_inner, encoder_outer, encoder_down,
            encoder_up, encoder_mixing,
        ),
    )

    def input_back(dq, dkv, dbefore, dafter, weights, g1, rows, halo):
        half = rows // 2
        return exchange_call(
            partial(input_back_kernel, n_seq, halo),
            next(ids),
            [((2, half, width), F32)],
            exchange_scratch(
                half,
                ((2, halo, cols), BF16),
                ((2, halo, cols), BF16),
                ((2, 2, SEGMENT, cols), BF16),
                "total",
            ),
            (4 if wide else 2) + 2 + 1,
            half // SEGMENT,
            6 * rows * width * cols,
            (halves(dq), dkv, dbefore, dafter, weights, g1),
        )[0].reshape(rows, width)

    dq, dbefore, dkv, dafter, decoder_prefix_gradient = attend_back(
        decoder_q, decoder_da.reshape(target_rows, cols), decoder_wide, decoder_total, decoder_parts,
        decoder_prefix, decoder_docs, True,
    )
    target_gradient = input_back(
        dq, dkv, dbefore, dafter, decoder_attention, decoder_g1, target_rows, target_halo
    )
    dq, dbefore, dkv, dafter, encoder_prefix_gradient = attend_back(
        encoder_q, encoder_da.reshape(source_rows, cols), encoder_wide, encoder_total, encoder_parts,
        encoder_prefix, encoder_docs, False,
    )
    source_gradient = input_back(
        dq, dkv, dbefore, dafter, encoder_attention, encoder_g1, source_rows, source_halo
    )

    cut = slice(0, PREFIX)
    weight_totals = lax.psum(
        (
            encoder_prefix_gradient[:, cut],
            encoder_down_gradient,
            encoder_up_gradient,
            decoder_prefix_gradient[:, cut],
            cross_prefix_gradient[:, cut],
            decoder_down_gradient,
            decoder_up_gradient,
        ),
        "seq",
    )
    return (decoded.reshape(target_rows, width), source_gradient, target_gradient) + tuple(weight_totals)


def solution(mesh):
    return jax.shard_map(
        partial(on_device, mesh.shape["seq"], True),
        mesh=mesh,
        in_specs=(
            P("seq", None),
            P("seq", None),
            P(),
            P(),
            P("seq", None),
            P(None, None, "tp"),
            P("tp", None),
            P(),
            P(None, "tp"),
            P("tp", None),
            P(None, None, "tp"),
            P(None, "tp"),
            P("tp", None),
            P(None, None, "tp"),
            P("tp", None),
            P(None, None, "tp"),
            P(None, "tp"),
            P(None, None, "tp"),
            P("tp", None),
            P(None, None, "tp"),
            P(),
            P(None, "tp"),
            P("tp", None),
            P(None, "tp"),
            P("tp", None),
        ),
        out_specs=(
            P("seq", None),
            P("seq", None),
            P("seq", None),
            P(None, None, "tp"),
            P(None, "tp"),
            P("tp", None),
            P(None, None, "tp"),
            P(None, None, "tp"),
            P(None, "tp"),
            P("tp", None),
        ),
        check_vma=False,
    )
```

```python
from functools import partial

import jax
import jax.numpy as jnp
from jax import lax
from jax.experimental import pallas as pl
from jax.experimental.pallas import tpu as pltpu
from jax.sharding import PartitionSpec as P

HEAD_DIM = 64
EPSILON = 1e-05
NEGATIVE = -1e30
HEADS = 4
KEY_BLOCK = 256
PREFIX = 30
PREFIX_ROWS = 32
SEGMENT = 64
MESH = pl.DeviceIdType.MESH
F32 = jnp.float32
BF16 = jnp.bfloat16
VMEM_BYTES = 56 * 2**20


def mm(left, right):
    return jnp.dot(left, right, preferred_element_type=F32)


def mm_nt(left, right):
    return lax.dot_general(left, right, (((1,), (1,)), ((), ())), preferred_element_type=F32)


def mm_tn(left, right):
    return lax.dot_general(left, right, (((0,), (0,)), ((), ())), preferred_element_type=F32)


def normalize(inputs, scaling):
    centered = inputs - jnp.mean(inputs, axis=-1, keepdims=True)
    spread = lax.rsqrt(jnp.mean(centered * centered, axis=-1, keepdims=True) + EPSILON)
    return scaling * (centered * spread)


def normalize_back(inputs, scaling, gradient):
    centered = inputs - jnp.mean(inputs, axis=-1, keepdims=True)
    spread = lax.rsqrt(jnp.mean(centered * centered, axis=-1, keepdims=True) + EPSILON)
    unit = centered * spread
    scaled = gradient * scaling
    first = jnp.mean(scaled, axis=-1, keepdims=True)
    second = jnp.mean(scaled * unit, axis=-1, keepdims=True)
    return spread * (scaled - first - unit * second)


def gelu_parts(inputs):
    chance = 0.5 * (1.0 + lax.erf(inputs * (0.5**0.5)))
    density = jnp.exp(-0.5 * inputs * inputs) * 0.3989422804014327
    return (inputs * chance).astype(BF16), (chance + inputs * density).astype(BF16)


def project_kernel(x_ref, w_ref, q_ref, kv_ref):
    rows = x_ref[...]
    q_ref[...] = mm(rows, w_ref[0]).astype(BF16)
    kv_ref[0] = mm(rows, w_ref[1]).astype(BF16)
    kv_ref[1] = mm(rows, w_ref[2]).astype(BF16)


def project(inputs, weights):
    rows, width = inputs.shape
    block = 256
    cols = weights.shape[2]
    return pl.pallas_call(
        project_kernel,
        grid=(rows // block,),
        in_specs=[
            pl.BlockSpec((block, width), lambda i: (i, 0)),
            pl.BlockSpec(weights.shape, lambda i: (0, 0, 0)),
        ],
        out_specs=[
            pl.BlockSpec((block, cols), lambda i: (i, 0)),
            pl.BlockSpec((2, block, cols), lambda i: (0, i, 0)),
        ],
        out_shape=[
            jax.ShapeDtypeStruct((rows, cols), BF16),
            jax.ShapeDtypeStruct((2, rows, cols), BF16),
        ],
        compiler_params=pltpu.CompilerParams(vmem_limit_bytes=VMEM_BYTES),
        cost_estimate=pl.CostEstimate(
            flops=6 * rows * width * cols, bytes_accessed=8 * rows * cols + 6 * width * cols, transcendentals=0
        ),
    )(inputs, weights)


def by_heads(rows, lane_head):
    zero = jnp.zeros_like(rows)
    return jnp.concatenate([jnp.where(lane_head == h, rows, zero) for h in range(HEADS)], axis=0)


def head_bias(kd_ref, qd_ref, start, first_query, halo, block, causal):
    key_doc = kd_ref[pl.ds(start, KEY_BLOCK), :]
    allowed = key_doc == qd_ref[0]
    if causal:
        key_place = start - halo + lax.broadcasted_iota(jnp.int32, (KEY_BLOCK, block), 0)
        query_place = first_query + lax.broadcasted_iota(jnp.int32, (KEY_BLOCK, block), 1)
        allowed = allowed & (key_place <= query_place)
    bias = jnp.where(allowed, 0.0, NEGATIVE)
    return jnp.concatenate([bias] * HEADS, axis=1)


def prefix_scores(pre_ref, stacked):
    scores = mm_nt(pre_ref[0], stacked)
    row = lax.broadcasted_iota(jnp.int32, scores.shape, 0)
    return jnp.where(row < PREFIX, scores, NEGATIVE)


def fill_window(window, parts, index):
    at = 0
    for part in parts:
        size = part.shape[1]
        window[at : at + size, :] = part[index]
        at += size


def attend_kernel(
    halo, causal, lo_ref, hi_ref, q_ref, bef_ref, own_ref, aft_ref, pre_ref, qd_ref, kd_ref,
    wide_ref, low_ref, total_ref, keys, values, blended,
):
    i = pl.program_id(0)
    block = q_ref.shape[0]
    parts = (bef_ref, own_ref, aft_ref)

    @pl.when(i == 0)
    def _():
        fill_window(keys, parts, 0)
        at = 0
        for part in parts:
            for k in range(part.shape[1] // KEY_BLOCK):
                values[at] = part[1, k * KEY_BLOCK : (k + 1) * KEY_BLOCK, :].T
                at += 1

    lane_head = lax.broadcasted_iota(jnp.int32, q_ref.shape, 1) // HEAD_DIM
    stacked = by_heads(q_ref[...] * jnp.asarray(HEAD_DIM**-0.5, BF16), lane_head)
    scores = prefix_scores(pre_ref, stacked)
    highest = jnp.max(scores, axis=0, keepdims=True)
    chances = jnp.exp(scores - highest)
    summed = jnp.sum(chances, axis=0, keepdims=True)
    low = chances.astype(BF16)
    pre_values = pre_ref[1].T
    for h in range(HEADS):
        rows = slice(h * HEAD_DIM, (h + 1) * HEAD_DIM)
        blended[rows, :] = mm(pre_values[rows, :], low[:, h * block : (h + 1) * block])

    def step(kb, carry):
        highest, summed = carry
        start = pl.multiple_of(kb * KEY_BLOCK, KEY_BLOCK)
        scores = mm_nt(keys[pl.ds(start, KEY_BLOCK), :], stacked)
        scores = scores + head_bias(kd_ref, qd_ref, start, i * block, halo, block, causal)
        top = jnp.maximum(highest, jnp.max(scores, axis=0, keepdims=True))
        fade = jnp.exp(highest - top)
        chances = jnp.exp(scores - top)
        summed = summed * fade + jnp.sum(chances, axis=0, keepdims=True)
        low = chances.astype(BF16)
        for h in range(HEADS):
            rows = slice(h * HEAD_DIM, (h + 1) * HEAD_DIM)
            cols = slice(h * block, (h + 1) * block)
            blended[rows, :] = blended[rows, :] * fade[:, cols] + mm(values[kb, rows, :], low[:, cols])
        return top, summed

    highest, summed = lax.fori_loop(lo_ref[i], hi_ref[i], step, (highest, summed))
    total_ref[0] = highest + jnp.log(summed)
    inverse = 1.0 / summed
    for h in range(HEADS):
        rows = slice(h * HEAD_DIM, (h + 1) * HEAD_DIM)
        blended[rows, :] = blended[rows, :] * inverse[:, h * block : (h + 1) * block]
    result = blended[...].T
    wide_ref[...] = result
    low_ref[...] = result.astype(BF16)


def attend(queries, parts, prefix, docs, causal):
    query_doc, key_doc, lo, hi = docs
    rows, cols = queries.shape
    count, _, block = query_doc.shape
    window = key_doc.shape[0]
    halo = parts[0].shape[1]

    def whole(array):
        return pl.BlockSpec(array.shape, lambda i, *_: (0,) * array.ndim)

    return pl.pallas_call(
        partial(attend_kernel, halo, causal),
        grid_spec=pltpu.PrefetchScalarGridSpec(
            num_scalar_prefetch=2,
            grid=(count,),
            in_specs=[
                pl.BlockSpec((block, cols), lambda i, *_: (i, 0)),
                whole(parts[0]),
                whole(parts[1]),
                whole(parts[2]),
                whole(prefix),
                pl.BlockSpec((1, 1, block), lambda i, *_: (i, 0, 0)),
                whole(key_doc),
            ],
            out_specs=[
                pl.BlockSpec((block, cols), lambda i, *_: (i, 0)),
                pl.BlockSpec((block, cols), lambda i, *_: (i, 0)),
                pl.BlockSpec((1, 1, HEADS * block), lambda i, *_: (i, 0, 0)),
            ],
            scratch_shapes=[
                pltpu.VMEM((window, cols), BF16),
                pltpu.VMEM((window // KEY_BLOCK, cols, KEY_BLOCK), BF16),
                pltpu.VMEM((cols, block), F32),
            ],
        ),
        out_shape=[
            jax.ShapeDtypeStruct((rows, cols), F32),
            jax.ShapeDtypeStruct((rows, cols), BF16),
            jax.ShapeDtypeStruct((count, 1, HEADS * block), F32),
        ],
        compiler_params=pltpu.CompilerParams(vmem_limit_bytes=VMEM_BYTES),
        cost_estimate=pl.CostEstimate(
            flops=16 * rows * 1024 * cols, bytes_accessed=8 * window * cols, transcendentals=4 * rows * 1024
        ),
    )(lo, hi, queries, *parts, prefix, query_doc, key_doc)


def attend_back_kernel(
    halo, causal, lo_ref, hi_ref, q_ref, g_ref, wide_ref, total_ref, bef_ref, own_ref, aft_ref, pre_ref,
    qd_ref, kd_ref, dq_ref, dbef_ref, down_ref, daft_ref, dpre_ref,
    keys, values, turned, key_sum, value_sum, query_sum, prefix_sum,
):
    i = pl.program_id(0)
    block = q_ref.shape[0]
    parts = (bef_ref, own_ref, aft_ref)

    @pl.when(i == 0)
    def _():
        fill_window(keys, parts, 0)
        fill_window(values, parts, 1)
        at = 0
        for part in parts:
            for k in range(part.shape[1] // KEY_BLOCK):
                turned[at] = part[0, k * KEY_BLOCK : (k + 1) * KEY_BLOCK, :].T
                at += 1
        key_sum[...] = jnp.zeros_like(key_sum)
        value_sum[...] = jnp.zeros_like(value_sum)
        prefix_sum[...] = jnp.zeros_like(prefix_sum)

    lane_head = lax.broadcasted_iota(jnp.int32, q_ref.shape, 1) // HEAD_DIM
    stacked = by_heads(q_ref[...] * jnp.asarray(HEAD_DIM**-0.5, BF16), lane_head)
    grads = by_heads(g_ref[...], lane_head)
    mixed = (g_ref[...].astype(F32) * wide_ref[...]).T
    offsets = jnp.concatenate(
        [
            jnp.sum(mixed[h * HEAD_DIM : (h + 1) * HEAD_DIM, :], axis=0, keepdims=True)
            for h in range(HEADS)
        ],
        axis=1,
    )
    total = total_ref[0]
    chances = jnp.exp(prefix_scores(pre_ref, stacked) - total)
    score_grad = (chances * (mm_nt(pre_ref[1], grads) - offsets)).astype(BF16)
    prefix_sum[0] += mm(score_grad, stacked)
    prefix_sum[1] += mm(chances.astype(BF16), grads)
    pre_keys = pre_ref[0].T
    for h in range(HEADS):
        rows = slice(h * HEAD_DIM, (h + 1) * HEAD_DIM)
        query_sum[rows, :] = mm(pre_keys[rows, :], score_grad[:, h * block : (h + 1) * block])

    def step(kb, carry):
        start = pl.multiple_of(kb * KEY_BLOCK, KEY_BLOCK)
        here = pl.ds(start, KEY_BLOCK)
        scores = mm_nt(keys[here, :], stacked)
        scores = scores + head_bias(kd_ref, qd_ref, start, i * block, halo, block, causal)
        chances = jnp.exp(scores - total)
        score_grad = (chances * (mm_nt(values[here, :], grads) - offsets)).astype(BF16)
        key_sum[here, :] += mm(score_grad, stacked)
        value_sum[here, :] += mm(chances.astype(BF16), grads)
        for h in range(HEADS):
            rows = slice(h * HEAD_DIM, (h + 1) * HEAD_DIM)
            query_sum[rows, :] += mm(turned[kb, rows, :], score_grad[:, h * block : (h + 1) * block])
        return carry

    lax.fori_loop(lo_ref[i], hi_ref[i], step, 0)
    dq_ref[...] = (query_sum[...].T * HEAD_DIM**-0.5).astype(BF16)

    @pl.when(i == pl.num_programs(0) - 1)
    def _():
        at = 0
        for part in (dbef_ref, down_ref, daft_ref):
            size = part.shape[1]
            part[0] = key_sum[at : at + size, :].astype(part.dtype)
            part[1] = value_sum[at : at + size, :].astype(part.dtype)
            at += size
        at = 0
        for k in range(2):
            for c in range(2):
                dpre_ref[at : at + PREFIX_ROWS, :] = prefix_sum[k, :, c * 128 : (c + 1) * 128].astype(BF16)
                at += PREFIX_ROWS


def attend_back(queries, grads, wide, total, parts, prefix, docs, causal):
    query_doc, key_doc, lo, hi = docs
    rows, cols = queries.shape
    count, _, block = query_doc.shape
    window = key_doc.shape[0]
    halo = parts[0].shape[1]

    def whole(shape):
        return pl.BlockSpec(shape, lambda i, *_: (0,) * len(shape))

    def blocked():
        return pl.BlockSpec((block, cols), lambda i, *_: (i, 0))

    return pl.pallas_call(
        partial(attend_back_kernel, halo, causal),
        grid_spec=pltpu.PrefetchScalarGridSpec(
            num_scalar_prefetch=2,
            grid=(count,),
            in_specs=[
                blocked(),
                blocked(),
                blocked(),
                pl.BlockSpec((1, 1, HEADS * block), lambda i, *_: (i, 0, 0)),
                whole(parts[0].shape),
                whole(parts[1].shape),
                whole(parts[2].shape),
                whole(prefix.shape),
                pl.BlockSpec((1, 1, block), lambda i, *_: (i, 0, 0)),
                whole(key_doc.shape),
            ],
            out_specs=[
                blocked(),
                whole(parts[0].shape),
                whole(parts[1].shape),
                whole(parts[2].shape),
                whole((4 * PREFIX_ROWS, 128)),
            ],
            scratch_shapes=[
                pltpu.VMEM((window, cols), BF16),
                pltpu.VMEM((window, cols), BF16),
                pltpu.VMEM((window // KEY_BLOCK, cols, KEY_BLOCK), BF16),
                pltpu.VMEM((window, cols), F32),
                pltpu.VMEM((window, cols), F32),
                pltpu.VMEM((cols, block), F32),
                pltpu.VMEM(prefix.shape, F32),
            ],
        ),
        out_shape=[
            jax.ShapeDtypeStruct((rows, cols), BF16),
            jax.ShapeDtypeStruct(parts[0].shape, BF16),
            jax.ShapeDtypeStruct(parts[1].shape, F32),
            jax.ShapeDtypeStruct(parts[2].shape, BF16),
            jax.ShapeDtypeStruct((4 * PREFIX_ROWS, 128), BF16),
        ],
        compiler_params=pltpu.CompilerParams(vmem_limit_bytes=VMEM_BYTES),
        cost_estimate=pl.CostEstimate(
            flops=40 * rows * 1024 * cols, bytes_accessed=16 * window * cols, transcendentals=4 * rows * 1024
        ),
    )(lo, hi, queries, grads, wide, total, *parts, prefix, query_doc, key_doc)


class Place:
    def __init__(self, n_seq):
        self.n_seq = n_seq
        self.s = lax.axis_index("seq")
        self.t = lax.axis_index("tp")
        self.core = self.t % 2
        self.other = 1 - self.core
        self.twin_t = self.t + 1 - 2 * self.core
        self.across_t = (self.t + 2) % 4
        self.corner_t = 3 - self.t
        self.twin = (self.s, self.twin_t)
        self.across = (self.s, self.across_t)
        self.corner = (self.s, self.corner_t)
        self.after = ((self.s + 1) % n_seq, self.t)
        self.before = ((self.s + n_seq - 1) % n_seq, self.t)

    def greet(self, partners, whole_seq=False):
        barrier = pltpu.get_barrier_semaphore()
        for partner in partners:
            pl.semaphore_signal(barrier, inc=1, device_id=partner, device_id_type=MESH)
        count = len(partners)
        if whole_seq:

            def signal(k, carry):
                pl.semaphore_signal(barrier, inc=1, device_id=self.along(k), device_id_type=MESH)
                return carry

            lax.fori_loop(1, self.n_seq, signal, 0)
            count += self.n_seq - 1
        pl.semaphore_wait(barrier, count)

    def along(self, k):
        return ((self.s + k) % self.n_seq, self.t)


class Sems:
    def __init__(self, send, receive):
        self.send, self.receive, self.used = send, receive, 0

    def take(self):
        kind = self.used
        self.used += 1
        return kind


def remote(sems, kind, j, src, dst, device):
    return pltpu.make_async_remote_copy(
        src_ref=src,
        dst_ref=dst,
        send_sem=sems.send.at[kind, j],
        recv_sem=sems.receive.at[kind, j],
        device_id=device,
        device_id_type=MESH,
    )


def span(j):
    return pl.ds(pl.multiple_of(j * SEGMENT, SEGMENT), SEGMENT)


class Loaded:
    def __init__(self, source, buf, sem):
        self.buf, self.at = buf, buf.at
        self.copy = pltpu.make_async_copy(source, buf, sem)
        self.copy.start()

    def wait(self):
        self.copy.wait()

    def __getitem__(self, index):
        return self.buf[index]


class Stored:
    def __init__(self, sems, result, buf, parts):
        self.result, self.buf, self.parts, self.sems = result, buf, parts, sems
        self.at, self.shape = buf.at, buf.shape
        self.kind = sems.take()

    def copies(self, j):
        return [
            pltpu.make_async_copy(
                self.buf.at[part], self.result.at[part], self.sems.receive.at[self.kind, 2 * j + i]
            )
            for i, part in enumerate(self.parts(j))
        ]

    def flush(self, j):
        for copy in self.copies(j):
            copy.start()

    def drain(self, j):
        for copy in self.copies(j):
            copy.wait()

    def __getitem__(self, index):
        return self.buf[index]

    def __setitem__(self, index, value):
        self.buf[index] = value


class Twins:
    def __init__(self, place, sems, buf):
        self.place, self.sems, self.buf, self.kind = place, sems, buf, sems.take()

    def copy(self, j, half):
        part = self.buf.at[half, span(j)]
        return remote(self.sems, self.kind, j, part, part, self.place.twin)

    def put(self, j, value):
        self.buf[self.place.core, span(j)] = value
        self.copy(j, self.place.core).start()

    def wait(self, j):
        self.copy(j, self.place.other).wait_recv()

    def both(self, j):
        return jnp.concatenate([self.buf[self.place.core, span(j)], self.buf[self.place.other, span(j)]], axis=0)

    def drain(self, j):
        self.copy(j, self.place.core).wait_send()


class TwinResult:
    def __init__(self, place, sems, local, result, stage):
        self.place, self.sems, self.local, self.result, self.stage = place, sems, local, result, stage
        self.kind, self.kind_local = sems.take(), local.take()

    def copies(self, j):
        rows, core = span(j), self.place.core
        return (
            remote(self.sems, self.kind, j, self.stage.at[rows], self.result.at[core, rows], self.place.twin),
            pltpu.make_async_copy(
                self.stage.at[rows], self.result.at[core, rows], self.local.receive.at[self.kind_local, 2 * j]
            ),
        )

    def put(self, j, value):
        self.stage[span(j)] = value
        for copy in self.copies(j):
            copy.start()

    def drain(self, j):
        out, local = self.copies(j)
        out.wait_send()
        local.wait()
        part = self.result.at[self.place.other, span(j)]
        remote(self.sems, self.kind, j, part, part, self.place.twin).wait_recv()


class Total:
    SHAPES = staticmethod(
        lambda half: [
            pltpu.VMEM((half, 1024), F32),
            pltpu.VMEM((half, 1024), BF16),
            pltpu.VMEM((half, 1024), BF16),
            pltpu.VMEM((half, 1024), BF16),
            pltpu.VMEM((half, 1024), BF16),
        ]
    )

    def __init__(self, place, sems, refs):
        self.place, self.sems = place, sems
        self.mine, self.away, self.came, self.chip, self.far = refs
        self.kind_twin, self.kind_across = sems.take(), sems.take()

    def twin_copy(self, j):
        rows = span(j)
        return remote(self.sems, self.kind_twin, j, self.away.at[rows], self.came.at[rows], self.place.twin)

    def across_copy(self, j):
        rows = span(j)
        return remote(self.sems, self.kind_across, j, self.chip.at[rows], self.far.at[rows], self.place.across)

    def put(self, j, value):
        self.mine[span(j)] = value[:SEGMENT]
        self.away[span(j)] = value[SEGMENT:].astype(BF16)
        self.twin_copy(j).start()

    def middle(self, j):
        self.twin_copy(j).wait_recv()
        self.chip[span(j)] = (self.mine[span(j)] + self.came[span(j)].astype(F32)).astype(BF16)
        self.across_copy(j).start()

    def get(self, j):
        self.across_copy(j).wait_recv()
        return self.chip[span(j)].astype(F32) + self.far[span(j)].astype(F32)

    def drain(self, j):
        self.twin_copy(j).wait_send()
        self.across_copy(j).wait_send()


class SeqSum:
    @staticmethod
    def scratch(n_seq, rows):
        dma = pltpu.SemaphoreType.DMA
        return [
            pltpu.VMEM((rows, 128), BF16),
            pltpu.VMEM((n_seq, rows // n_seq, 128), BF16),
            pltpu.VMEM((rows, 128), BF16),
            dma((2, n_seq)),
            dma((2, n_seq)),
        ]

    def __init__(self, place, refs):
        self.place = place
        self.terms, self.landing, self.total, self.sent, self.came = refs
        self.size = self.landing.shape[1]

    def piece(self, s):
        return pl.ds(pl.multiple_of(s * self.size, self.size), self.size)

    def copy(self, phase, k, src, dst):
        return pltpu.make_async_remote_copy(
            src_ref=src,
            dst_ref=dst,
            send_sem=self.sent.at[phase, k],
            recv_sem=self.came.at[phase, k],
            device_id=self.place.along(k),
            device_id_type=MESH,
        )

    def term_copy(self, k):
        to = self.place.along(k)[0]
        return self.copy(0, k, self.terms.at[self.piece(to)], self.landing.at[k])

    def total_copy(self, k):
        mine = self.total.at[self.piece(self.place.s)]
        return self.copy(1, k, mine, mine)

    def total_arrival(self, k):
        theirs = self.total.at[self.piece((self.place.s + self.place.n_seq - k) % self.place.n_seq)]
        return self.copy(1, k, theirs, theirs)

    def loop(self, action):
        def step(k, carry):
            action(k)
            return carry

        lax.fori_loop(1, self.place.n_seq, step, 0)

    def start(self):
        self.loop(lambda k: self.term_copy(k).start())

    def add(self, j):
        self.loop(lambda k: self.term_copy(k).wait_recv())
        mine = self.piece(self.place.s)

        def step(k, total):
            return total + self.landing[k].astype(F32)

        total = lax.fori_loop(1, self.place.n_seq, step, self.terms[mine].astype(F32))
        self.total[mine] = total.astype(BF16)
        self.loop(lambda k: self.total_copy(k).start())

    def wait(self):
        self.loop(lambda k: self.total_arrival(k).wait_recv())

    def drain(self):
        self.loop(lambda k: self.term_copy(k).wait_send())
        self.loop(lambda k: self.total_copy(k).wait_send())


def put_weight_terms(terms, down_grad, up_grad):
    rows = down_grad.shape[0]
    terms[0:rows] = down_grad[...].astype(BF16)
    terms[rows : 2 * rows] = up_grad[...].astype(BF16)


class Heads:
    def __init__(self, place, sems, own, buf):
        self.place, self.sems, self.own, self.buf = place, sems, own, buf
        self.kinds = [sems.take() for _ in range(3)]

    def copies(self, j):
        p, rows = self.place, span(j)
        landing = self.buf.at[p.t, rows]
        return [
            remote(self.sems, self.kinds[0], j, self.own.at[p.core, rows], landing, p.across),
            remote(self.sems, self.kinds[1], j, self.own.at[p.other, rows], landing, p.corner),
            remote(self.sems, self.kinds[2], j, self.own.at[p.other, rows], landing, p.twin),
        ]

    def send(self, j):
        for copy in self.copies(j):
            copy.start()
        self.buf[self.place.t, span(j)] = self.own[self.place.core, span(j)]

    def wait(self, j):
        p, rows = self.place, span(j)
        for kind, source, device in zip(
            self.kinds, (p.across_t, p.corner_t, p.twin_t), (p.across, p.corner, p.twin)
        ):
            part = self.buf.at[source, rows]
            remote(self.sems, kind, j, part, part, device).wait_recv()

    def mix(self, j, weight):
        rows = span(j)
        total = mm(self.buf[0, rows], weight[0])
        for k in range(1, 4):
            total = total + mm(self.buf[k, rows], weight[k])
        return total

    def drain(self, j):
        for copy in self.copies(j):
            copy.wait_send()


class Halo:
    def __init__(self, place, sems, rows, halo):
        self.place, self.sems, self.rows, self.halo = place, sems, rows, halo
        self.half = rows // 2
        self.up = [sems.take() if hh * self.half >= rows - halo else None for hh in range(2)]
        self.down = [sems.take() if hh * self.half < halo else None for hh in range(2)]

    def place_up(self, hh, j):
        return span(j + (hh * self.half - (self.rows - self.halo)) // SEGMENT)

    def place_down(self, hh, j):
        return span(j + hh * self.half // SEGMENT)

    def out_copies(self, j, own, before, after):
        copies = []
        for hh in range(2):
            src = own.at[:, self.place_down(hh, j)]
            if self.up[hh] is not None:
                dst = before.at[:, self.place_up(hh, j)]
                copies.append(remote(self.sems, self.up[hh], j, src, dst, self.place.after))
            if self.down[hh] is not None:
                dst = after.at[:, self.place_down(hh, j)]
                copies.append(remote(self.sems, self.down[hh], j, src, dst, self.place.before))
        return copies

    def back_copies(self, j, before, after, from_before, from_after):
        copies = []
        for hh in range(2):
            if self.up[hh] is not None:
                where = self.place_up(hh, j)
                copies.append(
                    remote(self.sems, self.up[hh], j, before.at[:, where], from_after.at[:, where], self.place.before)
                )
            if self.down[hh] is not None:
                where = self.place_down(hh, j)
                copies.append(
                    remote(self.sems, self.down[hh], j, after.at[:, where], from_before.at[:, where], self.place.after)
                )
        return copies

    def gathered(self, j, hh, own, from_before, from_after):
        total = own[:, self.place_down(hh, j)]
        if self.down[hh] is not None:
            total = total + from_before[:, self.place_down(hh, j)].astype(F32)
        if self.up[hh] is not None:
            total = total + from_after[:, self.place_up(hh, j)].astype(F32)
        return total


def pipeline(stages):
    last = max(delay + n for delay, n, _ in stages)

    def step(s, carry):
        for delay, n, stage in stages:
            pl.when((s >= delay) & (s < n + delay))(partial(stage, s - delay))
        return carry

    lax.fori_loop(0, last, step, 0)


def at_first(j, *loads):
    @pl.when(j == 0)
    def _():
        for load in loads:
            load.wait()


def each(n, *actions):
    def step(j, carry):
        for action in actions:
            action(j)
        return carry

    lax.fori_loop(0, n, step, 0)


def exchange_call(kernel, cid, args, loads, outs, scratch, kinds, local_kinds, n, flops):
    anywhere = pl.BlockSpec(memory_space=pl.ANY)
    moved = sum(a.size * a.dtype.itemsize for a in args)
    dma = pltpu.SemaphoreType.DMA
    return pl.pallas_call(
        kernel,
        in_specs=[anywhere] * len(args),
        out_specs=[anywhere] * len(outs),
        out_shape=[jax.ShapeDtypeStruct(shape, kind) for shape, kind in outs],
        scratch_shapes=[pltpu.VMEM(shape, a.dtype) for shape, a in zip(loads, args)]
        + scratch
        + [dma((len(args),)), dma((max(local_kinds, 1), 2 * n)), dma((kinds, n)), dma((kinds, n))],
        compiler_params=pltpu.CompilerParams(
            collective_id=cid, has_side_effects=True, vmem_limit_bytes=VMEM_BYTES
        ),
        cost_estimate=pl.CostEstimate(flops=flops, bytes_accessed=moved, transcendentals=0),
    )(*args)


def feed_rows(rows, w1, w2, wd, wu):
    inner, inner_slope = gelu_parts(mm(rows, w1[...]))
    side, side_slope = gelu_parts(mm(rows, wd[...]))
    return mm(inner, w2[...]) + 4.0 * mm(side, wu[...]), inner_slope, side, side_slope


def feed_rows_back(grads, four, inner_slope, side_slope, w1, w2, wd, wu):
    grad_inner = (inner_slope.astype(F32) * mm_nt(grads, w2[...])).astype(BF16)
    grad_side = (side_slope.astype(F32) * mm_nt(four, wu[...])).astype(BF16)
    return mm_nt(grad_inner, w1[...]) + mm_nt(grad_side, wd[...]), grad_side


def rows_of(place, *_):
    return lambda j: [span(j)]


def both_rows(place):
    return lambda j: [(place.core, span(j)), (place.other, span(j))]


def own_first(place, ref, j):
    return jnp.concatenate([ref[place.core, span(j)], ref[place.other, span(j)]], axis=0)


def put_both(place, ref, j, value):
    ref[place.core, span(j)] = value[:SEGMENT]
    ref[place.other, span(j)] = value[SEGMENT:]


def forward_kernel(
    n_seq, halo_rows,
    a_, x_, gains_, wo_, w1_, w2_, wd_, wu_, wkv_, da_, dx_, dgains_, dwo_, dwq_,
    e1_, e3_, hidden_, slope_, side_, side_slope_, kv_, before, after, t1_, t2_, q_,
    a, x, gains, wo, w1, w2, wd, wu, wkv, da, dx, dgains, dwo, dwq,
    e1, e3, hidden, slope, side, side_slope, kv, t1, t2, q,
    heads_buf, e2, s0, s1, s2, s3, s4, encoded, dheads_buf, dhidden,
    loading, local_sems, send, receive,
):
    place, sems, local = Place(n_seq), Sems(send, receive), Sems(local_sems, local_sems)
    half, dec_half = e1.shape[0], t1.shape[0]
    n, m = half // SEGMENT, dec_half // SEGMENT
    core = place.core
    a = Loaded(a_, a, loading.at[0])
    x = Loaded(x_.at[core], x, loading.at[1])
    gains = Loaded(gains_, gains, loading.at[2])
    wo = Loaded(wo_, wo, loading.at[3])
    w1 = Loaded(w1_, w1, loading.at[4])
    w2 = Loaded(w2_, w2, loading.at[5])
    wd = Loaded(wd_, wd, loading.at[6])
    wu = Loaded(wu_, wu, loading.at[7])
    da = Loaded(da_, da, loading.at[8])
    dx = Loaded(dx_.at[core], dx, loading.at[9])
    dgains = Loaded(dgains_, dgains, loading.at[10])
    dwo = Loaded(dwo_, dwo, loading.at[11])
    dwq = Loaded(dwq_, dwq, loading.at[12])
    wkv = Loaded(wkv_, wkv, loading.at[13])
    rows_j, both_j = rows_of(place), both_rows(place)
    e1 = Stored(local, e1_, e1, rows_j)
    e3 = Stored(local, e3_, e3, rows_j)
    hidden = Stored(local, hidden_, hidden, both_j)
    slope = Stored(local, slope_, slope, lambda j: [j])
    side = Stored(local, side_, side, lambda j: [j])
    side_slope = Stored(local, side_slope_, side_slope, lambda j: [j])
    kv = Stored(local, kv_, kv, lambda j: [(slice(None), span(j)), (slice(None), span(j + n))])
    t1 = Stored(local, t1_, t1, rows_j)
    t2 = Stored(local, t2_, t2, rows_j)
    q = Stored(local, q_, q, both_j)
    heads = Heads(place, sems, a, heads_buf)
    low = Twins(place, sems, hidden)
    total = Total(place, sems, (s0, s1, s2, s3, s4))
    low_encoded = Twins(place, sems, encoded)
    halo = Halo(place, sems, 2 * half, halo_rows)
    dec_heads = Heads(place, sems, da, dheads_buf)
    dec_low = Twins(place, sems, dhidden)
    place.greet([place.twin, place.across, place.corner, place.before, place.after])
    a.wait()
    each(n, heads.send)
    da.wait()
    each(m, dec_heads.send)

    def mix(j):
        at_first(j, x, gains, wo)
        heads.wait(j)
        rows = span(j)
        first = x[rows].astype(F32) + heads.mix(j, wo)
        e1[rows] = first
        e1.flush(j)
        middle = normalize(first, gains[0:1])
        e2[rows] = middle
        low.put(j, middle.astype(BF16))

    def feed(j):
        at_first(j, w1, w2, wd, wu)
        low.wait(j)
        hidden.flush(j)
        piece, slopes, side_rows, side_slopes = feed_rows(low.both(j), w1, w2, wd, wu)
        total.put(j, piece)
        slope[j] = slopes
        side[j] = side_rows
        side_slope[j] = side_slopes
        slope.flush(j)
        side.flush(j)
        side_slope.flush(j)

    def finish(j):
        rows = span(j)
        second = e2[rows] + total.get(j)
        low_encoded.put(j, normalize(second, gains[1:2]).astype(BF16))
        e3[rows] = second
        e3.flush(j)

    def memory(j):
        at_first(j, wkv)
        low_encoded.wait(j)
        rows = low_encoded.both(j)
        for i in range(2):
            made = mm(rows, wkv[i]).astype(BF16)
            kv[i, span(j + place.core * n)] = made[:SEGMENT]
            kv[i, span(j + place.other * n)] = made[SEGMENT:]
        for copy in halo.out_copies(j, kv, before, after):
            copy.start()
        kv.flush(j)

    def dec_mix(j):
        at_first(j, dx, dgains, dwo)
        dec_heads.wait(j)
        rows = span(j)
        first = dx[rows].astype(F32) + dec_heads.mix(j, dwo)
        t1[rows] = first
        t1.flush(j)
        middle = normalize(first, dgains[0:1])
        t2[rows] = middle
        t2.flush(j)
        dec_low.put(j, middle.astype(BF16))

    def dec_query(j):
        at_first(j, dwq)
        dec_low.wait(j)
        put_both(place, q, j, mm(dec_low.both(j), dwq[...]).astype(BF16))
        q.flush(j)

    pipeline(
        [
            (2, n, total.middle), (0, n, mix), (1, n, feed), (3, m, dec_mix), (4, m, dec_query),
            (4, n, finish), (5, n, memory),
        ]
    )

    def arrived(j):
        for copy in halo.out_copies(j, kv, before, after):
            copy.wait()

    each(
        n, heads.drain, low.drain, total.drain, low_encoded.drain, arrived, e1.drain, e3.drain, hidden.drain,
        slope.drain, side.drain, side_slope.drain, kv.drain,
    )
    each(m, dec_heads.drain, dec_low.drain, t1.drain, t2.drain, q.drain)


def decoder_chain_kernel(
    n_seq,
    a_, t2_, real_, cotangent_, gains_, wo_, w1_, w2_, wd_, wu_, mixing_,
    decoded, g2_, da_, terms_,
    a, t2, real, cotangent, gains, wo, w1, w2, wd, wu, mixing,
    g2, da, terms, down_grad, up_grad, stage,
    heads_buf, t3, t4, g3, hidden, low_g3, low_g2, inner_slope, side, side_slope,
    f0, f1, f2, f3, f4, b0, b1, b2, b3, b4,
    loading, local_sems, send, receive,
):
    place, sems, local = Place(n_seq), Sems(send, receive), Sems(local_sems, local_sems)
    half = t2.shape[0]
    n = half // SEGMENT
    core = place.core
    a = Loaded(a_, a, loading.at[0])
    t2 = Loaded(t2_, t2, loading.at[1])
    gains = Loaded(gains_, gains, loading.at[2])
    wo = Loaded(wo_, wo, loading.at[3])
    w1 = Loaded(w1_, w1, loading.at[4])
    w2 = Loaded(w2_, w2, loading.at[5])
    wd = Loaded(wd_, wd, loading.at[6])
    wu = Loaded(wu_, wu, loading.at[7])
    real = Loaded(real_.at[core], real, loading.at[8])
    cotangent = Loaded(cotangent_.at[core], cotangent, loading.at[9])
    mixing = Loaded(mixing_, mixing, loading.at[10])
    g2 = Stored(local, g2_, g2, rows_of(place))
    da = Stored(local, da_, da, both_rows(place))
    terms = Stored(local, terms_, terms, lambda j: [slice(None)])
    heads = Heads(place, sems, a, heads_buf)
    low = Twins(place, sems, hidden)
    ahead = Total(place, sems, (f0, f1, f2, f3, f4))
    result = TwinResult(place, sems, local, decoded, stage)
    back3 = Twins(place, sems, low_g3)
    behind = Total(place, sems, (b0, b1, b2, b3, b4))
    back2 = Twins(place, sems, low_g2)
    place.greet([place.twin, place.across, place.corner])
    a.wait()
    each(n, heads.send)
    down_grad[...] = jnp.zeros(down_grad.shape, F32)
    up_grad[...] = jnp.zeros(up_grad.shape, F32)

    def mix(j):
        at_first(j, t2, gains, wo)
        heads.wait(j)
        rows = span(j)
        second = t2[rows] + heads.mix(j, wo)
        t3[rows] = second
        late = normalize(second, gains[1:2])
        t4[rows] = late
        low.put(j, late.astype(BF16))

    def feed(j):
        at_first(j, w1, w2, wd, wu)
        low.wait(j)
        piece, slope, side_rows, slope_side = feed_rows(low.both(j), w1, w2, wd, wu)
        ahead.put(j, piece)
        inner_slope[j] = slope
        side[j] = side_rows
        side_slope[j] = slope_side

    def turn(j):
        at_first(j, real, cotangent)
        rows = span(j)
        third = t4[rows] + ahead.get(j)
        mask = real[rows]
        grad = normalize_back(third, gains[2:3], cotangent[rows].astype(F32) * mask)
        back3.put(j, grad.astype(BF16))
        g3[rows] = grad
        result.put(j, normalize(third, gains[2:3]) * mask)

    def feed_back(j):
        back3.wait(j)
        grads = back3.both(j)
        four = (4.0 * grads.astype(F32)).astype(BF16)
        piece, grad_side = feed_rows_back(grads, four, inner_slope[j], side_slope[j], w1, w2, wd, wu)
        behind.put(j, piece)
        down_grad[...] += mm_tn(low.both(j), grad_side)
        up_grad[...] += mm_tn(four, side[j])

        @pl.when(j == n - 1)
        def _():
            put_weight_terms(terms, down_grad, up_grad)
            terms.flush(0)

    def finish(j):
        rows = span(j)
        grad = normalize_back(t3[rows], gains[1:2], g3[rows] + behind.get(j))
        back2.put(j, grad.astype(BF16))
        g2[rows] = grad
        g2.flush(j)

    def heads_back(j):
        at_first(j, mixing)
        back2.wait(j)
        put_both(place, da, j, mm_nt(back2.both(j), mixing[...]).astype(BF16))
        da.flush(j)

    pipeline(
        [
            (2, n, ahead.middle), (6, n, behind.middle), (0, n, mix), (1, n, feed), (4, n, turn),
            (5, n, feed_back), (8, n, finish), (9, n, heads_back),
        ]
    )
    each(
        n, heads.drain, low.drain, ahead.drain, result.drain, back3.drain, behind.drain, back2.drain,
        g2.drain, da.drain,
    )
    terms.drain(0)


def key_rows(place, halo, j, scratch, own, from_before, from_after):
    for hh in range(2):
        scratch[hh] = halo.gathered(j, hh, own, from_before, from_after).astype(BF16)
    return [
        jnp.concatenate([scratch[place.core, i], scratch[place.other, i]], axis=0) for i in range(2)
    ]


def backward_kernel(
    n_seq, halo_rows,
    dbefore_, dafter_, dkv_, wkv_, e3_, e1_, gains_, hidden_, slope_, side_, side_slope_, w1_, w2_, wd_, wu_,
    mixing_, dq_, dg2_, t1_, dgains_, dwq_, dmixing_, dterms_,
    g1_, da_, terms_, dg1_, dda_, ddown_, dup_,
    dbefore, dafter, dkv, wkv, e3, e1, gains, hidden, slope, side, side_slope, w1, w2, wd, wu,
    mixing, dq, dg2, t1, dgains, dwq, dmixing, seq_terms,
    g1, da, terms, dg1, dda, ddown, dup, down_grad, up_grad,
    from_before, from_after, rounded, g2, low_g2, low_g1,
    f0, f1, f2, f3, f4, b0, b1, b2, b3, b4, dlow_g1, d0, d1, d2, d3, d4,
    seq_landing, seq_total, seq_sent, seq_came,
    loading, local_sems, send, receive,
):
    place, sems, local = Place(n_seq), Sems(send, receive), Sems(local_sems, local_sems)
    half, dec_half = e1.shape[0], t1.shape[0]
    n, m = half // SEGMENT, dec_half // SEGMENT
    dbefore = Loaded(dbefore_, dbefore, loading.at[0])
    dafter = Loaded(dafter_, dafter, loading.at[1])
    dterms = Loaded(dterms_, seq_terms, loading.at[22])
    seq_sum = SeqSum(place, (seq_terms, seq_landing, seq_total, seq_sent, seq_came))
    dq = Loaded(dq_, dq, loading.at[16])
    dwq = Loaded(dwq_, dwq, loading.at[20])
    dkv = Loaded(dkv_, dkv, loading.at[2])
    wkv = Loaded(wkv_, wkv, loading.at[3])
    e3 = Loaded(e3_, e3, loading.at[4])
    gains = Loaded(gains_, gains, loading.at[6])
    dg2 = Loaded(dg2_, dg2, loading.at[17])
    t1 = Loaded(t1_, t1, loading.at[18])
    dgains = Loaded(dgains_, dgains, loading.at[19])
    dmixing = Loaded(dmixing_, dmixing, loading.at[21])
    hidden = Loaded(hidden_, hidden, loading.at[7])
    slope = Loaded(slope_, slope, loading.at[8])
    side = Loaded(side_, side, loading.at[9])
    side_slope = Loaded(side_slope_, side_slope, loading.at[10])
    w1 = Loaded(w1_, w1, loading.at[11])
    w2 = Loaded(w2_, w2, loading.at[12])
    wd = Loaded(wd_, wd, loading.at[13])
    wu = Loaded(wu_, wu, loading.at[14])
    e1 = Loaded(e1_, e1, loading.at[5])
    mixing = Loaded(mixing_, mixing, loading.at[15])
    rows_j, both_j = rows_of(place), both_rows(place)
    g1 = Stored(local, g1_, g1, rows_j)
    da = Stored(local, da_, da, both_j)
    terms = Stored(local, terms_, terms, lambda j: [slice(None)])
    dg1 = Stored(local, dg1_, dg1, rows_j)
    dda = Stored(local, dda_, dda, both_j)
    ddown = Stored(local, ddown_, ddown, lambda j: [slice(None)])
    dup = Stored(local, dup_, dup, lambda j: [slice(None)])
    halo = Halo(place, sems, 2 * half, halo_rows)
    first = Total(place, sems, (f0, f1, f2, f3, f4))
    back2 = Twins(place, sems, low_g2)
    second = Total(place, sems, (b0, b1, b2, b3, b4))
    back1 = Twins(place, sems, low_g1)
    dec_total = Total(place, sems, (d0, d1, d2, d3, d4))
    dec_back = Twins(place, sems, dlow_g1)
    place.greet([place.twin, place.across], True)
    dbefore.wait()
    dafter.wait()

    def leave(j):
        for copy in halo.back_copies(j, dbefore, dafter, from_before, from_after):
            copy.start()

    each(n, leave)
    dterms.wait()
    seq_sum.start()
    down_grad[...] = jnp.zeros(down_grad.shape, F32)
    up_grad[...] = jnp.zeros(up_grad.shape, F32)

    def start(j):
        at_first(j, dkv, wkv)
        for copy in halo.back_copies(j, dbefore, dafter, from_before, from_after):
            copy.wait_recv()
        key_grad, value_grad = key_rows(place, halo, j, rounded, dkv, from_before, from_after)
        first.put(j, mm_nt(key_grad, wkv[0]) + mm_nt(value_grad, wkv[1]))

    def turn(j):
        at_first(j, e3, gains)
        rows = span(j)
        grad = normalize_back(e3[rows], gains[1:2], first.get(j))
        g2[rows] = grad
        back2.put(j, grad.astype(BF16))

    def feed_back(j):
        at_first(j, hidden, slope, side, side_slope, w1, w2, wd, wu)
        back2.wait(j)
        grads = back2.both(j)
        four = (4.0 * grads.astype(F32)).astype(BF16)
        piece, grad_side = feed_rows_back(grads, four, slope[j], side_slope[j], w1, w2, wd, wu)
        second.put(j, piece)
        down_grad[...] += mm_tn(own_first(place, hidden, j), grad_side)
        up_grad[...] += mm_tn(four, side[j])

        @pl.when(j == n - 1)
        def _():
            put_weight_terms(terms, down_grad, up_grad)
            terms.flush(0)

    def finish(j):
        at_first(j, e1)
        rows = span(j)
        grad = normalize_back(e1[rows], gains[0:1], g2[rows] + second.get(j))
        back1.put(j, grad.astype(BF16))
        g1[rows] = grad
        g1.flush(j)

    def heads_back(j):
        at_first(j, mixing)
        back1.wait(j)
        put_both(place, da, j, mm_nt(back1.both(j), mixing[...]).astype(BF16))
        da.flush(j)

    def dec_start(j):
        at_first(j, dq, dwq)
        dec_total.put(j, mm_nt(own_first(place, dq, j), dwq[...]))

    def dec_finish(j):
        at_first(j, dg2, t1, dgains)
        rows = span(j)
        grad = normalize_back(t1[rows], dgains[0:1], dg2[rows] + dec_total.get(j))
        dec_back.put(j, grad.astype(BF16))
        dg1[rows] = grad
        dg1.flush(j)

    def dec_heads_back(j):
        at_first(j, dmixing)
        dec_back.wait(j)
        put_both(place, dda, j, mm_nt(dec_back.both(j), dmixing[...]).astype(BF16))
        dda.flush(j)

    pipeline(
        [
            (1, m, dec_total.middle), (1, n, first.middle), (5, n, second.middle), (0, m, dec_start),
            (0, n, start), (3, n, turn), (4, n, feed_back), (5, m, dec_finish), (6, m, dec_heads_back),
            (7, n, finish), (8, n, heads_back), (n, 1, seq_sum.add),
        ]
    )
    seq_sum.wait()
    rows = ddown.shape[0]
    ddown[...] = seq_total[0:rows].astype(F32)
    dup[...] = seq_total[rows : 2 * rows].astype(F32).T
    ddown.flush(0)
    dup.flush(0)
    seq_sum.drain()

    def left(j):
        for copy in halo.back_copies(j, dbefore, dafter, from_before, from_after):
            copy.wait_send()

    each(n, left, first.drain, back2.drain, second.drain, back1.drain, g1.drain, da.drain)
    each(m, dec_total.drain, dec_back.drain, dg1.drain, dda.drain)
    terms.drain(0)
    ddown.drain(0)
    dup.drain(0)


def input_back_kernel(n_seq, halos, *refs):
    refs = list(refs)

    def take(count):
        taken = refs[:count]
        del refs[:count]
        return taken

    operands = [take(6), take(6)]
    term_operands = take(4)
    results = take(2)
    sum_results = take(5)
    buffers = [take(6), take(6)]
    take(4)
    stages = take(2)
    sums = take(5)
    scratch = [take(8), take(8)]
    seq_refs = take(5)
    loading, local_sems, send, receive = refs
    place, sems, local = Place(n_seq), Sems(send, receive), Sems(local_sems, local_sems)
    loads = [
        [Loaded(src, buf, loading.at[6 * k + i]) for i, (src, buf) in enumerate(zip(operands[k], buffers[k]))]
        for k in range(2)
    ]
    seq_terms = seq_refs[0]
    seq_sum = SeqSum(place, seq_refs)
    at, term_loads = 0, []
    for i, term in enumerate(term_operands):
        term_loads.append(Loaded(term, seq_terms.at[at : at + term.shape[0]], loading.at[12 + i]))
        at += term.shape[0]
    sums = [Stored(local, result, buf, lambda j: [slice(None)]) for result, buf in zip(sum_results, sums)]
    seq_terms[at:] = jnp.zeros((seq_terms.shape[0] - at, 128), BF16)
    place.greet([place.twin, place.across], True)
    pieces, drains = [], []
    for k in range(2):
        dbefore, dafter, dq, dkv, weights, g1 = loads[k]
        from_before, from_after, rounded = scratch[k][:3]
        half = stages[k].shape[0]
        n = half // SEGMENT
        halo = Halo(place, sems, 2 * half, halos[k])
        total = Total(place, sems, scratch[k][3:])
        result = TwinResult(place, sems, local, results[k], stages[k])
        dbefore.wait()
        dafter.wait()

        def copies(j, halo=halo, refs=(dbefore, dafter, from_before, from_after)):
            return halo.back_copies(j, *refs)

        def leave(j, copies=copies):
            for copy in copies(j):
                copy.start()

        def start(j, k=k, halo=halo, total=total, copies=copies):
            dbefore, dafter, dq, dkv, weights, g1 = loads[k]
            from_before, from_after, rounded = scratch[k][:3]
            at_first(j, dq, dkv, weights)
            for copy in copies(j):
                copy.wait_recv()
            key_grad, value_grad = key_rows(place, halo, j, rounded, dkv, from_before, from_after)
            piece = mm_nt(own_first(place, dq, j), weights[0])
            total.put(j, piece + mm_nt(key_grad, weights[1]) + mm_nt(value_grad, weights[2]))

        def finish(j, g1=g1, total=total, result=result):
            at_first(j, g1)
            result.put(j, g1[span(j)] + total.get(j))

        def left(j, copies=copies):
            for copy in copies(j):
                copy.wait_send()

        each(n, leave)
        pieces.append((n, start, total, finish))
        drains.append((n, left, total.drain, result.drain))
    for load in term_loads:
        load.wait()
    seq_sum.start()
    stages_ = [(6, 1, seq_sum.add)]
    for offset, (n, start, total, finish) in zip((0, 2), pieces):
        stages_ += [(offset + 1, n, total.middle), (offset, n, start), (offset + 3, n, finish)]
    pipeline(stages_)
    seq_sum.wait()
    seq_total = seq_refs[2]
    rows = sums[0].shape[0]
    sums[0][...] = seq_total[0:rows].astype(F32)
    sums[1][...] = seq_total[rows : 2 * rows].astype(F32).T
    at = 2 * rows
    for k in range(2, 5):
        for i in range(2):
            for c in range(2):
                part = seq_total[at : at + PREFIX_ROWS].astype(F32)
                sums[k][i, :, c * 128 : (c + 1) * 128] = part[0:PREFIX]
                at += PREFIX_ROWS
    for result in sums:
        result.flush(0)
    for n, *actions in drains:
        each(n, *actions)
    seq_sum.drain()
    for result in sums:
        result.drain(0)


def document_plan(query_docs, key_docs, query_rows, key_rows_, halo, block, causal):
    s = lax.axis_index("seq")
    own = lax.dynamic_slice_in_dim(query_docs, s * query_rows, query_rows)
    filler = jnp.full((halo,), -1, jnp.int32)
    padded = jnp.concatenate([filler, key_docs, filler])
    window = key_rows_ + 2 * halo
    keys = lax.dynamic_slice_in_dim(padded, s * key_rows_, window)
    blocks = own.reshape(-1, block)
    top = jnp.max(blocks, axis=1)
    bottom = jnp.min(jnp.where(blocks >= 0, blocks, 2**30), axis=1)
    read = (keys[None] >= bottom[:, None]) & (keys[None] <= top[:, None])
    index = jnp.arange(window, dtype=jnp.int32)[None]
    lo = jnp.min(jnp.where(read, index, window), axis=1) // KEY_BLOCK
    hi = (jnp.max(jnp.where(read, index + 1, 0), axis=1) + KEY_BLOCK - 1) // KEY_BLOCK
    if causal:
        ends = halo + block * (1 + jnp.arange(blocks.shape[0], dtype=jnp.int32))
        hi = jnp.minimum(hi, (ends + KEY_BLOCK - 1) // KEY_BLOCK)
    rows = jnp.where(blocks >= 0, blocks, -2)[:, None, :]
    return rows, keys[:, None], lo, hi


def halo_parts(kv, halo):
    size = lax.axis_size("seq")
    rows = kv.shape[1]
    up = [(i, i + 1) for i in range(size - 1)]
    down = [(i + 1, i) for i in range(size - 1)]
    before = lax.ppermute(kv[:, rows - halo :], "seq", up)
    after = lax.ppermute(kv[:, :halo], "seq", down)
    return before, kv, after


def halves(array):
    return array.reshape((2, array.shape[0] // 2) + array.shape[1:])


def exchange_scratch(half, *kinds):
    shapes = []
    for kind in kinds:
        if kind == "total":
            shapes += Total.SHAPES(half)
        else:
            shape, dtype = kind
            shapes.append(pltpu.VMEM(shape, dtype))
    return shapes


def reaches_far(n_seq, source_document, target_document):
    source_docs = source_document.reshape(n_seq, -1)
    target_docs = target_document.reshape(n_seq, -1)

    def smallest(docs):
        return jnp.min(jnp.where(docs >= 0, docs, 2**30), axis=1)

    lows = jnp.minimum(smallest(source_docs), smallest(target_docs))
    highs = jnp.maximum(jnp.max(source_docs, axis=1), jnp.max(target_docs, axis=1))
    after_low = jnp.concatenate([lows[1:], jnp.full((1,), 2**30, jnp.int32)])[:, None]
    before_high = jnp.concatenate([jnp.full((1,), -1, jnp.int32), highs[:-1]])[:, None]
    far = False
    for docs in (source_docs, target_docs):
        half = docs.shape[1] // 2
        far = far | jnp.any(docs[:, :half] >= after_low)
        far = far | jnp.any((docs[:, half:] >= 0) & (docs[:, half:] <= before_high))
    return far


def on_device(n_seq, *args):
    far = reaches_far(n_seq, args[2], args[3])
    return lax.cond(far, partial(on_device_with, n_seq, True), partial(on_device_with, n_seq, False), *args)


def on_device_with(
    n_seq,
    wide,
    source,
    target,
    source_document,
    target_document,
    cotangent,
    encoder_attention,
    encoder_mixing,
    encoder_gains,
    encoder_inner,
    encoder_outer,
    encoder_prefix,
    encoder_down,
    encoder_up,
    decoder_attention,
    decoder_mixing,
    decoder_prefix,
    cross_query,
    cross_memory,
    cross_mixing,
    cross_prefix,
    decoder_gains,
    decoder_inner,
    decoder_outer,
    decoder_down,
    decoder_up,
):
    ids = iter(range(1 + 16 * int(wide), 100))
    source_rows, width = source.shape
    target_rows = target.shape[0]
    cols = encoder_mixing.shape[0]
    hidden = encoder_inner.shape[1]
    adapt = encoder_down.shape[1]
    source_halo = source_rows if wide else source_rows // 2
    target_halo = target_rows if wide else target_rows // 2
    source_half, target_half = source_rows // 2, target_rows // 2
    source_n, target_n = source_half // SEGMENT, target_half // SEGMENT
    chunk = 2 * SEGMENT

    encoder_wo = lax.all_gather(encoder_mixing, "tp")
    decoder_wo = lax.all_gather(decoder_mixing, "tp")
    cross_wo = lax.all_gather(cross_mixing, "tp")

    def padded(prefix):
        return jnp.pad(prefix, ((0, 0), (0, PREFIX_ROWS - prefix.shape[1]), (0, 0)))

    encoder_prefix, decoder_prefix, cross_prefix = map(padded, (encoder_prefix, decoder_prefix, cross_prefix))

    encoder_q, encoder_kv = project(source, encoder_attention)
    encoder_parts = halo_parts(encoder_kv, source_halo)
    decoder_q, decoder_kv = project(target, decoder_attention)
    decoder_parts = halo_parts(decoder_kv, target_halo)

    encoder_docs = document_plan(
        source_document, source_document, source_rows, source_rows, source_halo, 256, False
    )
    decoder_docs = document_plan(
        target_document, target_document, target_rows, target_rows, target_halo, 128, True
    )
    cross_docs = document_plan(
        target_document, source_document, target_rows, source_rows, source_halo, 128, False
    )
    own_target = lax.dynamic_slice_in_dim(target_document, lax.axis_index("seq") * target_rows, target_rows)
    real = halves((own_target >= 0).astype(F32)[:, None])

    encoder_wide, encoder_low, encoder_total = attend(
        encoder_q, encoder_parts, encoder_prefix, encoder_docs, False
    )
    decoder_wide, decoder_low, decoder_total = attend(
        decoder_q, decoder_parts, decoder_prefix, decoder_docs, True
    )
    gathered_source = ((source_half, width), F32)
    gathered_target = ((target_half, width), F32)
    source_low = ((2, source_half, width), BF16)
    target_low = ((2, target_half, width), BF16)
    source_cols = ((2, source_half, cols), BF16)
    target_cols = ((2, target_half, cols), BF16)
    slopes = [((source_n, chunk, hidden), BF16), ((source_n, chunk, adapt), BF16), ((source_n, chunk, adapt), BF16)]
    halo_cols = ((2, source_halo, cols), BF16)
    kv_cols = ((2, source_rows, cols), BF16)
    stored = [gathered_source, gathered_source, source_low, *slopes, kv_cols]
    stored_target = [gathered_target, gathered_target, target_cols]
    args = (
        halves(encoder_low), halves(source), encoder_gains, encoder_wo, encoder_inner, encoder_outer,
        encoder_down, encoder_up, cross_memory, halves(decoder_low), halves(target), decoder_gains,
        decoder_wo, cross_query,
    )
    loads = [a.shape for a in args]
    loads[1], loads[10] = (source_half, width), (target_half, width)
    (
        e1, e3, encoder_hidden, encoder_slope, encoder_side, encoder_side_slope, cross_kv, cross_before,
        cross_after, t1, t2, cross_q,
    ) = exchange_call(
        partial(forward_kernel, n_seq, source_halo),
        next(ids),
        args,
        loads,
        [*stored, halo_cols, halo_cols, *stored_target],
        exchange_scratch(
            source_half,
            *stored,
            *stored_target,
            ((4, source_half, cols), BF16),
            gathered_source,
            "total",
            source_low,
            ((4, target_half, cols), BF16),
            target_low,
        ),
        3 + 1 + 2 + 1 + (4 if wide else 2) + 3 + 1,
        10,
        source_n,
        2 * source_rows * width * (2 * hidden + 2 * adapt + 6 * cols),
    )
    cross_parts = (cross_before, cross_kv, cross_after)
    cross_q = cross_q.reshape(target_rows, cols)
    cross_wide, cross_low, cross_total = attend(cross_q, cross_parts, cross_prefix, cross_docs, False)

    weight_grads = [((width, adapt), F32), ((width, adapt), F32)]
    weight_terms = ((2 * width, adapt), BF16)
    weight_sums = [((width, adapt), F32), ((adapt, width), F32)]
    args = (
        halves(cross_low), t2, real, halves(cotangent), decoder_gains, cross_wo, decoder_inner,
        decoder_outer, decoder_down, decoder_up, cross_mixing,
    )
    loads = [a.shape for a in args]
    loads[2], loads[3] = (target_half, 1), (target_half, width)
    stored = [gathered_target, target_cols, weight_terms]
    decoded, g2, cross_da, decoder_terms = exchange_call(
        partial(decoder_chain_kernel, n_seq),
        next(ids),
        args,
        loads,
        [((2, target_half, width), F32), *stored],
        exchange_scratch(
            target_half,
            *stored,
            *weight_grads,
            gathered_target,
            ((4, target_half, cols), BF16),
            gathered_target,
            gathered_target,
            gathered_target,
            target_low,
            target_low,
            target_low,
            ((target_n, chunk, hidden), BF16),
            ((target_n, chunk, adapt), BF16),
            ((target_n, chunk, adapt), BF16),
            "total",
            "total",
        ),
        3 + 1 + 2 + 1 + 1 + 2 + 1,
        4,
        target_n,
        2 * target_rows * width * (4 * hidden + 6 * adapt + 2 * cols),
    )
    cross_dq, cross_dbefore, cross_dkv, cross_dafter, cross_prefix_terms = attend_back(
        cross_q, cross_da.reshape(target_rows, cols), cross_wide, cross_total, cross_parts, cross_prefix,
        cross_docs, False,
    )
    args = (
        cross_dbefore, cross_dafter, cross_dkv, cross_memory, e3, e1, encoder_gains, encoder_hidden,
        encoder_slope, encoder_side, encoder_side_slope, encoder_inner, encoder_outer, encoder_down,
        encoder_up, encoder_mixing, halves(cross_dq), g2, t1, decoder_gains, cross_query, decoder_mixing,
        decoder_terms,
    )
    stored = [gathered_source, source_cols, weight_terms, gathered_target, target_cols, *weight_sums]
    (
        encoder_g1, encoder_da, encoder_terms, decoder_g1, decoder_da, decoder_down_gradient, decoder_up_gradient,
    ) = exchange_call(
        partial(backward_kernel, n_seq, source_halo),
        next(ids),
        args,
        [a.shape for a in args],
        stored,
        exchange_scratch(
            source_half,
            *stored,
            *weight_grads,
            halo_cols,
            halo_cols,
            ((2, 2, SEGMENT, cols), BF16),
            gathered_source,
            source_low,
            source_low,
            "total",
            "total",
            target_low,
        )
        + exchange_scratch(target_half, "total")
        + SeqSum.scratch(n_seq, 2 * width)[1:],
        (4 if wide else 2) + 2 + 1 + 2 + 1 + 2 + 1,
        7,
        source_n,
        2 * source_rows * width * (2 * hidden + 4 * adapt + 4 * cols),
    )
    ddq, ddbefore, ddkv, ddafter, decoder_prefix_terms = attend_back(
        decoder_q, decoder_da.reshape(target_rows, cols), decoder_wide, decoder_total, decoder_parts,
        decoder_prefix, decoder_docs, True,
    )
    edq, edbefore, edkv, edafter, encoder_prefix_terms = attend_back(
        encoder_q, encoder_da.reshape(source_rows, cols), encoder_wide, encoder_total, encoder_parts,
        encoder_prefix, encoder_docs, False,
    )
    args = (
        edbefore, edafter, halves(edq), edkv, encoder_attention, encoder_g1,
        ddbefore, ddafter, halves(ddq), ddkv, decoder_attention, decoder_g1,
        encoder_terms, encoder_prefix_terms, decoder_prefix_terms, cross_prefix_terms,
    )
    loads = [a.shape for a in args[:12]] + [(16, 128)] * 4
    prefix_sum = ((2, PREFIX, cols), F32)
    results = [*weight_sums, prefix_sum, prefix_sum, prefix_sum]
    seq_rows = 2 * width + 512
    (
        source_gradient, target_gradient, encoder_down_gradient, encoder_up_gradient, encoder_prefix_gradient,
        decoder_prefix_gradient, cross_prefix_gradient,
    ) = exchange_call(
        partial(input_back_kernel, n_seq, (source_halo, target_halo)),
        next(ids),
        args,
        loads,
        [((2, source_half, width), F32), ((2, target_half, width), F32), *results],
        exchange_scratch(source_half, gathered_source, gathered_target, *results)
        + exchange_scratch(source_half, halo_cols, halo_cols, ((2, 2, SEGMENT, cols), BF16), "total")
        + exchange_scratch(
            target_half,
            ((2, target_halo, cols), BF16),
            ((2, target_halo, cols), BF16),
            ((2, 2, SEGMENT, cols), BF16),
            "total",
        )
        + SeqSum.scratch(n_seq, seq_rows),
        2 * ((4 if wide else 2) + 2 + 1),
        7,
        source_n,
        6 * (source_rows + target_rows) * width * cols,
    )
    source_gradient = source_gradient.reshape(source_rows, width)
    target_gradient = target_gradient.reshape(target_rows, width)

    weight_totals = (
        encoder_prefix_gradient,
        encoder_down_gradient,
        encoder_up_gradient,
        decoder_prefix_gradient,
        cross_prefix_gradient,
        decoder_down_gradient,
        decoder_up_gradient,
    )
    return (decoded.reshape(target_rows, width), source_gradient, target_gradient) + tuple(weight_totals)


def solution(mesh):
    return jax.shard_map(
        partial(on_device, mesh.shape["seq"]),
        mesh=mesh,
        in_specs=(
            P("seq", None),
            P("seq", None),
            P(),
            P(),
            P("seq", None),
            P(None, None, "tp"),
            P("tp", None),
            P(),
            P(None, "tp"),
            P("tp", None),
            P(None, None, "tp"),
            P(None, "tp"),
            P("tp", None),
            P(None, None, "tp"),
            P("tp", None),
            P(None, None, "tp"),
            P(None, "tp"),
            P(None, None, "tp"),
            P("tp", None),
            P(None, None, "tp"),
            P(),
            P(None, "tp"),
            P("tp", None),
            P(None, "tp"),
            P("tp", None),
        ),
        out_specs=(
            P("seq", None),
            P("seq", None),
            P("seq", None),
            P(None, None, "tp"),
            P(None, "tp"),
            P("tp", None),
            P(None, None, "tp"),
            P(None, None, "tp"),
            P(None, "tp"),
            P("tp", None),
        ),
        check_vma=False,
    )
```

```python
from functools import partial

import jax
import jax.numpy as jnp
from jax import lax
from jax.experimental import pallas as pl
from jax.experimental.pallas import tpu as pltpu
from jax.sharding import PartitionSpec as P

HEAD_DIM = 64
EPSILON = 1e-05
NEGATIVE = -1e30
HEADS = 4
KEY_BLOCK = 256
QUERY_BLOCK = 256
PREFIX = 30
PREFIX_ROWS = 32
SEGMENT = 64
MESH = pl.DeviceIdType.MESH
F32 = jnp.float32
BF16 = jnp.bfloat16
VMEM_BYTES = 56 * 2**20


def mm(left, right):
    return jnp.dot(left, right, preferred_element_type=F32)


def mm_nt(left, right):
    return lax.dot_general(left, right, (((1,), (1,)), ((), ())), preferred_element_type=F32)


def mm_tn(left, right):
    return lax.dot_general(left, right, (((0,), (0,)), ((), ())), preferred_element_type=F32)


def normalize(inputs, scaling):
    centered = inputs - jnp.mean(inputs, axis=-1, keepdims=True)
    spread = lax.rsqrt(jnp.mean(centered * centered, axis=-1, keepdims=True) + EPSILON)
    return scaling * (centered * spread)


def normalize_back(inputs, scaling, gradient):
    centered = inputs - jnp.mean(inputs, axis=-1, keepdims=True)
    spread = lax.rsqrt(jnp.mean(centered * centered, axis=-1, keepdims=True) + EPSILON)
    unit = centered * spread
    scaled = gradient * scaling
    first = jnp.mean(scaled, axis=-1, keepdims=True)
    second = jnp.mean(scaled * unit, axis=-1, keepdims=True)
    return spread * (scaled - first - unit * second)


def gelu_parts(inputs):
    chance = 0.5 * (1.0 + lax.erf(inputs * (0.5**0.5)))
    density = jnp.exp(-0.5 * inputs * inputs) * 0.3989422804014327
    return (inputs * chance).astype(BF16), (chance + inputs * density).astype(BF16)


def project_kernel(x_ref, w_ref, q_ref, kv_ref):
    rows = x_ref[...]
    q_ref[...] = mm(rows, w_ref[0]).astype(BF16)
    kv_ref[0] = mm(rows, w_ref[1]).astype(BF16)
    kv_ref[1] = mm(rows, w_ref[2]).astype(BF16)


def project(inputs, weights):
    rows, width = inputs.shape
    block = 256
    cols = weights.shape[2]
    return pl.pallas_call(
        project_kernel,
        grid=(rows // block,),
        in_specs=[
            pl.BlockSpec((block, width), lambda i: (i, 0)),
            pl.BlockSpec(weights.shape, lambda i: (0, 0, 0)),
        ],
        out_specs=[
            pl.BlockSpec((block, cols), lambda i: (i, 0)),
            pl.BlockSpec((2, block, cols), lambda i: (0, i, 0)),
        ],
        out_shape=[
            jax.ShapeDtypeStruct((rows, cols), BF16),
            jax.ShapeDtypeStruct((2, rows, cols), BF16),
        ],
        compiler_params=pltpu.CompilerParams(vmem_limit_bytes=VMEM_BYTES),
        cost_estimate=pl.CostEstimate(
            flops=6 * rows * width * cols, bytes_accessed=8 * rows * cols + 6 * width * cols, transcendentals=0
        ),
    )(inputs, weights)


def by_heads(rows, lane_head):
    zero = jnp.zeros_like(rows)
    return jnp.concatenate([jnp.where(lane_head == h, rows, zero) for h in range(HEADS)], axis=0)


def head_bias(kd_ref, qd_ref, start, first_query, halo, block, causal):
    key_doc = kd_ref[pl.ds(start, KEY_BLOCK), :]
    allowed = key_doc == qd_ref[0]
    if causal:
        key_place = start - halo + lax.broadcasted_iota(jnp.int32, (KEY_BLOCK, block), 0)
        query_place = first_query + lax.broadcasted_iota(jnp.int32, (KEY_BLOCK, block), 1)
        allowed = allowed & (key_place <= query_place)
    bias = jnp.where(allowed, 0.0, NEGATIVE)
    return jnp.concatenate([bias] * HEADS, axis=1)


def prefix_scores(pre_ref, stacked):
    scores = mm_nt(pre_ref[0], stacked)
    row = lax.broadcasted_iota(jnp.int32, scores.shape, 0)
    return jnp.where(row < PREFIX, scores, NEGATIVE)


def fill_window(window, parts, index):
    at = 0
    for part in parts:
        size = part.shape[1]
        window[at : at + size, :] = part[index]
        at += size


def attend_kernel(
    halo, causal, lo_ref, hi_ref, q_ref, bef_ref, own_ref, aft_ref, pre_ref, qd_ref, kd_ref,
    wide_ref, low_ref, total_ref, keys, values, blended,
):
    i = pl.program_id(0)
    block = q_ref.shape[0]
    parts = (bef_ref, own_ref, aft_ref)

    @pl.when(i == 0)
    def _():
        fill_window(keys, parts, 0)
        at = 0
        for part in parts:
            for k in range(part.shape[1] // KEY_BLOCK):
                values[at] = part[1, k * KEY_BLOCK : (k + 1) * KEY_BLOCK, :].T
                at += 1

    lane_head = lax.broadcasted_iota(jnp.int32, q_ref.shape, 1) // HEAD_DIM
    stacked = by_heads(q_ref[...] * jnp.asarray(HEAD_DIM**-0.5, BF16), lane_head)
    scores = prefix_scores(pre_ref, stacked)
    highest = jnp.max(scores, axis=0, keepdims=True)
    chances = jnp.exp(scores - highest)
    summed = jnp.sum(chances, axis=0, keepdims=True)
    low = chances.astype(BF16)
    pre_values = pre_ref[1].T
    for h in range(HEADS):
        rows = slice(h * HEAD_DIM, (h + 1) * HEAD_DIM)
        blended[rows, :] = mm(pre_values[rows, :], low[:, h * block : (h + 1) * block])

    def step(kb, carry):
        highest, summed = carry
        start = pl.multiple_of(kb * KEY_BLOCK, KEY_BLOCK)
        scores = mm_nt(keys[pl.ds(start, KEY_BLOCK), :], stacked)
        scores = scores + head_bias(kd_ref, qd_ref, start, i * block, halo, block, causal)
        top = jnp.maximum(highest, jnp.max(scores, axis=0, keepdims=True))
        fade = jnp.exp(highest - top)
        chances = jnp.exp(scores - top)
        summed = summed * fade + jnp.sum(chances, axis=0, keepdims=True)
        low = chances.astype(BF16)
        for h in range(HEADS):
            rows = slice(h * HEAD_DIM, (h + 1) * HEAD_DIM)
            cols = slice(h * block, (h + 1) * block)
            blended[rows, :] = blended[rows, :] * fade[:, cols] + mm(values[kb, rows, :], low[:, cols])
        return top, summed

    highest, summed = lax.fori_loop(lo_ref[i], hi_ref[i], step, (highest, summed))
    total_ref[0] = highest + jnp.log(summed)
    inverse = 1.0 / summed
    for h in range(HEADS):
        rows = slice(h * HEAD_DIM, (h + 1) * HEAD_DIM)
        blended[rows, :] = blended[rows, :] * inverse[:, h * block : (h + 1) * block]
    result = blended[...].T
    wide_ref[...] = result
    low_ref[...] = result.astype(BF16)


def attend(queries, parts, prefix, docs, causal):
    query_doc, key_doc, lo, hi = docs
    rows, cols = queries.shape
    count, _, block = query_doc.shape
    window = key_doc.shape[0]
    halo = parts[0].shape[1]

    def whole(array):
        return pl.BlockSpec(array.shape, lambda i, *_: (0,) * array.ndim)

    return pl.pallas_call(
        partial(attend_kernel, halo, causal),
        grid_spec=pltpu.PrefetchScalarGridSpec(
            num_scalar_prefetch=2,
            grid=(count,),
            in_specs=[
                pl.BlockSpec((block, cols), lambda i, *_: (i, 0)),
                whole(parts[0]),
                whole(parts[1]),
                whole(parts[2]),
                whole(prefix),
                pl.BlockSpec((1, 1, block), lambda i, *_: (i, 0, 0)),
                whole(key_doc),
            ],
            out_specs=[
                pl.BlockSpec((block, cols), lambda i, *_: (i, 0)),
                pl.BlockSpec((block, cols), lambda i, *_: (i, 0)),
                pl.BlockSpec((1, 1, HEADS * block), lambda i, *_: (i, 0, 0)),
            ],
            scratch_shapes=[
                pltpu.VMEM((window, cols), BF16),
                pltpu.VMEM((window // KEY_BLOCK, cols, KEY_BLOCK), BF16),
                pltpu.VMEM((cols, block), F32),
            ],
        ),
        out_shape=[
            jax.ShapeDtypeStruct((rows, cols), F32),
            jax.ShapeDtypeStruct((rows, cols), BF16),
            jax.ShapeDtypeStruct((count, 1, HEADS * block), F32),
        ],
        compiler_params=pltpu.CompilerParams(vmem_limit_bytes=VMEM_BYTES),
        cost_estimate=pl.CostEstimate(
            flops=16 * rows * 1024 * cols, bytes_accessed=8 * window * cols, transcendentals=4 * rows * 1024
        ),
    )(lo, hi, queries, *parts, prefix, query_doc, key_doc)


def attend_back_kernel(
    halo, causal, lo_ref, hi_ref, q_ref, g_ref, wide_ref, total_ref, bef_ref, own_ref, aft_ref, pre_ref,
    qd_ref, kd_ref, dq_ref, dbef_ref, down_ref, daft_ref, dpre_ref,
    keys, values, turned, key_sum, value_sum, query_sum, prefix_sum,
):
    i = pl.program_id(0)
    block = q_ref.shape[0]
    parts = (bef_ref, own_ref, aft_ref)

    @pl.when(i == 0)
    def _():
        fill_window(keys, parts, 0)
        fill_window(values, parts, 1)
        at = 0
        for part in parts:
            for k in range(part.shape[1] // KEY_BLOCK):
                turned[at] = part[0, k * KEY_BLOCK : (k + 1) * KEY_BLOCK, :].T
                at += 1
        key_sum[...] = jnp.zeros_like(key_sum)
        value_sum[...] = jnp.zeros_like(value_sum)
        prefix_sum[...] = jnp.zeros_like(prefix_sum)

    lane_head = lax.broadcasted_iota(jnp.int32, q_ref.shape, 1) // HEAD_DIM
    stacked = by_heads(q_ref[...] * jnp.asarray(HEAD_DIM**-0.5, BF16), lane_head)
    grads = by_heads(g_ref[...], lane_head)
    mixed = (g_ref[...].astype(F32) * wide_ref[...]).T
    offsets = jnp.concatenate(
        [
            jnp.sum(mixed[h * HEAD_DIM : (h + 1) * HEAD_DIM, :], axis=0, keepdims=True)
            for h in range(HEADS)
        ],
        axis=1,
    )
    total = total_ref[0]
    chances = jnp.exp(prefix_scores(pre_ref, stacked) - total)
    score_grad = (chances * (mm_nt(pre_ref[1], grads) - offsets)).astype(BF16)
    prefix_sum[0] += mm(score_grad, stacked)
    prefix_sum[1] += mm(chances.astype(BF16), grads)
    pre_keys = pre_ref[0].T
    for h in range(HEADS):
        rows = slice(h * HEAD_DIM, (h + 1) * HEAD_DIM)
        query_sum[rows, :] = mm(pre_keys[rows, :], score_grad[:, h * block : (h + 1) * block])

    def step(kb, carry):
        start = pl.multiple_of(kb * KEY_BLOCK, KEY_BLOCK)
        here = pl.ds(start, KEY_BLOCK)
        scores = mm_nt(keys[here, :], stacked)
        scores = scores + head_bias(kd_ref, qd_ref, start, i * block, halo, block, causal)
        chances = jnp.exp(scores - total)
        score_grad = (chances * (mm_nt(values[here, :], grads) - offsets)).astype(BF16)
        key_sum[here, :] += mm(score_grad, stacked)
        value_sum[here, :] += mm(chances.astype(BF16), grads)
        for h in range(HEADS):
            rows = slice(h * HEAD_DIM, (h + 1) * HEAD_DIM)
            query_sum[rows, :] += mm(turned[kb, rows, :], score_grad[:, h * block : (h + 1) * block])
        return carry

    lax.fori_loop(lo_ref[i], hi_ref[i], step, 0)
    dq_ref[...] = (query_sum[...].T * HEAD_DIM**-0.5).astype(BF16)

    @pl.when(i == pl.num_programs(0) - 1)
    def _():
        at = 0
        for part in (dbef_ref, down_ref, daft_ref):
            size = part.shape[1]
            part[0] = key_sum[at : at + size, :].astype(part.dtype)
            part[1] = value_sum[at : at + size, :].astype(part.dtype)
            at += size
        at = 0
        for k in range(2):
            for c in range(2):
                dpre_ref[at : at + PREFIX_ROWS, :] = prefix_sum[k, :, c * 128 : (c + 1) * 128].astype(BF16)
                at += PREFIX_ROWS


def attend_back(queries, grads, wide, total, parts, prefix, docs, causal):
    query_doc, key_doc, lo, hi = docs
    rows, cols = queries.shape
    count, _, block = query_doc.shape
    window = key_doc.shape[0]
    halo = parts[0].shape[1]

    def whole(shape):
        return pl.BlockSpec(shape, lambda i, *_: (0,) * len(shape))

    def blocked():
        return pl.BlockSpec((block, cols), lambda i, *_: (i, 0))

    return pl.pallas_call(
        partial(attend_back_kernel, halo, causal),
        grid_spec=pltpu.PrefetchScalarGridSpec(
            num_scalar_prefetch=2,
            grid=(count,),
            in_specs=[
                blocked(),
                blocked(),
                blocked(),
                pl.BlockSpec((1, 1, HEADS * block), lambda i, *_: (i, 0, 0)),
                whole(parts[0].shape),
                whole(parts[1].shape),
                whole(parts[2].shape),
                whole(prefix.shape),
                pl.BlockSpec((1, 1, block), lambda i, *_: (i, 0, 0)),
                whole(key_doc.shape),
            ],
            out_specs=[
                blocked(),
                whole(parts[0].shape),
                whole(parts[1].shape),
                whole(parts[2].shape),
                whole((4 * PREFIX_ROWS, 128)),
            ],
            scratch_shapes=[
                pltpu.VMEM((window, cols), BF16),
                pltpu.VMEM((window, cols), BF16),
                pltpu.VMEM((window // KEY_BLOCK, cols, KEY_BLOCK), BF16),
                pltpu.VMEM((window, cols), F32),
                pltpu.VMEM((window, cols), F32),
                pltpu.VMEM((cols, block), F32),
                pltpu.VMEM(prefix.shape, F32),
            ],
        ),
        out_shape=[
            jax.ShapeDtypeStruct((rows, cols), BF16),
            jax.ShapeDtypeStruct(parts[0].shape, BF16),
            jax.ShapeDtypeStruct(parts[1].shape, F32),
            jax.ShapeDtypeStruct(parts[2].shape, BF16),
            jax.ShapeDtypeStruct((4 * PREFIX_ROWS, 128), BF16),
        ],
        compiler_params=pltpu.CompilerParams(vmem_limit_bytes=VMEM_BYTES),
        cost_estimate=pl.CostEstimate(
            flops=40 * rows * 1024 * cols, bytes_accessed=16 * window * cols, transcendentals=4 * rows * 1024
        ),
    )(lo, hi, queries, grads, wide, total, *parts, prefix, query_doc, key_doc)


class Place:
    def __init__(self, n_seq):
        self.n_seq = n_seq
        self.s = lax.axis_index("seq")
        self.t = lax.axis_index("tp")
        self.core = self.t % 2
        self.other = 1 - self.core
        self.twin_t = self.t + 1 - 2 * self.core
        self.across_t = (self.t + 2) % 4
        self.corner_t = 3 - self.t
        self.twin = (self.s, self.twin_t)
        self.across = (self.s, self.across_t)
        self.corner = (self.s, self.corner_t)
        self.after = ((self.s + 1) % n_seq, self.t)
        self.before = ((self.s + n_seq - 1) % n_seq, self.t)

    def greet(self, partners, whole_seq=False):
        barrier = pltpu.get_barrier_semaphore()
        for partner in partners:
            pl.semaphore_signal(barrier, inc=1, device_id=partner, device_id_type=MESH)
        count = len(partners)
        if whole_seq:

            def signal(k, carry):
                pl.semaphore_signal(barrier, inc=1, device_id=self.along(k), device_id_type=MESH)
                return carry

            lax.fori_loop(1, self.n_seq, signal, 0)
            count += self.n_seq - 1
        pl.semaphore_wait(barrier, count)

    def along(self, k):
        return ((self.s + k) % self.n_seq, self.t)


class Sems:
    def __init__(self, send, receive):
        self.send, self.receive, self.used = send, receive, 0

    def take(self):
        kind = self.used
        self.used += 1
        return kind


def remote(sems, kind, j, src, dst, device):
    return pltpu.make_async_remote_copy(
        src_ref=src,
        dst_ref=dst,
        send_sem=sems.send.at[kind, j],
        recv_sem=sems.receive.at[kind, j],
        device_id=device,
        device_id_type=MESH,
    )


def span(j):
    return pl.ds(pl.multiple_of(j * SEGMENT, SEGMENT), SEGMENT)


class Loaded:
    def __init__(self, loads, buf, *sources):
        self.buf, self.at, self.shape = buf, buf.at, buf.shape
        self.copies = []
        for source, part in sources:
            target = buf if part is None else buf.at[part]
            self.copies.append(pltpu.make_async_copy(source, target, loads.send.at[loads.take()]))
        for copy in self.copies:
            copy.start()

    def wait(self):
        for copy in self.copies:
            copy.wait()

    def __getitem__(self, index):
        return self.buf[index]


class Stored:
    def __init__(self, sems, result, buf, parts):
        self.result, self.buf, self.parts, self.sems = result, buf, parts, sems
        self.at, self.shape = buf.at, buf.shape
        self.kind = sems.take()

    def copies(self, j):
        return [
            pltpu.make_async_copy(
                self.buf.at[part], self.result.at[part], self.sems.receive.at[self.kind, 2 * j + i]
            )
            for i, part in enumerate(self.parts(j))
        ]

    def flush(self, j):
        for copy in self.copies(j):
            copy.start()

    def drain(self, j):
        for copy in self.copies(j):
            copy.wait()

    def __getitem__(self, index):
        return self.buf[index]

    def __setitem__(self, index, value):
        self.buf[index] = value


class Twins:
    def __init__(self, place, sems, buf):
        self.place, self.sems, self.buf, self.kind = place, sems, buf, sems.take()

    def copy(self, j, half):
        part = self.buf.at[half, span(j)]
        return remote(self.sems, self.kind, j, part, part, self.place.twin)

    def put(self, j, value):
        self.buf[self.place.core, span(j)] = value
        self.copy(j, self.place.core).start()

    def wait(self, j):
        self.copy(j, self.place.other).wait_recv()

    def both(self, j):
        return jnp.concatenate([self.buf[self.place.core, span(j)], self.buf[self.place.other, span(j)]], axis=0)

    def drain(self, j):
        self.copy(j, self.place.core).wait_send()


class TwinResult:
    def __init__(self, place, sems, local, result, stage):
        self.place, self.sems, self.local, self.result, self.stage = place, sems, local, result, stage
        self.kind, self.kind_local = sems.take(), local.take()

    def copies(self, j):
        rows, core = span(j), self.place.core
        return (
            remote(self.sems, self.kind, j, self.stage.at[rows], self.result.at[core, rows], self.place.twin),
            pltpu.make_async_copy(
                self.stage.at[rows], self.result.at[core, rows], self.local.receive.at[self.kind_local, 2 * j]
            ),
        )

    def put(self, j, value):
        self.stage[span(j)] = value
        for copy in self.copies(j):
            copy.start()

    def drain(self, j):
        out, local = self.copies(j)
        out.wait_send()
        local.wait()
        part = self.result.at[self.place.other, span(j)]
        remote(self.sems, self.kind, j, part, part, self.place.twin).wait_recv()


class Total:
    SHAPES = staticmethod(
        lambda half: [
            pltpu.VMEM((half, 1024), F32),
            pltpu.VMEM((half, 1024), BF16),
            pltpu.VMEM((half, 1024), BF16),
            pltpu.VMEM((half, 1024), BF16),
            pltpu.VMEM((half, 1024), BF16),
        ]
    )

    def __init__(self, place, sems, refs):
        self.place, self.sems = place, sems
        self.mine, self.away, self.came, self.chip, self.far = refs
        self.kind_twin, self.kind_across = sems.take(), sems.take()

    def twin_copy(self, j):
        rows = span(j)
        return remote(self.sems, self.kind_twin, j, self.away.at[rows], self.came.at[rows], self.place.twin)

    def across_copy(self, j):
        rows = span(j)
        return remote(self.sems, self.kind_across, j, self.chip.at[rows], self.far.at[rows], self.place.across)

    def put(self, j, value):
        self.mine[span(j)] = value[:SEGMENT]
        self.away[span(j)] = value[SEGMENT:].astype(BF16)
        self.twin_copy(j).start()

    def middle(self, j):
        self.twin_copy(j).wait_recv()
        self.chip[span(j)] = (self.mine[span(j)] + self.came[span(j)].astype(F32)).astype(BF16)
        self.across_copy(j).start()

    def get(self, j):
        self.across_copy(j).wait_recv()
        return self.chip[span(j)].astype(F32) + self.far[span(j)].astype(F32)

    def drain(self, j):
        self.twin_copy(j).wait_send()
        self.across_copy(j).wait_send()


class SeqSum:
    @staticmethod
    def scratch(n_seq, rows):
        dma = pltpu.SemaphoreType.DMA
        return [
            pltpu.VMEM((rows, 128), BF16),
            pltpu.VMEM((n_seq, rows // n_seq, 128), BF16),
            pltpu.VMEM((rows, 128), BF16),
            dma((2, n_seq)),
            dma((2, n_seq)),
        ]

    def __init__(self, place, refs):
        self.place = place
        self.terms, self.landing, self.total, self.sent, self.came = refs
        self.size = self.landing.shape[1]

    def piece(self, s):
        return pl.ds(pl.multiple_of(s * self.size, self.size), self.size)

    def copy(self, phase, k, src, dst):
        return pltpu.make_async_remote_copy(
            src_ref=src,
            dst_ref=dst,
            send_sem=self.sent.at[phase, k],
            recv_sem=self.came.at[phase, k],
            device_id=self.place.along(k),
            device_id_type=MESH,
        )

    def term_copy(self, k):
        to = self.place.along(k)[0]
        return self.copy(0, k, self.terms.at[self.piece(to)], self.landing.at[k])

    def total_copy(self, k):
        mine = self.total.at[self.piece(self.place.s)]
        return self.copy(1, k, mine, mine)

    def total_arrival(self, k):
        theirs = self.total.at[self.piece((self.place.s + self.place.n_seq - k) % self.place.n_seq)]
        return self.copy(1, k, theirs, theirs)

    def loop(self, action):
        def step(k, carry):
            action(k)
            return carry

        lax.fori_loop(1, self.place.n_seq, step, 0)

    def some(self, j, action):
        lot = -(-(self.place.n_seq - 1) // 4)

        def step(k, carry):
            action(k)
            return carry

        lax.fori_loop(1 + j * lot, jnp.minimum(1 + (j + 1) * lot, self.place.n_seq), step, 0)

    def send_terms(self, j):
        self.some(j, lambda k: self.term_copy(k).start())

    def add(self, j):
        self.loop(lambda k: self.term_copy(k).wait_recv())
        mine = self.piece(self.place.s)

        def step(k, total):
            return total + self.landing[k].astype(F32)

        total = lax.fori_loop(1, self.place.n_seq, step, self.terms[mine].astype(F32))
        self.total[mine] = total.astype(BF16)

    def send_totals(self, j):
        self.some(j, lambda k: self.total_copy(k).start())

    def stages(self, delay):
        return [(delay, 4, self.send_terms), (delay + 6, 1, self.add), (delay + 6, 4, self.send_totals)]

    def wait(self):
        self.loop(lambda k: self.total_arrival(k).wait_recv())

    def drain(self):
        self.loop(lambda k: self.term_copy(k).wait_send())
        self.loop(lambda k: self.total_copy(k).wait_send())


def weight_terms(terms, rows, grad_side, side, grads):
    tall = rows.shape[0] * rows.shape[1]
    width, adapt = rows.shape[2], side.shape[2]

    def flat(ref):
        return ref[...].reshape(tall, ref.shape[2])

    down = mm_tn(flat(grad_side), flat(rows))
    up = 4.0 * mm_tn(flat(side), flat(grads))
    for i, term in enumerate((down, up)):
        for c in range(width // 128):
            at = (i * (width // 128) + c) * adapt
            terms[at : at + adapt] = term[:, c * 128 : (c + 1) * 128].astype(BF16)


def weight_sums(total, down, up):
    width, adapt = down.shape
    for c in range(width // 128):
        down[c * 128 : (c + 1) * 128, :] = total[c * adapt : (c + 1) * adapt].astype(F32).T
        at = (width // 128 + c) * adapt
        up[:, c * 128 : (c + 1) * 128] = total[at : at + adapt].astype(F32)


class Heads:
    def __init__(self, place, sems, own, buf):
        self.place, self.sems, self.own, self.buf = place, sems, own, buf
        self.cols = own.shape[2]
        self.kinds = [sems.take() for _ in range(3)]

    def part(self, j, t):
        return self.buf.at[span(j), pl.ds(pl.multiple_of(t * self.cols, self.cols), self.cols)]

    def copies(self, j):
        p, rows = self.place, span(j)
        landing = self.part(j, p.t)
        return [
            remote(self.sems, self.kinds[0], j, self.own.at[p.core, rows], landing, p.across),
            remote(self.sems, self.kinds[1], j, self.own.at[p.other, rows], landing, p.corner),
            remote(self.sems, self.kinds[2], j, self.own.at[p.other, rows], landing, p.twin),
        ]

    def send(self, j):
        for copy in self.copies(j):
            copy.start()
        self.part(j, self.place.t)[...] = self.own[self.place.core, span(j)]

    def wait(self, j):
        p = self.place
        for kind, source, device in zip(
            self.kinds, (p.across_t, p.corner_t, p.twin_t), (p.across, p.corner, p.twin)
        ):
            part = self.part(j, source)
            remote(self.sems, kind, j, part, part, device).wait_recv()

    def drain(self, j):
        for copy in self.copies(j):
            copy.wait_send()


class Halo:
    def __init__(self, place, sems, rows, halo):
        self.place, self.sems, self.rows, self.halo = place, sems, rows, halo
        self.half = rows // 2
        self.up = [sems.take() if hh * self.half >= rows - halo else None for hh in range(2)]
        self.down = [sems.take() if hh * self.half < halo else None for hh in range(2)]

    def place_up(self, hh, j):
        return span(j + (hh * self.half - (self.rows - self.halo)) // SEGMENT)

    def place_down(self, hh, j):
        return span(j + hh * self.half // SEGMENT)

    def out_copies(self, j, own, before, after):
        copies = []
        for hh in range(2):
            src = own.at[:, self.place_down(hh, j)]
            if self.up[hh] is not None:
                dst = before.at[:, self.place_up(hh, j)]
                copies.append(remote(self.sems, self.up[hh], j, src, dst, self.place.after))
            if self.down[hh] is not None:
                dst = after.at[:, self.place_down(hh, j)]
                copies.append(remote(self.sems, self.down[hh], j, src, dst, self.place.before))
        return copies

    def back_copies(self, j, before, after, from_before, from_after):
        copies = []
        for hh in range(2):
            if self.up[hh] is not None:
                where = self.place_up(hh, j)
                copies.append(
                    remote(self.sems, self.up[hh], j, before.at[:, where], from_after.at[:, where], self.place.before)
                )
            if self.down[hh] is not None:
                where = self.place_down(hh, j)
                copies.append(
                    remote(self.sems, self.down[hh], j, after.at[:, where], from_before.at[:, where], self.place.after)
                )
        return copies

    def gathered(self, j, hh, own, from_before, from_after):
        total = own[:, self.place_down(hh, j)]
        if self.down[hh] is not None:
            total = total + from_before[:, self.place_down(hh, j)].astype(F32)
        if self.up[hh] is not None:
            total = total + from_after[:, self.place_up(hh, j)].astype(F32)
        return total


def pipeline(stages):
    last = max(delay + n for delay, n, _ in stages)

    def step(s, carry):
        for delay, n, stage in stages:
            pl.when((s >= delay) & (s < n + delay))(partial(stage, s - delay))
        return carry

    lax.fori_loop(0, last, step, 0)


def at_first(j, *loads):
    @pl.when(j == 0)
    def _():
        for load in loads:
            load.wait()


def each(n, *actions):
    def step(j, carry):
        for action in actions:
            action(j)
        return carry

    lax.fori_loop(0, n, step, 0)


def exchange_call(kernel, cid, args, loads, outs, scratch, kinds, local_kinds, n, flops):
    anywhere = pl.BlockSpec(memory_space=pl.ANY)
    moved = sum(a.size * a.dtype.itemsize for a in args)
    dma = pltpu.SemaphoreType.DMA
    return pl.pallas_call(
        kernel,
        in_specs=[anywhere] * len(args),
        out_specs=[anywhere] * len(outs),
        out_shape=[jax.ShapeDtypeStruct(shape, kind) for shape, kind in outs],
        scratch_shapes=[pltpu.VMEM(shape, kind) for shape, kind in loads]
        + scratch
        + [dma((2 * len(args),)), dma((max(local_kinds, 1), 2 * n)), dma((kinds, n)), dma((kinds, n))],
        compiler_params=pltpu.CompilerParams(
            collective_id=cid, has_side_effects=True, vmem_limit_bytes=VMEM_BYTES
        ),
        cost_estimate=pl.CostEstimate(flops=flops, bytes_accessed=moved, transcendentals=0),
    )(*args)


def feed_rows(rows, inner, outer, hidden):
    acts, slopes = gelu_parts(mm(rows, inner[...]))
    side = acts[:, hidden:]
    four = (4.0 * side.astype(F32)).astype(BF16)
    return mm(jnp.concatenate([acts[:, :hidden], four], axis=1), outer[...]), slopes, side


def feed_rows_back(grads, slopes, inner, outer, hidden):
    back = slopes.astype(F32) * mm_nt(grads, outer[...])
    grad_side = (4.0 * back[:, hidden:]).astype(BF16)
    back = jnp.concatenate([back[:, :hidden].astype(BF16), grad_side], axis=1)
    return mm_nt(back, inner[...]), grad_side


def rows_of(place, *_):
    return lambda j: [span(j)]


def both_rows(place):
    return lambda j: [(place.core, span(j)), (place.other, span(j))]


def own_first(place, ref, j):
    return jnp.concatenate([ref[place.core, span(j)], ref[place.other, span(j)]], axis=0)


def put_both(place, ref, j, value):
    ref[place.core, span(j)] = value[:SEGMENT]
    ref[place.other, span(j)] = value[SEGMENT:]


def forward_kernel(
    n_seq, halo_rows,
    a_, x_, gains_, wo_, w1_, w2_, wd_, wu_, wkv_, da_, dx_, dgains_, dwo_, dwq_,
    e1_, e3_, hidden_, slope_, side_, kv_, before, after, t1_, t2_, q_,
    a, x, gains, wo, inner, outer, wkv, da, dx, dgains, dwo, dwq,
    e1, e3, hidden, slope, side, kv, t1, t2, q,
    heads_buf, e2, s0, s1, s2, s3, s4, encoded, dheads_buf, dhidden,
    loading, local_sems, send, receive,
):
    place, sems, local = Place(n_seq), Sems(send, receive), Sems(local_sems, local_sems)
    loads = Sems(loading, loading)
    half, dec_half = e1.shape[0], t1.shape[0]
    n, m = half // SEGMENT, dec_half // SEGMENT
    core = place.core
    width, wide_hidden, cols = w1_.shape[0], w1_.shape[1], dwq_.shape[1]
    a = Loaded(loads, a, (a_, None))
    x = Loaded(loads, x, (x_.at[core], None))
    gains = Loaded(loads, gains, (gains_, None))
    wo = Loaded(loads, wo, (wo_, None))
    inner = Loaded(
        loads, inner, (w1_, (slice(None), slice(0, wide_hidden))), (wd_, (slice(None), slice(wide_hidden, None)))
    )
    outer = Loaded(loads, outer, (w2_, slice(0, wide_hidden)), (wu_, slice(wide_hidden, None)))
    da = Loaded(loads, da, (da_, None))
    dx = Loaded(loads, dx, (dx_.at[core], None))
    dgains = Loaded(loads, dgains, (dgains_, None))
    dwo = Loaded(loads, dwo, (dwo_, None))
    dwq = Loaded(loads, dwq, (dwq_, None))
    wkv = Loaded(
        loads, wkv, (wkv_.at[0], (slice(None), slice(0, cols))), (wkv_.at[1], (slice(None), slice(cols, None)))
    )
    rows_j, both_j = rows_of(place), both_rows(place)
    e1 = Stored(local, e1_, e1, rows_j)
    e3 = Stored(local, e3_, e3, rows_j)
    hidden = Stored(local, hidden_, hidden, both_j)
    slope = Stored(local, slope_, slope, lambda j: [j])
    side = Stored(local, side_, side, both_j)
    kv = Stored(local, kv_, kv, lambda j: [(slice(None), span(j)), (slice(None), span(j + n))])
    t1 = Stored(local, t1_, t1, rows_j)
    t2 = Stored(local, t2_, t2, rows_j)
    q = Stored(local, q_, q, both_j)
    heads = Heads(place, sems, a, heads_buf)
    low = Twins(place, sems, hidden)
    total = Total(place, sems, (s0, s1, s2, s3, s4))
    low_encoded = Twins(place, sems, encoded)
    halo = Halo(place, sems, 2 * half, halo_rows)
    dec_heads = Heads(place, sems, da, dheads_buf)
    dec_low = Twins(place, sems, dhidden)
    place.greet([place.twin, place.across, place.corner, place.before, place.after])
    a.wait()
    da.wait()

    def mix(j):
        at_first(j, x, gains, wo)
        heads.wait(j)
        rows = span(j)
        first = x[rows].astype(F32) + mm(heads_buf[rows], wo[...])
        e1[rows] = first
        e1.flush(j)
        middle = normalize(first, gains[0:1])
        e2[rows] = middle
        low.put(j, middle.astype(BF16))

    def feed(j):
        at_first(j, inner, outer)
        low.wait(j)
        hidden.flush(j)
        piece, slopes, side_rows = feed_rows(low.both(j), inner, outer, wide_hidden)
        total.put(j, piece)
        slope[j] = slopes
        put_both(place, side, j, side_rows)
        slope.flush(j)
        side.flush(j)

    def finish(j):
        rows = span(j)
        second = e2[rows] + total.get(j)
        low_encoded.put(j, normalize(second, gains[1:2]).astype(BF16))
        e3[rows] = second
        e3.flush(j)

    def memory(j):
        at_first(j, wkv)
        low_encoded.wait(j)
        made = mm(low_encoded.both(j), wkv[...]).astype(BF16)
        for i in range(2):
            kv[i, span(j + place.core * n)] = made[:SEGMENT, i * cols : (i + 1) * cols]
            kv[i, span(j + place.other * n)] = made[SEGMENT:, i * cols : (i + 1) * cols]
        for copy in halo.out_copies(j, kv, before, after):
            copy.start()
        kv.flush(j)

    def dec_mix(j):
        at_first(j, dx, dgains, dwo)
        dec_heads.wait(j)
        rows = span(j)
        first = dx[rows].astype(F32) + mm(dheads_buf[rows], dwo[...])
        t1[rows] = first
        t1.flush(j)
        middle = normalize(first, dgains[0:1])
        t2[rows] = middle
        t2.flush(j)
        dec_low.put(j, middle.astype(BF16))

    def dec_query(j):
        at_first(j, dwq)
        dec_low.wait(j)
        put_both(place, q, j, mm(dec_low.both(j), dwq[...]).astype(BF16))
        q.flush(j)

    pipeline(
        [
            (0, n, heads.send), (3, n, total.middle), (1, n, mix), (2, n, feed), (3, m, dec_heads.send),
            (5, m, dec_mix), (6, m, dec_query), (4, n, finish), (5, n, memory),
        ]
    )

    def arrived(j):
        for copy in halo.out_copies(j, kv, before, after):
            copy.wait()

    each(
        n, heads.drain, low.drain, total.drain, low_encoded.drain, arrived, e1.drain, e3.drain, hidden.drain,
        slope.drain, side.drain, kv.drain,
    )
    each(m, dec_heads.drain, dec_low.drain, t1.drain, t2.drain, q.drain)


def decoder_chain_kernel(
    n_seq,
    a_, t2_, real_, cotangent_, gains_, wo_, w1_, w2_, wd_, wu_, mixing_,
    decoded, g2_, da_, terms_,
    a, t2, real, cotangent, gains, wo, inner, outer, mixing,
    g2, da, terms, stage,
    heads_buf, t3, t4, g3, hidden, low_g3, low_g2, slope, side, grad_side,
    f0, f1, f2, f3, f4, b0, b1, b2, b3, b4,
    loading, local_sems, send, receive,
):
    place, sems, local = Place(n_seq), Sems(send, receive), Sems(local_sems, local_sems)
    loads = Sems(loading, loading)
    half = t2.shape[0]
    n = half // SEGMENT
    core = place.core
    wide_hidden = w1_.shape[1]
    a = Loaded(loads, a, (a_, None))
    t2 = Loaded(loads, t2, (t2_, None))
    gains = Loaded(loads, gains, (gains_, None))
    wo = Loaded(loads, wo, (wo_, None))
    inner = Loaded(
        loads, inner, (w1_, (slice(None), slice(0, wide_hidden))), (wd_, (slice(None), slice(wide_hidden, None)))
    )
    outer = Loaded(loads, outer, (w2_, slice(0, wide_hidden)), (wu_, slice(wide_hidden, None)))
    real = Loaded(loads, real, (real_.at[core], None))
    cotangent = Loaded(loads, cotangent, (cotangent_.at[core], None))
    mixing = Loaded(loads, mixing, (mixing_, None))
    g2 = Stored(local, g2_, g2, rows_of(place))
    da = Stored(local, da_, da, both_rows(place))
    terms = Stored(local, terms_, terms, lambda j: [slice(None)])
    heads = Heads(place, sems, a, heads_buf)
    low = Twins(place, sems, hidden)
    ahead = Total(place, sems, (f0, f1, f2, f3, f4))
    result = TwinResult(place, sems, local, decoded, stage)
    back3 = Twins(place, sems, low_g3)
    behind = Total(place, sems, (b0, b1, b2, b3, b4))
    back2 = Twins(place, sems, low_g2)
    place.greet([place.twin, place.across, place.corner])
    a.wait()

    def mix(j):
        at_first(j, t2, gains, wo)
        heads.wait(j)
        rows = span(j)
        second = t2[rows] + mm(heads_buf[rows], wo[...])
        t3[rows] = second
        late = normalize(second, gains[1:2])
        t4[rows] = late
        low.put(j, late.astype(BF16))

    def feed(j):
        at_first(j, inner, outer)
        low.wait(j)
        piece, slopes, side_rows = feed_rows(low.both(j), inner, outer, wide_hidden)
        ahead.put(j, piece)
        slope[j] = slopes
        put_both(place, side, j, side_rows)

    def turn(j):
        at_first(j, real, cotangent)
        rows = span(j)
        third = t4[rows] + ahead.get(j)
        mask = real[rows]
        grad = normalize_back(third, gains[2:3], cotangent[rows].astype(F32) * mask)
        back3.put(j, grad.astype(BF16))
        g3[rows] = grad
        result.put(j, normalize(third, gains[2:3]) * mask)

    def feed_back(j):
        back3.wait(j)
        piece, side_rows = feed_rows_back(back3.both(j), slope[j], inner, outer, wide_hidden)
        behind.put(j, piece)
        put_both(place, grad_side, j, side_rows)

    def weights(j):
        weight_terms(terms, hidden, grad_side, side, low_g3)
        terms.flush(0)

    def finish(j):
        rows = span(j)
        grad = normalize_back(t3[rows], gains[1:2], g3[rows] + behind.get(j))
        back2.put(j, grad.astype(BF16))
        g2[rows] = grad
        g2.flush(j)

    def heads_back(j):
        at_first(j, mixing)
        back2.wait(j)
        put_both(place, da, j, mm_nt(back2.both(j), mixing[...]).astype(BF16))
        da.flush(j)

    pipeline(
        [
            (0, n, heads.send), (3, n, ahead.middle), (7, n, behind.middle), (1, n, mix), (2, n, feed),
            (5, n, turn), (6, n, feed_back), (9, n, finish), (10, n, heads_back), (n + 7, 1, weights),
        ]
    )
    each(
        n, heads.drain, low.drain, ahead.drain, result.drain, back3.drain, behind.drain, back2.drain,
        g2.drain, da.drain,
    )
    terms.drain(0)


def key_rows(place, halo, j, scratch, own, from_before, from_after):
    for hh in range(2):
        scratch[hh] = halo.gathered(j, hh, own, from_before, from_after).astype(BF16)
    return jnp.concatenate(
        [
            jnp.concatenate([scratch[place.core, i], scratch[place.other, i]], axis=0) for i in range(2)
        ],
        axis=1,
    )


def backward_kernel(
    n_seq, halo_rows,
    dbefore_, dafter_, dkv_, wkv_, e3_, e1_, gains_, hidden_, slope_, side_, w1_, w2_, wd_, wu_,
    mixing_, dq_, dg2_, t1_, dgains_, dwq_, dmixing_, dterms_,
    g1_, da_, terms_, dg1_, dda_, ddown_, dup_,
    dbefore, dafter, dkv, wkv, e3, e1, gains, hidden, slope, side, inner, outer,
    mixing, dq, dg2, t1, dgains, dwq, dmixing, seq_terms,
    g1, da, terms, dg1, dda, ddown, dup,
    from_before, from_after, rounded, g2, low_g2, low_g1, grad_side,
    f0, f1, f2, f3, f4, b0, b1, b2, b3, b4, dlow_g1, d0, d1, d2, d3, d4,
    seq_landing, seq_total, seq_sent, seq_came,
    loading, local_sems, send, receive,
):
    place, sems, local = Place(n_seq), Sems(send, receive), Sems(local_sems, local_sems)
    loads = Sems(loading, loading)
    half, dec_half = e1.shape[0], t1.shape[0]
    n, m = half // SEGMENT, dec_half // SEGMENT
    wide_hidden, cols = w1_.shape[1], dwq_.shape[1]
    dbefore = Loaded(loads, dbefore, (dbefore_, None))
    dafter = Loaded(loads, dafter, (dafter_, None))
    dterms = Loaded(loads, seq_terms, (dterms_, None))
    seq_sum = SeqSum(place, (seq_terms, seq_landing, seq_total, seq_sent, seq_came))
    dq = Loaded(loads, dq, (dq_, None))
    dwq = Loaded(loads, dwq, (dwq_, None))
    dkv = Loaded(loads, dkv, (dkv_, None))
    wkv = Loaded(
        loads, wkv, (wkv_.at[0], (slice(None), slice(0, cols))), (wkv_.at[1], (slice(None), slice(cols, None)))
    )
    e3 = Loaded(loads, e3, (e3_, None))
    gains = Loaded(loads, gains, (gains_, None))
    dg2 = Loaded(loads, dg2, (dg2_, None))
    t1 = Loaded(loads, t1, (t1_, None))
    dgains = Loaded(loads, dgains, (dgains_, None))
    dmixing = Loaded(loads, dmixing, (dmixing_, None))
    outer = Loaded(loads, outer, (w2_, slice(0, wide_hidden)), (wu_, slice(wide_hidden, None)))
    slope = Loaded(loads, slope, (slope_, None))
    inner = Loaded(
        loads, inner, (w1_, (slice(None), slice(0, wide_hidden))), (wd_, (slice(None), slice(wide_hidden, None)))
    )
    e1 = Loaded(loads, e1, (e1_, None))
    mixing = Loaded(loads, mixing, (mixing_, None))
    hidden = Loaded(loads, hidden, (hidden_, None))
    side = Loaded(loads, side, (side_, None))
    rows_j, both_j = rows_of(place), both_rows(place)
    g1 = Stored(local, g1_, g1, rows_j)
    da = Stored(local, da_, da, both_j)
    terms = Stored(local, terms_, terms, lambda j: [slice(None)])
    dg1 = Stored(local, dg1_, dg1, rows_j)
    dda = Stored(local, dda_, dda, both_j)
    ddown = Stored(local, ddown_, ddown, lambda j: [slice(None)])
    dup = Stored(local, dup_, dup, lambda j: [slice(None)])
    halo = Halo(place, sems, 2 * half, halo_rows)
    first = Total(place, sems, (f0, f1, f2, f3, f4))
    back2 = Twins(place, sems, low_g2)
    second = Total(place, sems, (b0, b1, b2, b3, b4))
    back1 = Twins(place, sems, low_g1)
    dec_total = Total(place, sems, (d0, d1, d2, d3, d4))
    dec_back = Twins(place, sems, dlow_g1)
    place.greet([place.twin, place.across], True)
    dbefore.wait()
    dafter.wait()

    def leave(j):
        for copy in halo.back_copies(j, dbefore, dafter, from_before, from_after):
            copy.start()

    dterms.wait()

    def start(j):
        at_first(j, dkv, wkv)
        for copy in halo.back_copies(j, dbefore, dafter, from_before, from_after):
            copy.wait_recv()
        first.put(j, mm_nt(key_rows(place, halo, j, rounded, dkv, from_before, from_after), wkv[...]))

    def turn(j):
        at_first(j, e3, gains)
        rows = span(j)
        grad = normalize_back(e3[rows], gains[1:2], first.get(j))
        g2[rows] = grad
        back2.put(j, grad.astype(BF16))

    def feed_back(j):
        at_first(j, slope, inner, outer)
        back2.wait(j)
        piece, side_rows = feed_rows_back(back2.both(j), slope[j], inner, outer, wide_hidden)
        second.put(j, piece)
        put_both(place, grad_side, j, side_rows)

    def weights(j):
        hidden.wait()
        side.wait()
        weight_terms(terms, hidden, grad_side, side, low_g2)
        terms.flush(0)

    def finish(j):
        at_first(j, e1)
        rows = span(j)
        grad = normalize_back(e1[rows], gains[0:1], g2[rows] + second.get(j))
        back1.put(j, grad.astype(BF16))
        g1[rows] = grad
        g1.flush(j)

    def heads_back(j):
        at_first(j, mixing)
        back1.wait(j)
        put_both(place, da, j, mm_nt(back1.both(j), mixing[...]).astype(BF16))
        da.flush(j)

    def dec_start(j):
        at_first(j, dq, dwq)
        dec_total.put(j, mm_nt(own_first(place, dq, j), dwq[...]))

    def dec_finish(j):
        at_first(j, dg2, t1, dgains)
        rows = span(j)
        grad = normalize_back(t1[rows], dgains[0:1], dg2[rows] + dec_total.get(j))
        dec_back.put(j, grad.astype(BF16))
        dg1[rows] = grad
        dg1.flush(j)

    def dec_heads_back(j):
        at_first(j, dmixing)
        dec_back.wait(j)
        put_both(place, dda, j, mm_nt(dec_back.both(j), dmixing[...]).astype(BF16))
        dda.flush(j)

    pipeline(
        [
            (0, n, leave), (1, m, dec_total.middle), (3, n, first.middle), (7, n, second.middle), (0, m, dec_start),
            (2, n, start), (5, n, turn), (6, n, feed_back), (3, m, dec_finish), (4, m, dec_heads_back),
            (9, n, finish), (10, n, heads_back), (n + 7, 1, weights), *seq_sum.stages(4),
        ]
    )
    seq_sum.wait()
    weight_sums(seq_total, ddown, dup)
    ddown.flush(0)
    dup.flush(0)
    seq_sum.drain()

    def left(j):
        for copy in halo.back_copies(j, dbefore, dafter, from_before, from_after):
            copy.wait_send()

    each(n, left, first.drain, back2.drain, second.drain, back1.drain, g1.drain, da.drain)
    each(m, dec_total.drain, dec_back.drain, dg1.drain, dda.drain)
    terms.drain(0)
    ddown.drain(0)
    dup.drain(0)


def input_back_kernel(n_seq, halos, *refs):
    refs = list(refs)

    def take(count):
        taken = refs[:count]
        del refs[:count]
        return taken

    operands = [take(6), take(6)]
    term_operands = take(4)
    results = take(2)
    sum_results = take(5)
    buffers = [take(6), take(6)]
    stages = take(2)
    sums = take(5)
    scratch = [take(8), take(8)]
    seq_refs = take(5)
    loading, local_sems, send, receive = refs
    place, sems, local = Place(n_seq), Sems(send, receive), Sems(local_sems, local_sems)
    counter = Sems(loading, loading)
    loads = []
    for k in range(2):
        weights = operands[k][4]
        parts = [[(operand, None)] for operand in operands[k]]
        parts[4] = [
            (weights.at[i], (slice(None), slice(i * weights.shape[2], (i + 1) * weights.shape[2])))
            for i in range(3)
        ]
        loads.append([Loaded(counter, buf, *part) for part, buf in zip(parts, buffers[k])])
    seq_terms = seq_refs[0]
    seq_sum = SeqSum(place, seq_refs)
    at, term_loads = 0, []
    for term in term_operands:
        term_loads.append(Loaded(counter, seq_terms, (term, slice(at, at + term.shape[0]))))
        at += term.shape[0]
    sums = [Stored(local, result, buf, lambda j: [slice(None)]) for result, buf in zip(sum_results, sums)]
    seq_terms[at:] = jnp.zeros((seq_terms.shape[0] - at, 128), BF16)
    place.greet([place.twin, place.across], True)
    pieces, drains = [], []
    for k in range(2):
        dbefore, dafter, dq, dkv, weights, g1 = loads[k]
        from_before, from_after, rounded = scratch[k][:3]
        half = stages[k].shape[0]
        n = half // SEGMENT
        halo = Halo(place, sems, 2 * half, halos[k])
        total = Total(place, sems, scratch[k][3:])
        result = TwinResult(place, sems, local, results[k], stages[k])
        dbefore.wait()
        dafter.wait()

        def copies(j, halo=halo, refs=(dbefore, dafter, from_before, from_after)):
            return halo.back_copies(j, *refs)

        def leave(j, copies=copies):
            for copy in copies(j):
                copy.start()

        def start(j, k=k, halo=halo, total=total, copies=copies):
            dbefore, dafter, dq, dkv, weights, g1 = loads[k]
            from_before, from_after, rounded = scratch[k][:3]
            at_first(j, dq, dkv, weights)
            for copy in copies(j):
                copy.wait_recv()
            key_grads = key_rows(place, halo, j, rounded, dkv, from_before, from_after)
            grads = jnp.concatenate([own_first(place, dq, j), key_grads], axis=1)
            total.put(j, mm_nt(grads, weights[...]))

        def finish(j, g1=g1, total=total, result=result):
            at_first(j, g1)
            result.put(j, g1[span(j)] + total.get(j))

        def left(j, copies=copies):
            for copy in copies(j):
                copy.wait_send()

        pieces.append((n, leave, start, total, finish))
        drains.append((n, left, total.drain, result.drain))
    for load in term_loads:
        load.wait()
    stages_ = seq_sum.stages(1)
    for offset, (n, leave, start, total, finish) in zip((0, 2), pieces):
        stages_ += [
            (offset, n, leave), (offset + 3, n, total.middle), (offset + 2, n, start), (offset + 5, n, finish),
        ]
    pipeline(stages_)
    seq_sum.wait()
    seq_total = seq_refs[2]
    weight_sums(seq_total, sums[0], sums[1])
    at = 2 * sums[0].shape[0]
    for k in range(2, 5):
        for i in range(2):
            for c in range(2):
                part = seq_total[at : at + PREFIX_ROWS].astype(F32)
                sums[k][i, :, c * 128 : (c + 1) * 128] = part[0:PREFIX]
                at += PREFIX_ROWS
    for result in sums:
        result.flush(0)
    for n, *actions in drains:
        each(n, *actions)
    seq_sum.drain()
    for result in sums:
        result.drain(0)


def document_plan(query_docs, key_docs, query_rows, key_rows_, halo, block, causal):
    s = lax.axis_index("seq")
    own = lax.dynamic_slice_in_dim(query_docs, s * query_rows, query_rows)
    filler = jnp.full((halo,), -1, jnp.int32)
    padded = jnp.concatenate([filler, key_docs, filler])
    window = key_rows_ + 2 * halo
    keys = lax.dynamic_slice_in_dim(padded, s * key_rows_, window)
    blocks = own.reshape(-1, block)
    top = jnp.max(blocks, axis=1)
    bottom = jnp.min(jnp.where(blocks >= 0, blocks, 2**30), axis=1)
    read = (keys[None] >= bottom[:, None]) & (keys[None] <= top[:, None])
    index = jnp.arange(window, dtype=jnp.int32)[None]
    lo = jnp.min(jnp.where(read, index, window), axis=1) // KEY_BLOCK
    hi = (jnp.max(jnp.where(read, index + 1, 0), axis=1) + KEY_BLOCK - 1) // KEY_BLOCK
    if causal:
        ends = halo + block * (1 + jnp.arange(blocks.shape[0], dtype=jnp.int32))
        hi = jnp.minimum(hi, (ends + KEY_BLOCK - 1) // KEY_BLOCK)
    rows = jnp.where(blocks >= 0, blocks, -2)[:, None, :]
    return rows, keys[:, None], lo, hi


def halo_parts(kv, halo):
    size = lax.axis_size("seq")
    rows = kv.shape[1]
    up = [(i, i + 1) for i in range(size - 1)]
    down = [(i + 1, i) for i in range(size - 1)]
    before = lax.ppermute(kv[:, rows - halo :], "seq", up)
    after = lax.ppermute(kv[:, :halo], "seq", down)
    return before, kv, after


def halves(array):
    return array.reshape((2, array.shape[0] // 2) + array.shape[1:])


def exchange_scratch(half, *kinds):
    shapes = []
    for kind in kinds:
        if kind == "total":
            shapes += Total.SHAPES(half)
        else:
            shape, dtype = kind
            shapes.append(pltpu.VMEM(shape, dtype))
    return shapes


def reaches_far(n_seq, source_document, target_document):
    source_docs = source_document.reshape(n_seq, -1)
    target_docs = target_document.reshape(n_seq, -1)

    def smallest(docs):
        return jnp.min(jnp.where(docs >= 0, docs, 2**30), axis=1)

    lows = jnp.minimum(smallest(source_docs), smallest(target_docs))
    highs = jnp.maximum(jnp.max(source_docs, axis=1), jnp.max(target_docs, axis=1))
    after_low = jnp.concatenate([lows[1:], jnp.full((1,), 2**30, jnp.int32)])[:, None]
    before_high = jnp.concatenate([jnp.full((1,), -1, jnp.int32), highs[:-1]])[:, None]
    far = False
    for docs in (source_docs, target_docs):
        half = docs.shape[1] // 2
        far = far | jnp.any(docs[:, :half] >= after_low)
        far = far | jnp.any((docs[:, half:] >= 0) & (docs[:, half:] <= before_high))
    return far


def on_device(n_seq, *args):
    far = reaches_far(n_seq, args[2], args[3])
    return lax.cond(far, partial(on_device_with, n_seq, True), partial(on_device_with, n_seq, False), *args)


def on_device_with(
    n_seq,
    wide,
    source,
    target,
    source_document,
    target_document,
    cotangent,
    encoder_attention,
    encoder_mixing,
    encoder_gains,
    encoder_inner,
    encoder_outer,
    encoder_prefix,
    encoder_down,
    encoder_up,
    decoder_attention,
    decoder_mixing,
    decoder_prefix,
    cross_query,
    cross_memory,
    cross_mixing,
    cross_prefix,
    decoder_gains,
    decoder_inner,
    decoder_outer,
    decoder_down,
    decoder_up,
):
    ids = iter(range(1 + 16 * int(wide), 100))
    source_rows, width = source.shape
    target_rows = target.shape[0]
    cols = encoder_mixing.shape[0]
    hidden = encoder_inner.shape[1]
    adapt = encoder_down.shape[1]
    source_halo = source_rows if wide else source_rows // 2
    target_halo = target_rows if wide else target_rows // 2
    source_half, target_half = source_rows // 2, target_rows // 2
    source_n, target_n = source_half // SEGMENT, target_half // SEGMENT
    chunk = 2 * SEGMENT

    encoder_wo = lax.all_gather(encoder_mixing, "tp", tiled=True)
    decoder_wo = lax.all_gather(decoder_mixing, "tp", tiled=True)
    cross_wo = lax.all_gather(cross_mixing, "tp", tiled=True)

    def padded(prefix):
        return jnp.pad(prefix, ((0, 0), (0, PREFIX_ROWS - prefix.shape[1]), (0, 0)))

    encoder_prefix, decoder_prefix, cross_prefix = map(padded, (encoder_prefix, decoder_prefix, cross_prefix))

    encoder_q, encoder_kv = project(source, encoder_attention)
    encoder_parts = halo_parts(encoder_kv, source_halo)
    decoder_q, decoder_kv = project(target, decoder_attention)
    decoder_parts = halo_parts(decoder_kv, target_halo)

    encoder_docs = document_plan(
        source_document, source_document, source_rows, source_rows, source_halo, QUERY_BLOCK, False
    )
    decoder_docs = document_plan(
        target_document, target_document, target_rows, target_rows, target_halo, QUERY_BLOCK, True
    )
    cross_docs = document_plan(
        target_document, source_document, target_rows, source_rows, source_halo, QUERY_BLOCK, False
    )
    own_target = lax.dynamic_slice_in_dim(target_document, lax.axis_index("seq") * target_rows, target_rows)
    real = halves((own_target >= 0).astype(F32)[:, None])

    encoder_wide, encoder_low, encoder_total = attend(
        encoder_q, encoder_parts, encoder_prefix, encoder_docs, False
    )
    decoder_wide, decoder_low, decoder_total = attend(
        decoder_q, decoder_parts, decoder_prefix, decoder_docs, True
    )
    gathered_source = ((source_half, width), F32)
    gathered_target = ((target_half, width), F32)
    source_low = ((2, source_half, width), BF16)
    target_low = ((2, target_half, width), BF16)
    source_cols = ((2, source_half, cols), BF16)
    target_cols = ((2, target_half, cols), BF16)
    slopes = [((source_n, chunk, hidden + adapt), BF16), ((2, source_half, adapt), BF16)]
    inner_buf, outer_buf = ((width, hidden + adapt), BF16), ((hidden + adapt, width), BF16)

    def whole(*arrays):
        return [(array.shape, array.dtype) for array in arrays]

    halo_cols = ((2, source_halo, cols), BF16)
    kv_cols = ((2, source_rows, cols), BF16)
    stored = [gathered_source, gathered_source, source_low, *slopes, kv_cols]
    stored_target = [gathered_target, gathered_target, target_cols]
    args = (
        halves(encoder_low), halves(source), encoder_gains, encoder_wo, encoder_inner, encoder_outer,
        encoder_down, encoder_up, cross_memory, halves(decoder_low), halves(target), decoder_gains,
        decoder_wo, cross_query,
    )
    loads = [
        *whole(args[0]), ((source_half, width), BF16), *whole(args[2], args[3]), inner_buf, outer_buf,
        ((width, 2 * cols), BF16), *whole(args[9]), ((target_half, width), BF16), *whole(*args[11:]),
    ]
    (
        e1, e3, encoder_hidden, encoder_slope, encoder_side, cross_kv, cross_before, cross_after, t1, t2, cross_q,
    ) = exchange_call(
        partial(forward_kernel, n_seq, source_halo),
        next(ids),
        args,
        loads,
        [*stored, halo_cols, halo_cols, *stored_target],
        exchange_scratch(
            source_half,
            *stored,
            *stored_target,
            ((source_half, width), BF16),
            gathered_source,
            "total",
            source_low,
            ((target_half, width), BF16),
            target_low,
        ),
        3 + 1 + 2 + 1 + (4 if wide else 2) + 3 + 1,
        9,
        source_n,
        2 * source_rows * width * (2 * hidden + 2 * adapt + 6 * cols),
    )
    cross_parts = (cross_before, cross_kv, cross_after)
    cross_q = cross_q.reshape(target_rows, cols)
    cross_wide, cross_low, cross_total = attend(cross_q, cross_parts, cross_prefix, cross_docs, False)

    terms = ((2 * width, adapt), BF16)
    sums = [((width, adapt), F32), ((adapt, width), F32)]
    args = (
        halves(cross_low), t2, real, halves(cotangent), decoder_gains, cross_wo, decoder_inner,
        decoder_outer, decoder_down, decoder_up, cross_mixing,
    )
    loads = [
        *whole(args[0], args[1]), ((target_half, 1), F32), ((target_half, width), BF16), *whole(args[4], args[5]),
        inner_buf, outer_buf, *whole(args[10]),
    ]
    stored = [gathered_target, target_cols, terms]
    decoded, g2, cross_da, decoder_terms = exchange_call(
        partial(decoder_chain_kernel, n_seq),
        next(ids),
        args,
        loads,
        [((2, target_half, width), F32), *stored],
        exchange_scratch(
            target_half,
            *stored,
            gathered_target,
            ((target_half, width), BF16),
            gathered_target,
            gathered_target,
            gathered_target,
            target_low,
            target_low,
            target_low,
            ((target_n, chunk, hidden + adapt), BF16),
            ((2, target_half, adapt), BF16),
            ((2, target_half, adapt), BF16),
            "total",
            "total",
        ),
        3 + 1 + 2 + 1 + 1 + 2 + 1,
        4,
        target_n,
        2 * target_rows * width * (4 * hidden + 6 * adapt + 2 * cols),
    )
    cross_dq, cross_dbefore, cross_dkv, cross_dafter, cross_prefix_terms = attend_back(
        cross_q, cross_da.reshape(target_rows, cols), cross_wide, cross_total, cross_parts, cross_prefix,
        cross_docs, False,
    )
    args = (
        cross_dbefore, cross_dafter, cross_dkv, cross_memory, e3, e1, encoder_gains, encoder_hidden,
        encoder_slope, encoder_side, encoder_inner, encoder_outer, encoder_down, encoder_up,
        encoder_mixing, halves(cross_dq), g2, t1, decoder_gains, cross_query, decoder_mixing,
        decoder_terms,
    )
    loads = [
        *whole(*args[:3]), ((width, 2 * cols), BF16), *whole(*args[4:10]), inner_buf, outer_buf, *whole(*args[14:]),
    ]
    stored = [gathered_source, source_cols, terms, gathered_target, target_cols, *sums]
    (
        encoder_g1, encoder_da, encoder_terms, decoder_g1, decoder_da, decoder_down_gradient, decoder_up_gradient,
    ) = exchange_call(
        partial(backward_kernel, n_seq, source_halo),
        next(ids),
        args,
        loads,
        stored,
        exchange_scratch(
            source_half,
            *stored,
            halo_cols,
            halo_cols,
            ((2, 2, SEGMENT, cols), BF16),
            gathered_source,
            source_low,
            source_low,
            ((2, source_half, adapt), BF16),
            "total",
            "total",
            target_low,
        )
        + exchange_scratch(target_half, "total")
        + SeqSum.scratch(n_seq, 2 * width)[1:],
        (4 if wide else 2) + 2 + 1 + 2 + 1 + 2 + 1,
        7,
        source_n,
        2 * source_rows * width * (2 * hidden + 4 * adapt + 4 * cols),
    )
    ddq, ddbefore, ddkv, ddafter, decoder_prefix_terms = attend_back(
        decoder_q, decoder_da.reshape(target_rows, cols), decoder_wide, decoder_total, decoder_parts,
        decoder_prefix, decoder_docs, True,
    )
    edq, edbefore, edkv, edafter, encoder_prefix_terms = attend_back(
        encoder_q, encoder_da.reshape(source_rows, cols), encoder_wide, encoder_total, encoder_parts,
        encoder_prefix, encoder_docs, False,
    )
    args = (
        edbefore, edafter, halves(edq), edkv, encoder_attention, encoder_g1,
        ddbefore, ddafter, halves(ddq), ddkv, decoder_attention, decoder_g1,
        encoder_terms, encoder_prefix_terms, decoder_prefix_terms, cross_prefix_terms,
    )
    loads = whole(*args[:12])
    loads[4] = loads[10] = ((width, 3 * cols), BF16)
    prefix_sum = ((2, PREFIX, cols), F32)
    results = [*sums, prefix_sum, prefix_sum, prefix_sum]
    seq_rows = 2 * width + 512
    (
        source_gradient, target_gradient, encoder_down_gradient, encoder_up_gradient, encoder_prefix_gradient,
        decoder_prefix_gradient, cross_prefix_gradient,
    ) = exchange_call(
        partial(input_back_kernel, n_seq, (source_halo, target_halo)),
        next(ids),
        args,
        loads,
        [((2, source_half, width), F32), ((2, target_half, width), F32), *results],
        exchange_scratch(source_half, gathered_source, gathered_target, *results)
        + exchange_scratch(source_half, halo_cols, halo_cols, ((2, 2, SEGMENT, cols), BF16), "total")
        + exchange_scratch(
            target_half,
            ((2, target_halo, cols), BF16),
            ((2, target_halo, cols), BF16),
            ((2, 2, SEGMENT, cols), BF16),
            "total",
        )
        + SeqSum.scratch(n_seq, seq_rows),
        2 * ((4 if wide else 2) + 2 + 1),
        7,
        source_n,
        6 * (source_rows + target_rows) * width * cols,
    )
    source_gradient = source_gradient.reshape(source_rows, width)
    target_gradient = target_gradient.reshape(target_rows, width)

    weight_totals = (
        encoder_prefix_gradient,
        encoder_down_gradient,
        encoder_up_gradient,
        decoder_prefix_gradient,
        cross_prefix_gradient,
        decoder_down_gradient,
        decoder_up_gradient,
    )
    return (decoded.reshape(target_rows, width), source_gradient, target_gradient) + tuple(weight_totals)


def solution(mesh):
    return jax.shard_map(
        partial(on_device, mesh.shape["seq"]),
        mesh=mesh,
        in_specs=(
            P("seq", None),
            P("seq", None),
            P(),
            P(),
            P("seq", None),
            P(None, None, "tp"),
            P("tp", None),
            P(),
            P(None, "tp"),
            P("tp", None),
            P(None, None, "tp"),
            P(None, "tp"),
            P("tp", None),
            P(None, None, "tp"),
            P("tp", None),
            P(None, None, "tp"),
            P(None, "tp"),
            P(None, None, "tp"),
            P("tp", None),
            P(None, None, "tp"),
            P(),
            P(None, "tp"),
            P("tp", None),
            P(None, "tp"),
            P("tp", None),
        ),
        out_specs=(
            P("seq", None),
            P("seq", None),
            P("seq", None),
            P(None, None, "tp"),
            P(None, "tp"),
            P("tp", None),
            P(None, None, "tp"),
            P(None, None, "tp"),
            P(None, "tp"),
            P("tp", None),
        ),
        check_vma=False,
    )
```

```python
from functools import partial

import jax
import jax.numpy as jnp
from jax import lax
from jax.experimental import pallas as pl
from jax.experimental.pallas import tpu as pltpu
from jax.sharding import PartitionSpec as P

HEAD_DIM = 64
EPSILON = 1e-05
NEGATIVE = -1e30
HEADS = 4
KEY_BLOCK = 256
QUERY_BLOCK = 256
PREFIX = 30
PREFIX_ROWS = 32
SEGMENT = 64
MESH = pl.DeviceIdType.MESH
F32 = jnp.float32
BF16 = jnp.bfloat16
VMEM_BYTES = 63 * 2**20


def mm(left, right):
    return jnp.dot(left, right, preferred_element_type=F32)


def mm_nt(left, right):
    return lax.dot_general(left, right, (((1,), (1,)), ((), ())), preferred_element_type=F32)


def mm_tn(left, right):
    return lax.dot_general(left, right, (((0,), (0,)), ((), ())), preferred_element_type=F32)


def normalize(inputs, scaling):
    centered = inputs - jnp.mean(inputs, axis=-1, keepdims=True)
    spread = lax.rsqrt(jnp.mean(centered * centered, axis=-1, keepdims=True) + EPSILON)
    return scaling * (centered * spread)


def normalize_back(inputs, scaling, gradient):
    centered = inputs - jnp.mean(inputs, axis=-1, keepdims=True)
    spread = lax.rsqrt(jnp.mean(centered * centered, axis=-1, keepdims=True) + EPSILON)
    unit = centered * spread
    scaled = gradient * scaling
    first = jnp.mean(scaled, axis=-1, keepdims=True)
    second = jnp.mean(scaled * unit, axis=-1, keepdims=True)
    return spread * (scaled - first - unit * second)


def gelu_parts(inputs):
    chance = 0.5 * (1.0 + lax.erf(inputs * (0.5**0.5)))
    density = jnp.exp(-0.5 * inputs * inputs) * 0.3989422804014327
    return (inputs * chance).astype(BF16), (chance + inputs * density).astype(BF16)


def project_kernel(x_ref, w_ref, q_ref, kv_ref):
    rows = x_ref[...]
    q_ref[...] = mm(rows, w_ref[0]).astype(BF16)
    kv_ref[0] = mm(rows, w_ref[1]).astype(BF16)
    kv_ref[1] = mm(rows, w_ref[2]).astype(BF16)


def project(inputs, weights):
    rows, width = inputs.shape
    block = 256
    cols = weights.shape[2]
    return pl.pallas_call(
        project_kernel,
        grid=(rows // block,),
        in_specs=[
            pl.BlockSpec((block, width), lambda i: (i, 0)),
            pl.BlockSpec(weights.shape, lambda i: (0, 0, 0)),
        ],
        out_specs=[
            pl.BlockSpec((block, cols), lambda i: (i, 0)),
            pl.BlockSpec((2, block, cols), lambda i: (0, i, 0)),
        ],
        out_shape=[
            jax.ShapeDtypeStruct((rows, cols), BF16),
            jax.ShapeDtypeStruct((2, rows, cols), BF16),
        ],
        compiler_params=pltpu.CompilerParams(vmem_limit_bytes=VMEM_BYTES),
        cost_estimate=pl.CostEstimate(
            flops=6 * rows * width * cols, bytes_accessed=8 * rows * cols + 6 * width * cols, transcendentals=0
        ),
    )(inputs, weights)


def by_heads(rows, lane_head):
    zero = jnp.zeros_like(rows)
    return jnp.concatenate([jnp.where(lane_head == h, rows, zero) for h in range(HEADS)], axis=0)


def head_bias(kd_ref, qd_ref, start, first_query, halo, block, causal):
    key_doc = kd_ref[pl.ds(start, KEY_BLOCK), :]
    allowed = key_doc == qd_ref[0]
    if causal:
        key_place = start - halo + lax.broadcasted_iota(jnp.int32, (KEY_BLOCK, block), 0)
        query_place = first_query + lax.broadcasted_iota(jnp.int32, (KEY_BLOCK, block), 1)
        allowed = allowed & (key_place <= query_place)
    bias = jnp.where(allowed, 0.0, NEGATIVE)
    return jnp.concatenate([bias] * HEADS, axis=1)


def prefix_scores(pre_ref, stacked):
    scores = mm_nt(pre_ref[0], stacked)
    row = lax.broadcasted_iota(jnp.int32, scores.shape, 0)
    return jnp.where(row < PREFIX, scores, NEGATIVE)


def fill_window(window, parts, index):
    at = 0
    for part in parts:
        size = part.shape[1]
        window[at : at + size, :] = part[index]
        at += size


def attend_kernel(
    halo, causal, lo_ref, hi_ref, q_ref, bef_ref, own_ref, aft_ref, pre_ref, qd_ref, kd_ref,
    wide_ref, low_ref, total_ref, keys, values, blended,
):
    i = pl.program_id(0)
    block = q_ref.shape[0]
    parts = (bef_ref, own_ref, aft_ref)

    @pl.when(i == 0)
    def _():
        fill_window(keys, parts, 0)
        at = 0
        for part in parts:
            for k in range(part.shape[1] // KEY_BLOCK):
                values[at] = part[1, k * KEY_BLOCK : (k + 1) * KEY_BLOCK, :].T
                at += 1

    lane_head = lax.broadcasted_iota(jnp.int32, q_ref.shape, 1) // HEAD_DIM
    stacked = by_heads(q_ref[...] * jnp.asarray(HEAD_DIM**-0.5, BF16), lane_head)
    scores = prefix_scores(pre_ref, stacked)
    highest = jnp.max(scores, axis=0, keepdims=True)
    chances = jnp.exp(scores - highest)
    summed = jnp.sum(chances, axis=0, keepdims=True)
    low = chances.astype(BF16)
    pre_values = pre_ref[1].T
    for h in range(HEADS):
        rows = slice(h * HEAD_DIM, (h + 1) * HEAD_DIM)
        blended[rows, :] = mm(pre_values[rows, :], low[:, h * block : (h + 1) * block])

    def step(kb, carry):
        highest, summed = carry
        start = pl.multiple_of(kb * KEY_BLOCK, KEY_BLOCK)
        scores = mm_nt(keys[pl.ds(start, KEY_BLOCK), :], stacked)
        scores = scores + head_bias(kd_ref, qd_ref, start, i * block, halo, block, causal)
        top = jnp.maximum(highest, jnp.max(scores, axis=0, keepdims=True))
        fade = jnp.exp(highest - top)
        chances = jnp.exp(scores - top)
        summed = summed * fade + jnp.sum(chances, axis=0, keepdims=True)
        low = chances.astype(BF16)
        for h in range(HEADS):
            rows = slice(h * HEAD_DIM, (h + 1) * HEAD_DIM)
            cols = slice(h * block, (h + 1) * block)
            blended[rows, :] = blended[rows, :] * fade[:, cols] + mm(values[kb, rows, :], low[:, cols])
        return top, summed

    highest, summed = lax.fori_loop(lo_ref[i], hi_ref[i], step, (highest, summed))
    total_ref[0] = highest + jnp.log(summed)
    inverse = 1.0 / summed
    for h in range(HEADS):
        rows = slice(h * HEAD_DIM, (h + 1) * HEAD_DIM)
        blended[rows, :] = blended[rows, :] * inverse[:, h * block : (h + 1) * block]
    result = blended[...].T
    wide_ref[...] = result
    low_ref[...] = result.astype(BF16)


def attend(queries, parts, prefix, docs, causal):
    query_doc, key_doc, lo, hi = docs
    rows, cols = queries.shape
    count, _, block = query_doc.shape
    window = key_doc.shape[0]
    halo = parts[0].shape[1]

    def whole(array):
        return pl.BlockSpec(array.shape, lambda i, *_: (0,) * array.ndim)

    return pl.pallas_call(
        partial(attend_kernel, halo, causal),
        grid_spec=pltpu.PrefetchScalarGridSpec(
            num_scalar_prefetch=2,
            grid=(count,),
            in_specs=[
                pl.BlockSpec((block, cols), lambda i, *_: (i, 0)),
                whole(parts[0]),
                whole(parts[1]),
                whole(parts[2]),
                whole(prefix),
                pl.BlockSpec((1, 1, block), lambda i, *_: (i, 0, 0)),
                whole(key_doc),
            ],
            out_specs=[
                pl.BlockSpec((block, cols), lambda i, *_: (i, 0)),
                pl.BlockSpec((block, cols), lambda i, *_: (i, 0)),
                pl.BlockSpec((1, 1, HEADS * block), lambda i, *_: (i, 0, 0)),
            ],
            scratch_shapes=[
                pltpu.VMEM((window, cols), BF16),
                pltpu.VMEM((window // KEY_BLOCK, cols, KEY_BLOCK), BF16),
                pltpu.VMEM((cols, block), F32),
            ],
        ),
        out_shape=[
            jax.ShapeDtypeStruct((rows, cols), F32),
            jax.ShapeDtypeStruct((rows, cols), BF16),
            jax.ShapeDtypeStruct((count, 1, HEADS * block), F32),
        ],
        compiler_params=pltpu.CompilerParams(vmem_limit_bytes=VMEM_BYTES),
        cost_estimate=pl.CostEstimate(
            flops=16 * rows * 1024 * cols, bytes_accessed=8 * window * cols, transcendentals=4 * rows * 1024
        ),
    )(lo, hi, queries, *parts, prefix, query_doc, key_doc)


def attend_back_kernel(
    halo, causal, lo_ref, hi_ref, q_ref, g_ref, wide_ref, total_ref, bef_ref, own_ref, aft_ref, pre_ref,
    qd_ref, kd_ref, dq_ref, dbef_ref, down_ref, daft_ref, dpre_ref,
    keys, values, turned, key_sum, value_sum, query_sum, prefix_sum,
):
    i = pl.program_id(0)
    block = q_ref.shape[0]
    parts = (bef_ref, own_ref, aft_ref)

    @pl.when(i == 0)
    def _():
        fill_window(keys, parts, 0)
        fill_window(values, parts, 1)
        at = 0
        for part in parts:
            for k in range(part.shape[1] // KEY_BLOCK):
                turned[at] = part[0, k * KEY_BLOCK : (k + 1) * KEY_BLOCK, :].T
                at += 1
        key_sum[...] = jnp.zeros_like(key_sum)
        value_sum[...] = jnp.zeros_like(value_sum)
        prefix_sum[...] = jnp.zeros_like(prefix_sum)

    lane_head = lax.broadcasted_iota(jnp.int32, q_ref.shape, 1) // HEAD_DIM
    stacked = by_heads(q_ref[...] * jnp.asarray(HEAD_DIM**-0.5, BF16), lane_head)
    grads = by_heads(g_ref[...], lane_head)
    mixed = (g_ref[...].astype(F32) * wide_ref[...]).T
    offsets = jnp.concatenate(
        [
            jnp.sum(mixed[h * HEAD_DIM : (h + 1) * HEAD_DIM, :], axis=0, keepdims=True)
            for h in range(HEADS)
        ],
        axis=1,
    )
    total = total_ref[0]
    chances = jnp.exp(prefix_scores(pre_ref, stacked) - total)
    score_grad = (chances * (mm_nt(pre_ref[1], grads) - offsets)).astype(BF16)
    prefix_sum[0] += mm(score_grad, stacked)
    prefix_sum[1] += mm(chances.astype(BF16), grads)
    pre_keys = pre_ref[0].T
    for h in range(HEADS):
        rows = slice(h * HEAD_DIM, (h + 1) * HEAD_DIM)
        query_sum[rows, :] = mm(pre_keys[rows, :], score_grad[:, h * block : (h + 1) * block])

    def step(kb, carry):
        start = pl.multiple_of(kb * KEY_BLOCK, KEY_BLOCK)
        here = pl.ds(start, KEY_BLOCK)
        scores = mm_nt(keys[here, :], stacked)
        scores = scores + head_bias(kd_ref, qd_ref, start, i * block, halo, block, causal)
        chances = jnp.exp(scores - total)
        score_grad = (chances * (mm_nt(values[here, :], grads) - offsets)).astype(BF16)
        key_sum[here, :] += mm(score_grad, stacked)
        value_sum[here, :] += mm(chances.astype(BF16), grads)
        for h in range(HEADS):
            rows = slice(h * HEAD_DIM, (h + 1) * HEAD_DIM)
            query_sum[rows, :] += mm(turned[kb, rows, :], score_grad[:, h * block : (h + 1) * block])
        return carry

    lax.fori_loop(lo_ref[i], hi_ref[i], step, 0)
    dq_ref[...] = (query_sum[...].T * HEAD_DIM**-0.5).astype(BF16)

    @pl.when(i == pl.num_programs(0) - 1)
    def _():
        at = 0
        for part in (dbef_ref, down_ref, daft_ref):
            size = part.shape[1]
            part[0] = key_sum[at : at + size, :].astype(part.dtype)
            part[1] = value_sum[at : at + size, :].astype(part.dtype)
            at += size
        at = 0
        for k in range(2):
            for c in range(2):
                dpre_ref[at : at + PREFIX_ROWS, :] = prefix_sum[k, :, c * 128 : (c + 1) * 128].astype(BF16)
                at += PREFIX_ROWS


def attend_back(queries, grads, wide, total, parts, prefix, docs, causal):
    query_doc, key_doc, lo, hi = docs
    rows, cols = queries.shape
    count, _, block = query_doc.shape
    window = key_doc.shape[0]
    halo = parts[0].shape[1]

    def whole(shape):
        return pl.BlockSpec(shape, lambda i, *_: (0,) * len(shape))

    def blocked():
        return pl.BlockSpec((block, cols), lambda i, *_: (i, 0))

    return pl.pallas_call(
        partial(attend_back_kernel, halo, causal),
        grid_spec=pltpu.PrefetchScalarGridSpec(
            num_scalar_prefetch=2,
            grid=(count,),
            in_specs=[
                blocked(),
                blocked(),
                blocked(),
                pl.BlockSpec((1, 1, HEADS * block), lambda i, *_: (i, 0, 0)),
                whole(parts[0].shape),
                whole(parts[1].shape),
                whole(parts[2].shape),
                whole(prefix.shape),
                pl.BlockSpec((1, 1, block), lambda i, *_: (i, 0, 0)),
                whole(key_doc.shape),
            ],
            out_specs=[
                blocked(),
                whole(parts[0].shape),
                whole(parts[1].shape),
                whole(parts[2].shape),
                whole((4 * PREFIX_ROWS, 128)),
            ],
            scratch_shapes=[
                pltpu.VMEM((window, cols), BF16),
                pltpu.VMEM((window, cols), BF16),
                pltpu.VMEM((window // KEY_BLOCK, cols, KEY_BLOCK), BF16),
                pltpu.VMEM((window, cols), F32),
                pltpu.VMEM((window, cols), F32),
                pltpu.VMEM((cols, block), F32),
                pltpu.VMEM(prefix.shape, F32),
            ],
        ),
        out_shape=[
            jax.ShapeDtypeStruct((rows, cols), BF16),
            jax.ShapeDtypeStruct(parts[0].shape, BF16),
            jax.ShapeDtypeStruct(parts[1].shape, BF16),
            jax.ShapeDtypeStruct(parts[2].shape, BF16),
            jax.ShapeDtypeStruct((4 * PREFIX_ROWS, 128), BF16),
        ],
        compiler_params=pltpu.CompilerParams(vmem_limit_bytes=VMEM_BYTES),
        cost_estimate=pl.CostEstimate(
            flops=40 * rows * 1024 * cols, bytes_accessed=16 * window * cols, transcendentals=4 * rows * 1024
        ),
    )(lo, hi, queries, grads, wide, total, *parts, prefix, query_doc, key_doc)


class Place:
    def __init__(self, n_seq):
        self.n_seq = n_seq
        self.s = lax.axis_index("seq")
        self.t = lax.axis_index("tp")
        self.core = self.t % 2
        self.other = 1 - self.core
        self.y = self.t // 2
        self.twin_t = self.t + 1 - 2 * self.core
        self.across_t = (self.t + 2) % 4
        self.twin = (self.s, self.twin_t)
        self.across = (self.s, self.across_t)
        self.after = ((self.s + 1) % n_seq, self.t)
        self.before = ((self.s + n_seq - 1) % n_seq, self.t)

    def greet(self, partners, seq_sum=None):
        barrier = pltpu.get_barrier_semaphore()
        for partner in partners:
            pl.semaphore_signal(barrier, inc=1, device_id=partner, device_id_type=MESH)
        count = len(partners)
        if seq_sum is not None:
            count += seq_sum.greet(barrier)
        pl.semaphore_wait(barrier, count)


class Sems:
    def __init__(self, send, receive):
        self.send, self.receive, self.used = send, receive, 0

    def take(self):
        kind = self.used
        self.used += 1
        return kind


def remote(sems, kind, j, src, dst, device):
    return pltpu.make_async_remote_copy(
        src_ref=src,
        dst_ref=dst,
        send_sem=sems.send.at[kind, j],
        recv_sem=sems.receive.at[kind, j],
        device_id=device,
        device_id_type=MESH,
    )


def span(j):
    return pl.ds(pl.multiple_of(j * SEGMENT, SEGMENT), SEGMENT)


class Loaded:
    def __init__(self, loads, buf, *sources):
        self.buf, self.at, self.shape = buf, buf.at, buf.shape
        self.copies = []
        for source, part in sources:
            target = buf if part is None else buf.at[part]
            self.copies.append(pltpu.make_async_copy(source, target, loads.send.at[loads.take()]))
        for copy in self.copies:
            copy.start()

    def wait(self):
        for copy in self.copies:
            copy.wait()

    def __getitem__(self, index):
        return self.buf[index]


class Stored:
    def __init__(self, sems, result, buf, parts):
        self.result, self.buf, self.parts, self.sems = result, buf, parts, sems
        self.at, self.shape = buf.at, buf.shape
        self.kind = sems.take()

    def copies(self, j):
        return [
            pltpu.make_async_copy(
                self.buf.at[part], self.result.at[part], self.sems.receive.at[self.kind, 2 * j + i]
            )
            for i, part in enumerate(self.parts(j))
        ]

    def flush(self, j):
        for copy in self.copies(j):
            copy.start()

    def drain(self, j):
        for copy in self.copies(j):
            copy.wait()

    def __getitem__(self, index):
        return self.buf[index]

    def __setitem__(self, index, value):
        self.buf[index] = value


class Twins:
    def __init__(self, place, sems, buf):
        self.place, self.sems, self.buf, self.kind = place, sems, buf, sems.take()

    def copy(self, j, half):
        part = self.buf.at[half, span(j)]
        return remote(self.sems, self.kind, j, part, part, self.place.twin)

    def put(self, j, value):
        self.buf[self.place.core, span(j)] = value
        self.copy(j, self.place.core).start()

    def wait(self, j):
        self.copy(j, self.place.other).wait_recv()

    def both(self, j):
        return jnp.concatenate([self.buf[self.place.core, span(j)], self.buf[self.place.other, span(j)]], axis=0)

    def drain(self, j):
        self.copy(j, self.place.core).wait_send()


class TwinResult:
    def __init__(self, place, sems, local, result, stage):
        self.place, self.sems, self.local, self.result, self.stage = place, sems, local, result, stage
        self.kind, self.kind_local = sems.take(), local.take()

    def copies(self, j):
        rows, core = span(j), self.place.core
        return (
            remote(self.sems, self.kind, j, self.stage.at[rows], self.result.at[core, rows], self.place.twin),
            pltpu.make_async_copy(
                self.stage.at[rows], self.result.at[core, rows], self.local.receive.at[self.kind_local, 2 * j]
            ),
        )

    def put(self, j, value):
        self.stage[span(j)] = value
        for copy in self.copies(j):
            copy.start()

    def drain(self, j):
        out, local = self.copies(j)
        out.wait_send()
        local.wait()
        part = self.result.at[self.place.other, span(j)]
        remote(self.sems, self.kind, j, part, part, self.place.twin).wait_recv()


class Total:
    SHAPES = staticmethod(
        lambda half: [
            pltpu.VMEM((half, 1024), F32),
            pltpu.VMEM((half, 1024), BF16),
            pltpu.VMEM((half, 1024), BF16),
            pltpu.VMEM((half, 1024), BF16),
            pltpu.VMEM((half, 1024), BF16),
        ]
    )

    def __init__(self, place, sems, refs):
        self.place, self.sems = place, sems
        self.mine, self.away, self.came, self.chip, self.far = refs
        self.kind_twin, self.kind_across = sems.take(), sems.take()

    def twin_copy(self, j):
        rows = span(j)
        return remote(self.sems, self.kind_twin, j, self.away.at[rows], self.came.at[rows], self.place.twin)

    def across_copy(self, j):
        rows = span(j)
        return remote(self.sems, self.kind_across, j, self.chip.at[rows], self.far.at[rows], self.place.across)

    def put(self, j, value):
        self.mine[span(j)] = value[:SEGMENT]
        self.away[span(j)] = value[SEGMENT:].astype(BF16)
        self.twin_copy(j).start()

    def middle(self, j):
        self.twin_copy(j).wait_recv()
        self.chip[span(j)] = (self.mine[span(j)] + self.came[span(j)].astype(F32)).astype(BF16)
        self.across_copy(j).start()

    def get(self, j):
        self.across_copy(j).wait_recv()
        return self.chip[span(j)].astype(F32) + self.far[span(j)].astype(F32)

    def drain(self, j):
        self.twin_copy(j).wait_send()
        self.across_copy(j).wait_send()


class SeqSum:
    @staticmethod
    def scratch(n_seq, rows):
        dma = pltpu.SemaphoreType.DMA
        group = n_seq // 2
        return [
            pltpu.VMEM((rows, 128), BF16),
            pltpu.VMEM((group, rows // group, 128), BF16),
            pltpu.VMEM((2, rows // group, 128), BF16),
            pltpu.VMEM((rows, 128), BF16),
            dma((2, group)),
            dma((2, group)),
        ]

    def __init__(self, place, refs):
        self.place = place
        self.terms, self.landing, self.pair, self.total, self.sent, self.came = refs
        self.group, self.size = self.landing.shape[:2]
        self.parity, self.rank = place.s % 2, place.s // 2
        self.partner = (place.s + 1 - 2 * self.parity, place.t)

    def member(self, k):
        return (self.rank + k) % self.group

    def piece(self, rank):
        return pl.ds(pl.multiple_of(rank * self.size, self.size), self.size)

    def copy(self, phase, k, src, dst, device):
        return pltpu.make_async_remote_copy(
            src_ref=src,
            dst_ref=dst,
            send_sem=self.sent.at[phase, k],
            recv_sem=self.came.at[phase, k],
            device_id=device,
            device_id_type=MESH,
        )

    def device(self, k):
        return (self.member(k) * 2 + self.parity, self.place.t)

    def greet(self, barrier):
        def signal(k, carry):
            pl.semaphore_signal(barrier, inc=1, device_id=self.device(k), device_id_type=MESH)
            return carry

        lax.fori_loop(1, self.group, signal, 0)
        return self.group - 1

    def term_copy(self, k):
        return self.copy(0, k, self.terms.at[self.piece(self.member(k))], self.landing.at[k], self.device(k))

    def pair_copy(self):
        return self.copy(0, 0, self.pair.at[0], self.pair.at[1], self.partner)

    def total_copy(self, k):
        mine = self.total.at[self.piece(self.rank)]
        return self.copy(1, k, mine, mine, self.device(k))

    def total_arrival(self, k):
        theirs = self.total.at[self.piece(self.member(self.group - k))]
        return self.copy(1, k, theirs, theirs, self.device(k))

    def loop(self, action):
        def step(k, carry):
            action(k)
            return carry

        lax.fori_loop(1, self.group, step, 0)

    def some(self, j, action):
        lot = -(-(self.group - 1) // 3)

        def step(k, carry):
            action(k)
            return carry

        lax.fori_loop(1 + j * lot, jnp.minimum(1 + (j + 1) * lot, self.group), step, 0)

    def send_terms(self, j):
        self.some(j, lambda k: self.term_copy(k).start())

    def add(self, j):
        self.loop(lambda k: self.term_copy(k).wait_recv())

        def step(k, total):
            return total + self.landing[k].astype(F32)

        mine = self.terms[self.piece(self.rank)].astype(F32)
        self.pair[0] = lax.fori_loop(1, self.group, step, mine).astype(BF16)
        self.pair_copy().start()

    def join(self, j):
        self.pair_copy().wait_recv()
        total = self.pair[0].astype(F32) + self.pair[1].astype(F32)
        self.total[self.piece(self.rank)] = total.astype(BF16)

    def send_totals(self, j):
        self.some(j, lambda k: self.total_copy(k).start())

    def stages(self, delay):
        return [
            (delay, 3, self.send_terms), (delay + 5, 1, self.add), (delay + 7, 1, self.join),
            (delay + 7, 3, self.send_totals),
        ]

    def wait(self):
        self.loop(lambda k: self.total_arrival(k).wait_recv())

    def drain(self):
        self.loop(lambda k: self.term_copy(k).wait_send())
        self.pair_copy().wait_send()
        self.loop(lambda k: self.total_copy(k).wait_send())


def weight_terms(terms, rows, grad_side, side, grads):
    tall = rows.shape[0] * rows.shape[1]
    width, adapt = rows.shape[2], side.shape[2]

    def flat(ref):
        return ref[...].reshape(tall, ref.shape[2])

    down = mm_tn(flat(grad_side), flat(rows))
    up = 4.0 * mm_tn(flat(side), flat(grads))
    for i, term in enumerate((down, up)):
        for c in range(width // 128):
            at = (i * (width // 128) + c) * adapt
            terms[at : at + adapt] = term[:, c * 128 : (c + 1) * 128].astype(BF16)


def weight_sums(total, down, up):
    width, adapt = down.shape
    for c in range(width // 128):
        down[c * 128 : (c + 1) * 128, :] = total[c * adapt : (c + 1) * adapt].astype(F32).T
        at = (width // 128 + c) * adapt
        up[:, c * 128 : (c + 1) * 128] = total[at : at + adapt].astype(F32)


class Heads:
    @staticmethod
    def scratch(half, cols, width):
        return [
            pltpu.VMEM((2, half, 2 * cols), BF16),
            pltpu.VMEM((half, width), F32),
            pltpu.VMEM((half, width), BF16),
            pltpu.VMEM((half, width), BF16),
        ]

    def __init__(self, place, sems, own, refs):
        self.place, self.sems, self.own = place, sems, own
        self.both, self.mine, self.away, self.came = refs
        self.cols = own.shape[2]
        self.kind, self.kind_twin = sems.take(), sems.take()

    def part(self, j, y):
        return self.both.at[:, span(j), pl.ds(pl.multiple_of(y * self.cols, self.cols), self.cols)]

    def copy(self, j):
        src = self.own.at[:, span(j)]
        return remote(self.sems, self.kind, j, src, self.part(j, self.place.y), self.place.across)

    def arrival(self, j):
        part = self.part(j, 1 - self.place.y)
        return remote(self.sems, self.kind, j, part, part, self.place.across)

    def twin_copy(self, j):
        rows = span(j)
        return remote(self.sems, self.kind_twin, j, self.away.at[rows], self.came.at[rows], self.place.twin)

    def send(self, j):
        self.copy(j).start()
        self.part(j, self.place.y)[...] = self.own[:, span(j)]

    def mix(self, j, weight):
        self.arrival(j).wait_recv()
        piece = mm(own_first(self.place, self.both, j), weight[...])
        self.mine[span(j)] = piece[:SEGMENT]
        self.away[span(j)] = piece[SEGMENT:].astype(BF16)
        self.twin_copy(j).start()

    def get(self, j):
        self.twin_copy(j).wait_recv()
        return self.mine[span(j)] + self.came[span(j)].astype(F32)

    def drain(self, j):
        self.copy(j).wait_send()
        self.twin_copy(j).wait_send()


class Halo:
    def __init__(self, place, sems, rows, halo):
        self.place, self.sems, self.rows, self.halo = place, sems, rows, halo
        self.half = rows // 2
        self.up = [sems.take() if hh * self.half >= rows - halo else None for hh in range(2)]
        self.down = [sems.take() if hh * self.half < halo else None for hh in range(2)]

    def place_up(self, hh, j):
        return span(j + (hh * self.half - (self.rows - self.halo)) // SEGMENT)

    def place_down(self, hh, j):
        return span(j + hh * self.half // SEGMENT)

    def out_copies(self, j, own, before, after):
        copies = []
        for hh in range(2):
            src = own.at[:, self.place_down(hh, j)]
            if self.up[hh] is not None:
                dst = before.at[:, self.place_up(hh, j)]
                copies.append(remote(self.sems, self.up[hh], j, src, dst, self.place.after))
            if self.down[hh] is not None:
                dst = after.at[:, self.place_down(hh, j)]
                copies.append(remote(self.sems, self.down[hh], j, src, dst, self.place.before))
        return copies

    def back_copies(self, j, before, after, from_before, from_after):
        copies = []
        for hh in range(2):
            if self.up[hh] is not None:
                where = self.place_up(hh, j)
                copies.append(
                    remote(self.sems, self.up[hh], j, before.at[:, where], from_after.at[:, where], self.place.before)
                )
            if self.down[hh] is not None:
                where = self.place_down(hh, j)
                copies.append(
                    remote(self.sems, self.down[hh], j, after.at[:, where], from_before.at[:, where], self.place.after)
                )
        return copies

    def gathered(self, j, hh, own, from_before, from_after):
        total = own[:, self.place_down(hh, j)].astype(F32)
        if self.down[hh] is not None:
            total = total + from_before[:, self.place_down(hh, j)].astype(F32)
        if self.up[hh] is not None:
            total = total + from_after[:, self.place_up(hh, j)].astype(F32)
        return total


def pipeline(stages):
    last = max(delay + n for delay, n, _ in stages)

    def step(s, carry):
        for delay, n, stage in stages:
            pl.when((s >= delay) & (s < n + delay))(partial(stage, s - delay))
        return carry

    lax.fori_loop(0, last, step, 0)


def at_first(j, *loads):
    @pl.when(j == 0)
    def _():
        for load in loads:
            load.wait()


def each(n, *actions):
    def step(j, carry):
        for action in actions:
            action(j)
        return carry

    lax.fori_loop(0, n, step, 0)


def exchange_call(kernel, cid, args, loads, outs, scratch, kinds, local_kinds, n, flops):
    anywhere = pl.BlockSpec(memory_space=pl.ANY)
    moved = sum(a.size * a.dtype.itemsize for a in args)
    dma = pltpu.SemaphoreType.DMA
    return pl.pallas_call(
        kernel,
        in_specs=[anywhere] * len(args),
        out_specs=[anywhere] * len(outs),
        out_shape=[jax.ShapeDtypeStruct(shape, kind) for shape, kind in outs],
        scratch_shapes=[pltpu.VMEM(shape, kind) for shape, kind in loads]
        + scratch
        + [dma((3 * len(args),)), dma((max(local_kinds, 1), 2 * n)), dma((kinds, n)), dma((kinds, n))],
        compiler_params=pltpu.CompilerParams(
            collective_id=cid, has_side_effects=True, vmem_limit_bytes=VMEM_BYTES
        ),
        cost_estimate=pl.CostEstimate(flops=flops, bytes_accessed=moved, transcendentals=0),
    )(*args)


def feed_rows(rows, inner, outer, hidden):
    acts, slopes = gelu_parts(mm(rows, inner[...]))
    side = acts[:, hidden:]
    four = (4.0 * side.astype(F32)).astype(BF16)
    return mm(jnp.concatenate([acts[:, :hidden], four], axis=1), outer[...]), slopes, side


def feed_rows_back(grads, slopes, inner, outer, hidden):
    back = slopes.astype(F32) * mm_nt(grads, outer[...])
    grad_side = (4.0 * back[:, hidden:]).astype(BF16)
    back = jnp.concatenate([back[:, :hidden].astype(BF16), grad_side], axis=1)
    return mm_nt(back, inner[...]), grad_side


def rows_of(place, *_):
    return lambda j: [span(j)]


def both_rows(place):
    return lambda j: [(place.core, span(j)), (place.other, span(j))]


def own_first(place, ref, j):
    return jnp.concatenate([ref[place.core, span(j)], ref[place.other, span(j)]], axis=0)


def put_both(place, ref, j, value):
    ref[place.core, span(j)] = value[:SEGMENT]
    ref[place.other, span(j)] = value[SEGMENT:]


def forward_kernel(
    n_seq, halo_rows,
    a_, x_, gains_, wo_, w1_, w2_, wd_, wu_, wkv_, da_, dx_, dgains_, dwo_, dwq_,
    e1_, e3_, hidden_, slope_, side_, kv_, before, after, t1_, t2_, q_,
    a, x, gains, wo, inner, outer, wkv, da, dx, dgains, dwo, dwq,
    e1, e3, hidden, slope, side, kv, t1, t2, q,
    h0, h1, h2, h3, e2, s0, s1, s2, s3, s4, encoded, k0, k1, k2, k3, dhidden,
    loading, local_sems, send, receive,
):
    place, sems, local = Place(n_seq), Sems(send, receive), Sems(local_sems, local_sems)
    loads = Sems(loading, loading)
    half, dec_half = e1.shape[0], t1.shape[0]
    n, m = half // SEGMENT, dec_half // SEGMENT
    core = place.core
    width, wide_hidden, cols = w1_.shape[0], w1_.shape[1], dwq_.shape[1]
    a = Loaded(loads, a, (a_, None))
    x = Loaded(loads, x, (x_.at[core], None))
    gains = Loaded(loads, gains, (gains_, None))
    wo = Loaded(loads, wo, (wo_, None))
    inner = Loaded(
        loads, inner, (w1_, (slice(None), slice(0, wide_hidden))), (wd_, (slice(None), slice(wide_hidden, None)))
    )
    outer = Loaded(loads, outer, (w2_, slice(0, wide_hidden)), (wu_, slice(wide_hidden, None)))
    da = Loaded(loads, da, (da_, None))
    dx = Loaded(loads, dx, (dx_.at[core], None))
    dgains = Loaded(loads, dgains, (dgains_, None))
    dwo = Loaded(loads, dwo, (dwo_, None))
    dwq = Loaded(loads, dwq, (dwq_, None))
    wkv = Loaded(
        loads, wkv, (wkv_.at[0], (slice(None), slice(0, cols))), (wkv_.at[1], (slice(None), slice(cols, None)))
    )
    rows_j, both_j = rows_of(place), both_rows(place)
    e1 = Stored(local, e1_, e1, rows_j)
    e3 = Stored(local, e3_, e3, rows_j)
    hidden = Stored(local, hidden_, hidden, both_j)
    slope = Stored(local, slope_, slope, lambda j: [j])
    side = Stored(local, side_, side, both_j)
    kv = Stored(local, kv_, kv, lambda j: [(slice(None), span(j)), (slice(None), span(j + n))])
    t1 = Stored(local, t1_, t1, rows_j)
    t2 = Stored(local, t2_, t2, rows_j)
    q = Stored(local, q_, q, both_j)
    heads = Heads(place, sems, a, (h0, h1, h2, h3))
    low = Twins(place, sems, hidden)
    total = Total(place, sems, (s0, s1, s2, s3, s4))
    low_encoded = Twins(place, sems, encoded)
    halo = Halo(place, sems, 2 * half, halo_rows)
    dec_heads = Heads(place, sems, da, (k0, k1, k2, k3))
    dec_low = Twins(place, sems, dhidden)
    place.greet([place.twin, place.across, place.before, place.after])
    a.wait()
    da.wait()

    def mix(j):
        at_first(j, wo)
        heads.mix(j, wo)

    def mixed(j):
        at_first(j, x, gains)
        rows = span(j)
        first = x[rows].astype(F32) + heads.get(j)
        e1[rows] = first
        e1.flush(j)
        middle = normalize(first, gains[0:1])
        e2[rows] = middle
        low.put(j, middle.astype(BF16))

    def feed(j):
        at_first(j, inner, outer)
        low.wait(j)
        hidden.flush(j)
        piece, slopes, side_rows = feed_rows(low.both(j), inner, outer, wide_hidden)
        total.put(j, piece)
        slope[j] = slopes
        put_both(place, side, j, side_rows)
        slope.flush(j)
        side.flush(j)

    def finish(j):
        rows = span(j)
        second = e2[rows] + total.get(j)
        low_encoded.put(j, normalize(second, gains[1:2]).astype(BF16))
        e3[rows] = second
        e3.flush(j)

    def memory(j):
        at_first(j, wkv)
        low_encoded.wait(j)
        made = mm(low_encoded.both(j), wkv[...]).astype(BF16)
        for i in range(2):
            kv[i, span(j + place.core * n)] = made[:SEGMENT, i * cols : (i + 1) * cols]
            kv[i, span(j + place.other * n)] = made[SEGMENT:, i * cols : (i + 1) * cols]
        for copy in halo.out_copies(j, kv, before, after):
            copy.start()
        kv.flush(j)

    def dec_mix(j):
        at_first(j, dwo)
        dec_heads.mix(j, dwo)

    def dec_mixed(j):
        at_first(j, dx, dgains)
        rows = span(j)
        first = dx[rows].astype(F32) + dec_heads.get(j)
        t1[rows] = first
        t1.flush(j)
        middle = normalize(first, dgains[0:1])
        t2[rows] = middle
        t2.flush(j)
        dec_low.put(j, middle.astype(BF16))

    def dec_query(j):
        at_first(j, dwq)
        dec_low.wait(j)
        put_both(place, q, j, mm(dec_low.both(j), dwq[...]).astype(BF16))
        q.flush(j)

    pipeline(
        [
            (0, n, heads.send), (3, n, total.middle), (1, n, mix), (2, n, feed), (0, m, dec_heads.send),
            (2, m, dec_mix), (1, n, mixed), (3, m, dec_query), (4, n, finish), (2, m, dec_mixed), (5, n, memory),
        ]
    )

    def arrived(j):
        for copy in halo.out_copies(j, kv, before, after):
            copy.wait()

    each(
        n, heads.drain, low.drain, total.drain, low_encoded.drain, arrived, e1.drain, e3.drain, hidden.drain,
        slope.drain, side.drain, kv.drain,
    )
    each(m, dec_heads.drain, dec_low.drain, t1.drain, t2.drain, q.drain)


def decoder_chain_kernel(
    n_seq,
    a_, t2_, real_, cotangent_, gains_, wo_, w1_, w2_, wd_, wu_, mixing_,
    decoded, g2_, da_, terms_,
    a, t2, real, cotangent, gains, wo, inner, outer, mixing,
    g2, da, terms, stage,
    h0, h1, h2, h3, t3, t4, g3, hidden, low_g3, low_g2, slope, side, grad_side,
    f0, f1, f2, f3, f4, b0, b1, b2, b3, b4,
    loading, local_sems, send, receive,
):
    place, sems, local = Place(n_seq), Sems(send, receive), Sems(local_sems, local_sems)
    loads = Sems(loading, loading)
    half = t2.shape[0]
    n = half // SEGMENT
    core = place.core
    wide_hidden = w1_.shape[1]
    a = Loaded(loads, a, (a_, None))
    t2 = Loaded(loads, t2, (t2_, None))
    gains = Loaded(loads, gains, (gains_, None))
    wo = Loaded(loads, wo, (wo_, None))
    inner = Loaded(
        loads, inner, (w1_, (slice(None), slice(0, wide_hidden))), (wd_, (slice(None), slice(wide_hidden, None)))
    )
    outer = Loaded(loads, outer, (w2_, slice(0, wide_hidden)), (wu_, slice(wide_hidden, None)))
    real = Loaded(loads, real, (real_.at[core], None))
    cotangent = Loaded(loads, cotangent, (cotangent_.at[core], None))
    mixing = Loaded(loads, mixing, (mixing_, None))
    g2 = Stored(local, g2_, g2, rows_of(place))
    da = Stored(local, da_, da, both_rows(place))
    terms = Stored(local, terms_, terms, lambda j: [slice(None)])
    heads = Heads(place, sems, a, (h0, h1, h2, h3))
    low = Twins(place, sems, hidden)
    ahead = Total(place, sems, (f0, f1, f2, f3, f4))
    result = TwinResult(place, sems, local, decoded, stage)
    back3 = Twins(place, sems, low_g3)
    behind = Total(place, sems, (b0, b1, b2, b3, b4))
    back2 = Twins(place, sems, low_g2)
    place.greet([place.twin, place.across])
    a.wait()

    def mix(j):
        at_first(j, wo)
        heads.mix(j, wo)

    def mixed(j):
        at_first(j, t2, gains)
        rows = span(j)
        second = t2[rows] + heads.get(j)
        t3[rows] = second
        late = normalize(second, gains[1:2])
        t4[rows] = late
        low.put(j, late.astype(BF16))

    def feed(j):
        at_first(j, inner, outer)
        low.wait(j)
        piece, slopes, side_rows = feed_rows(low.both(j), inner, outer, wide_hidden)
        ahead.put(j, piece)
        slope[j] = slopes
        put_both(place, side, j, side_rows)

    def turn(j):
        at_first(j, real, cotangent)
        rows = span(j)
        third = t4[rows] + ahead.get(j)
        mask = real[rows]
        grad = normalize_back(third, gains[2:3], cotangent[rows].astype(F32) * mask)
        back3.put(j, grad.astype(BF16))
        g3[rows] = grad
        result.put(j, normalize(third, gains[2:3]) * mask)

    def feed_back(j):
        back3.wait(j)
        piece, side_rows = feed_rows_back(back3.both(j), slope[j], inner, outer, wide_hidden)
        behind.put(j, piece)
        put_both(place, grad_side, j, side_rows)

    def weights(j):
        weight_terms(terms, hidden, grad_side, side, low_g3)
        terms.flush(0)

    def finish(j):
        rows = span(j)
        grad = normalize_back(t3[rows], gains[1:2], g3[rows] + behind.get(j))
        back2.put(j, grad.astype(BF16))
        g2[rows] = grad
        g2.flush(j)

    def heads_back(j):
        at_first(j, mixing)
        back2.wait(j)
        put_both(place, da, j, mm_nt(back2.both(j), mixing[...]).astype(BF16))
        da.flush(j)

    pipeline(
        [
            (0, n, heads.send), (3, n, ahead.middle), (7, n, behind.middle), (1, n, mix), (2, n, feed),
            (1, n, mixed), (5, n, turn), (6, n, feed_back), (9, n, finish), (10, n, heads_back), (n + 7, 1, weights),
        ]
    )
    each(
        n, heads.drain, low.drain, ahead.drain, result.drain, back3.drain, behind.drain, back2.drain,
        g2.drain, da.drain,
    )
    terms.drain(0)


def key_rows(place, halo, j, scratch, own, from_before, from_after):
    for hh in range(2):
        scratch[hh] = halo.gathered(j, hh, own, from_before, from_after).astype(BF16)
    return jnp.concatenate(
        [
            jnp.concatenate([scratch[place.core, i], scratch[place.other, i]], axis=0) for i in range(2)
        ],
        axis=1,
    )


def backward_kernel(
    n_seq, halo_rows,
    dbefore_, dafter_, dkv_, wkv_, e3_, e1_, gains_, hidden_, slope_, side_, w1_, w2_, wd_, wu_,
    mixing_, dq_, dg2_, t1_, dgains_, dwq_, dmixing_, dterms_,
    g1_, da_, terms_, dg1_, dda_, ddown_, dup_,
    dbefore, dafter, dkv, wkv, e3, e1, gains, hidden, slope, side, inner, outer,
    mixing, dq, dg2, t1, dgains, dwq, dmixing, seq_terms,
    g1, da, terms, dg1, dda, ddown, dup,
    from_before, from_after, rounded, g2, low_g2, low_g1, grad_side,
    f0, f1, f2, f3, f4, b0, b1, b2, b3, b4, dlow_g1, d0, d1, d2, d3, d4,
    seq_landing, seq_pair, seq_total, seq_sent, seq_came,
    loading, local_sems, send, receive,
):
    place, sems, local = Place(n_seq), Sems(send, receive), Sems(local_sems, local_sems)
    loads = Sems(loading, loading)
    half, dec_half = e1.shape[0], t1.shape[0]
    n, m = half // SEGMENT, dec_half // SEGMENT
    wide_hidden, cols = w1_.shape[1], dwq_.shape[1]
    dbefore = Loaded(loads, dbefore, (dbefore_, None))
    dafter = Loaded(loads, dafter, (dafter_, None))
    dterms = Loaded(loads, seq_terms, (dterms_, None))
    seq_sum = SeqSum(place, (seq_terms, seq_landing, seq_pair, seq_total, seq_sent, seq_came))
    dq = Loaded(loads, dq, (dq_, None))
    dwq = Loaded(loads, dwq, (dwq_, None))
    dkv = Loaded(loads, dkv, (dkv_, None))
    wkv = Loaded(
        loads, wkv, (wkv_.at[0], (slice(None), slice(0, cols))), (wkv_.at[1], (slice(None), slice(cols, None)))
    )
    e3 = Loaded(loads, e3, (e3_, None))
    gains = Loaded(loads, gains, (gains_, None))
    dg2 = Loaded(loads, dg2, (dg2_, None))
    t1 = Loaded(loads, t1, (t1_, None))
    dgains = Loaded(loads, dgains, (dgains_, None))
    dmixing = Loaded(loads, dmixing, (dmixing_, None))
    outer = Loaded(loads, outer, (w2_, slice(0, wide_hidden)), (wu_, slice(wide_hidden, None)))
    slope = Loaded(loads, slope, (slope_, None))
    inner = Loaded(
        loads, inner, (w1_, (slice(None), slice(0, wide_hidden))), (wd_, (slice(None), slice(wide_hidden, None)))
    )
    e1 = Loaded(loads, e1, (e1_, None))
    mixing = Loaded(loads, mixing, (mixing_, None))
    hidden = Loaded(loads, hidden, (hidden_, None))
    side = Loaded(loads, side, (side_, None))
    rows_j, both_j = rows_of(place), both_rows(place)
    g1 = Stored(local, g1_, g1, rows_j)
    da = Stored(local, da_, da, both_j)
    terms = Stored(local, terms_, terms, lambda j: [slice(None)])
    dg1 = Stored(local, dg1_, dg1, rows_j)
    dda = Stored(local, dda_, dda, both_j)
    ddown = Stored(local, ddown_, ddown, lambda j: [slice(None)])
    dup = Stored(local, dup_, dup, lambda j: [slice(None)])
    halo = Halo(place, sems, 2 * half, halo_rows)
    first = Total(place, sems, (f0, f1, f2, f3, f4))
    back2 = Twins(place, sems, low_g2)
    second = Total(place, sems, (b0, b1, b2, b3, b4))
    back1 = Twins(place, sems, low_g1)
    dec_total = Total(place, sems, (d0, d1, d2, d3, d4))
    dec_back = Twins(place, sems, dlow_g1)
    place.greet([place.twin, place.across, place.before, place.after], seq_sum)
    dbefore.wait()
    dafter.wait()

    def leave(j):
        for copy in halo.back_copies(j, dbefore, dafter, from_before, from_after):
            copy.start()

    dterms.wait()

    def start(j):
        at_first(j, dkv, wkv)
        for copy in halo.back_copies(j, dbefore, dafter, from_before, from_after):
            copy.wait_recv()
        first.put(j, mm_nt(key_rows(place, halo, j, rounded, dkv, from_before, from_after), wkv[...]))

    def turn(j):
        at_first(j, e3, gains)
        rows = span(j)
        grad = normalize_back(e3[rows], gains[1:2], first.get(j))
        g2[rows] = grad
        back2.put(j, grad.astype(BF16))

    def feed_back(j):
        at_first(j, slope, inner, outer)
        back2.wait(j)
        piece, side_rows = feed_rows_back(back2.both(j), slope[j], inner, outer, wide_hidden)
        second.put(j, piece)
        put_both(place, grad_side, j, side_rows)

    def weights(j):
        hidden.wait()
        side.wait()
        weight_terms(terms, hidden, grad_side, side, low_g2)
        terms.flush(0)

    def finish(j):
        at_first(j, e1)
        rows = span(j)
        grad = normalize_back(e1[rows], gains[0:1], g2[rows] + second.get(j))
        back1.put(j, grad.astype(BF16))
        g1[rows] = grad
        g1.flush(j)

    def heads_back(j):
        at_first(j, mixing)
        back1.wait(j)
        put_both(place, da, j, mm_nt(back1.both(j), mixing[...]).astype(BF16))
        da.flush(j)

    def dec_start(j):
        at_first(j, dq, dwq)
        dec_total.put(j, mm_nt(own_first(place, dq, j), dwq[...]))

    def dec_finish(j):
        at_first(j, dg2, t1, dgains)
        rows = span(j)
        grad = normalize_back(t1[rows], dgains[0:1], dg2[rows] + dec_total.get(j))
        dec_back.put(j, grad.astype(BF16))
        dg1[rows] = grad
        dg1.flush(j)

    def dec_heads_back(j):
        at_first(j, dmixing)
        dec_back.wait(j)
        put_both(place, dda, j, mm_nt(dec_back.both(j), dmixing[...]).astype(BF16))
        dda.flush(j)

    pipeline(
        [
            (0, n, leave), (1, m, dec_total.middle), (3, n, first.middle), (7, n, second.middle), (0, m, dec_start),
            (2, n, start), (5, n, turn), (6, n, feed_back), (3, m, dec_finish), (4, m, dec_heads_back),
            (9, n, finish), (10, n, heads_back), (n + 7, 1, weights), *seq_sum.stages(4),
        ]
    )
    seq_sum.wait()
    weight_sums(seq_total, ddown, dup)
    ddown.flush(0)
    dup.flush(0)
    seq_sum.drain()

    def left(j):
        for copy in halo.back_copies(j, dbefore, dafter, from_before, from_after):
            copy.wait_send()

    each(n, left, first.drain, back2.drain, second.drain, back1.drain, g1.drain, da.drain)
    each(m, dec_total.drain, dec_back.drain, dg1.drain, dda.drain)
    terms.drain(0)
    ddown.drain(0)
    dup.drain(0)


def input_back_kernel(n_seq, halos, *refs):
    refs = list(refs)

    def take(count):
        taken = refs[:count]
        del refs[:count]
        return taken

    operands = [take(6), take(6)]
    term_operands = take(4)
    results = take(2)
    sum_results = take(5)
    buffers = [take(6), take(6)]
    stages = take(2)
    sums = take(5)
    scratch = [take(8), take(8)]
    seq_refs = take(6)
    loading, local_sems, send, receive = refs
    place, sems, local = Place(n_seq), Sems(send, receive), Sems(local_sems, local_sems)
    counter = Sems(loading, loading)
    loads = []
    for k in range(2):
        weights = operands[k][4]
        parts = [[(operand, None)] for operand in operands[k]]
        parts[4] = [
            (weights.at[i], (slice(None), slice(i * weights.shape[2], (i + 1) * weights.shape[2])))
            for i in range(3)
        ]
        loads.append([Loaded(counter, buf, *part) for part, buf in zip(parts, buffers[k])])
    seq_terms = seq_refs[0]
    seq_sum = SeqSum(place, seq_refs)
    at, term_loads = 0, []
    for term in term_operands:
        term_loads.append(Loaded(counter, seq_terms, (term, slice(at, at + term.shape[0]))))
        at += term.shape[0]
    sums = [Stored(local, result, buf, lambda j: [slice(None)]) for result, buf in zip(sum_results, sums)]
    seq_terms[at:] = jnp.zeros((seq_terms.shape[0] - at, 128), BF16)
    place.greet([place.twin, place.across, place.before, place.after], seq_sum)
    pieces, drains = [], []
    for k in range(2):
        dbefore, dafter, dq, dkv, weights, g1 = loads[k]
        from_before, from_after, rounded = scratch[k][:3]
        half = stages[k].shape[0]
        n = half // SEGMENT
        halo = Halo(place, sems, 2 * half, halos[k])
        total = Total(place, sems, scratch[k][3:])
        result = TwinResult(place, sems, local, results[k], stages[k])
        dbefore.wait()
        dafter.wait()

        def copies(j, halo=halo, refs=(dbefore, dafter, from_before, from_after)):
            return halo.back_copies(j, *refs)

        def leave(j, copies=copies):
            for copy in copies(j):
                copy.start()

        def start(j, k=k, halo=halo, total=total, copies=copies):
            dbefore, dafter, dq, dkv, weights, g1 = loads[k]
            from_before, from_after, rounded = scratch[k][:3]
            at_first(j, dq, dkv, weights)
            for copy in copies(j):
                copy.wait_recv()
            key_grads = key_rows(place, halo, j, rounded, dkv, from_before, from_after)
            grads = jnp.concatenate([own_first(place, dq, j), key_grads], axis=1)
            total.put(j, mm_nt(grads, weights[...]))

        def finish(j, g1=g1, total=total, result=result):
            at_first(j, g1)
            result.put(j, g1[span(j)] + total.get(j))

        def left(j, copies=copies):
            for copy in copies(j):
                copy.wait_send()

        pieces.append((n, leave, start, total, finish))
        drains.append((n, left, total.drain, result.drain))
    for load in term_loads:
        load.wait()
    stages_ = seq_sum.stages(1)
    for offset, (n, leave, start, total, finish) in zip((0, 0), pieces):
        stages_ += [
            (offset, n, leave), (offset + 3, n, total.middle), (offset + 2, n, start), (offset + 5, n, finish),
        ]
    pipeline(stages_)
    seq_sum.wait()
    seq_total = seq_refs[3]
    weight_sums(seq_total, sums[0], sums[1])
    at = 2 * sums[0].shape[0]
    for k in range(2, 5):
        for i in range(2):
            for c in range(2):
                part = seq_total[at : at + PREFIX_ROWS].astype(F32)
                sums[k][i, :, c * 128 : (c + 1) * 128] = part[0:PREFIX]
                at += PREFIX_ROWS
    for result in sums:
        result.flush(0)
    for n, *actions in drains:
        each(n, *actions)
    seq_sum.drain()
    for result in sums:
        result.drain(0)


def document_plan(query_docs, key_docs, query_rows, key_rows_, halo, block, causal):
    s = lax.axis_index("seq")
    own = lax.dynamic_slice_in_dim(query_docs, s * query_rows, query_rows)
    filler = jnp.full((halo,), -1, jnp.int32)
    padded = jnp.concatenate([filler, key_docs, filler])
    window = key_rows_ + 2 * halo
    keys = lax.dynamic_slice_in_dim(padded, s * key_rows_, window)
    blocks = own.reshape(-1, block)
    top = jnp.max(blocks, axis=1)
    bottom = jnp.min(jnp.where(blocks >= 0, blocks, 2**30), axis=1)
    read = (keys[None] >= bottom[:, None]) & (keys[None] <= top[:, None])
    index = jnp.arange(window, dtype=jnp.int32)[None]
    lo = jnp.min(jnp.where(read, index, window), axis=1) // KEY_BLOCK
    hi = (jnp.max(jnp.where(read, index + 1, 0), axis=1) + KEY_BLOCK - 1) // KEY_BLOCK
    if causal:
        ends = halo + block * (1 + jnp.arange(blocks.shape[0], dtype=jnp.int32))
        hi = jnp.minimum(hi, (ends + KEY_BLOCK - 1) // KEY_BLOCK)
    rows = jnp.where(blocks >= 0, blocks, -2)[:, None, :]
    return rows, keys[:, None], lo, hi


def halo_parts(kv, halo):
    size = lax.axis_size("seq")
    rows = kv.shape[1]
    up = [(i, i + 1) for i in range(size - 1)]
    down = [(i + 1, i) for i in range(size - 1)]
    before = lax.ppermute(kv[:, rows - halo :], "seq", up)
    after = lax.ppermute(kv[:, :halo], "seq", down)
    return before, kv, after


def across_y(array):
    return lax.all_gather(array, "tp", axis_index_groups=[[0, 2], [1, 3]], tiled=True)


def halves(array):
    return array.reshape((2, array.shape[0] // 2) + array.shape[1:])


def exchange_scratch(half, *kinds):
    shapes = []
    for kind in kinds:
        if kind == "total":
            shapes += Total.SHAPES(half)
        elif kind[0] == "heads":
            shapes += Heads.scratch(kind[1], 256, 1024)
        else:
            shape, dtype = kind
            shapes.append(pltpu.VMEM(shape, dtype))
    return shapes


def reaches_far(n_seq, source_document, target_document):
    source_docs = source_document.reshape(n_seq, -1)
    target_docs = target_document.reshape(n_seq, -1)

    def smallest(docs):
        return jnp.min(jnp.where(docs >= 0, docs, 2**30), axis=1)

    lows = jnp.minimum(smallest(source_docs), smallest(target_docs))
    highs = jnp.maximum(jnp.max(source_docs, axis=1), jnp.max(target_docs, axis=1))
    after_low = jnp.concatenate([lows[1:], jnp.full((1,), 2**30, jnp.int32)])[:, None]
    before_high = jnp.concatenate([jnp.full((1,), -1, jnp.int32), highs[:-1]])[:, None]
    far = False
    for docs in (source_docs, target_docs):
        half = docs.shape[1] // 2
        far = far | jnp.any(docs[:, :half] >= after_low)
        far = far | jnp.any((docs[:, half:] >= 0) & (docs[:, half:] <= before_high))
    return far


def on_device(n_seq, *args):
    far = reaches_far(n_seq, args[2], args[3])
    return lax.cond(far, partial(on_device_with, n_seq, True), partial(on_device_with, n_seq, False), *args)


def on_device_with(
    n_seq,
    wide,
    source,
    target,
    source_document,
    target_document,
    cotangent,
    encoder_attention,
    encoder_mixing,
    encoder_gains,
    encoder_inner,
    encoder_outer,
    encoder_prefix,
    encoder_down,
    encoder_up,
    decoder_attention,
    decoder_mixing,
    decoder_prefix,
    cross_query,
    cross_memory,
    cross_mixing,
    cross_prefix,
    decoder_gains,
    decoder_inner,
    decoder_outer,
    decoder_down,
    decoder_up,
):
    ids = iter(range(1 + 16 * int(wide), 100))
    source_rows, width = source.shape
    target_rows = target.shape[0]
    cols = encoder_mixing.shape[0]
    hidden = encoder_inner.shape[1]
    adapt = encoder_down.shape[1]
    source_halo = source_rows if wide else source_rows // 2
    target_halo = target_rows if wide else target_rows // 2
    source_half, target_half = source_rows // 2, target_rows // 2
    source_n, target_n = source_half // SEGMENT, target_half // SEGMENT
    chunk = 2 * SEGMENT

    encoder_wo, decoder_wo, cross_wo = map(across_y, (encoder_mixing, decoder_mixing, cross_mixing))

    def padded(prefix):
        return jnp.pad(prefix, ((0, 0), (0, PREFIX_ROWS - prefix.shape[1]), (0, 0)))

    encoder_prefix, decoder_prefix, cross_prefix = map(padded, (encoder_prefix, decoder_prefix, cross_prefix))

    encoder_q, encoder_kv = project(source, encoder_attention)
    encoder_parts = halo_parts(encoder_kv, source_halo)
    decoder_q, decoder_kv = project(target, decoder_attention)
    decoder_parts = halo_parts(decoder_kv, target_halo)

    encoder_docs = document_plan(
        source_document, source_document, source_rows, source_rows, source_halo, QUERY_BLOCK, False
    )
    decoder_docs = document_plan(
        target_document, target_document, target_rows, target_rows, target_halo, QUERY_BLOCK, True
    )
    cross_docs = document_plan(
        target_document, source_document, target_rows, source_rows, source_halo, QUERY_BLOCK, False
    )
    own_target = lax.dynamic_slice_in_dim(target_document, lax.axis_index("seq") * target_rows, target_rows)
    real = halves((own_target >= 0).astype(F32)[:, None])

    decoder_wide, decoder_low, decoder_total = attend(
        decoder_q, decoder_parts, decoder_prefix, decoder_docs, True
    )
    encoder_q, decoder_low = lax.optimization_barrier((encoder_q, decoder_low))
    encoder_wide, encoder_low, encoder_total = attend(
        encoder_q, encoder_parts, encoder_prefix, encoder_docs, False
    )
    gathered_source = ((source_half, width), F32)
    gathered_target = ((target_half, width), F32)
    source_low = ((2, source_half, width), BF16)
    target_low = ((2, target_half, width), BF16)
    source_cols = ((2, source_half, cols), BF16)
    target_cols = ((2, target_half, cols), BF16)
    slopes = [((source_n, chunk, hidden + adapt), BF16), ((2, source_half, adapt), BF16)]
    inner_buf, outer_buf = ((width, hidden + adapt), BF16), ((hidden + adapt, width), BF16)
    mixing_buf = ((2 * cols, width), BF16)

    def whole(*arrays):
        return [(array.shape, array.dtype) for array in arrays]

    halo_cols = ((2, source_halo, cols), BF16)
    kv_cols = ((2, source_rows, cols), BF16)
    stored = [gathered_source, gathered_source, source_low, *slopes, kv_cols]
    stored_target = [gathered_target, gathered_target, target_cols]
    args = (
        halves(encoder_low), halves(source), encoder_gains, encoder_wo, encoder_inner, encoder_outer,
        encoder_down, encoder_up, cross_memory, halves(decoder_low), halves(target), decoder_gains,
        decoder_wo, cross_query,
    )
    loads = [
        *whole(args[0]), ((source_half, width), BF16), *whole(args[2]), mixing_buf, inner_buf, outer_buf,
        ((width, 2 * cols), BF16), *whole(args[9]), ((target_half, width), BF16), *whole(args[11]), mixing_buf,
        *whole(args[13]),
    ]
    (
        e1, e3, encoder_hidden, encoder_slope, encoder_side, cross_kv, cross_before, cross_after, t1, t2, cross_q,
    ) = exchange_call(
        partial(forward_kernel, n_seq, source_halo),
        next(ids),
        args,
        loads,
        [*stored, halo_cols, halo_cols, *stored_target],
        exchange_scratch(
            source_half,
            *stored,
            *stored_target,
            ("heads", source_half),
            gathered_source,
            "total",
            source_low,
            ("heads", target_half),
            target_low,
        ),
        2 + 1 + 2 + 1 + (4 if wide else 2) + 2 + 1,
        9,
        source_n,
        2 * source_rows * width * (2 * hidden + 2 * adapt + 6 * cols),
    )
    cross_parts = (cross_before, cross_kv, cross_after)
    cross_q = cross_q.reshape(target_rows, cols)
    cross_wide, cross_low, cross_total = attend(cross_q, cross_parts, cross_prefix, cross_docs, False)

    terms = ((2 * width, adapt), BF16)
    sums = [((width, adapt), F32), ((adapt, width), F32)]
    args = (
        halves(cross_low), t2, real, halves(cotangent), decoder_gains, cross_wo, decoder_inner,
        decoder_outer, decoder_down, decoder_up, cross_mixing,
    )
    loads = [
        *whole(args[0], args[1]), ((target_half, 1), F32), ((target_half, width), BF16), *whole(args[4]),
        mixing_buf, inner_buf, outer_buf, *whole(args[10]),
    ]
    stored = [gathered_target, target_cols, terms]
    decoded, g2, cross_da, decoder_terms = exchange_call(
        partial(decoder_chain_kernel, n_seq),
        next(ids),
        args,
        loads,
        [((2, target_half, width), F32), *stored],
        exchange_scratch(
            target_half,
            *stored,
            gathered_target,
            ("heads", target_half),
            gathered_target,
            gathered_target,
            gathered_target,
            target_low,
            target_low,
            target_low,
            ((target_n, chunk, hidden + adapt), BF16),
            ((2, target_half, adapt), BF16),
            ((2, target_half, adapt), BF16),
            "total",
            "total",
        ),
        2 + 1 + 2 + 1 + 1 + 2 + 1,
        4,
        target_n,
        2 * target_rows * width * (4 * hidden + 6 * adapt + 2 * cols),
    )
    cross_dq, cross_dbefore, cross_dkv, cross_dafter, cross_prefix_terms = attend_back(
        cross_q, cross_da.reshape(target_rows, cols), cross_wide, cross_total, cross_parts, cross_prefix,
        cross_docs, False,
    )
    args = (
        cross_dbefore, cross_dafter, cross_dkv, cross_memory, e3, e1, encoder_gains, encoder_hidden,
        encoder_slope, encoder_side, encoder_inner, encoder_outer, encoder_down, encoder_up,
        encoder_mixing, halves(cross_dq), g2, t1, decoder_gains, cross_query, decoder_mixing,
        decoder_terms,
    )
    loads = [
        *whole(*args[:3]), ((width, 2 * cols), BF16), *whole(*args[4:10]), inner_buf, outer_buf, *whole(*args[14:]),
    ]
    stored = [gathered_source, source_cols, terms, gathered_target, target_cols, *sums]
    (
        encoder_g1, encoder_da, encoder_terms, decoder_g1, decoder_da, decoder_down_gradient, decoder_up_gradient,
    ) = exchange_call(
        partial(backward_kernel, n_seq, source_halo),
        next(ids),
        args,
        loads,
        stored,
        exchange_scratch(
            source_half,
            *stored,
            halo_cols,
            halo_cols,
            ((2, 2, SEGMENT, cols), BF16),
            gathered_source,
            source_low,
            source_low,
            ((2, source_half, adapt), BF16),
            "total",
            "total",
            target_low,
        )
        + exchange_scratch(target_half, "total")
        + SeqSum.scratch(n_seq, 2 * width)[1:],
        (4 if wide else 2) + 2 + 1 + 2 + 1 + 2 + 1,
        7,
        source_n,
        2 * source_rows * width * (2 * hidden + 4 * adapt + 4 * cols),
    )
    ddq, ddbefore, ddkv, ddafter, decoder_prefix_terms = attend_back(
        decoder_q, decoder_da.reshape(target_rows, cols), decoder_wide, decoder_total, decoder_parts,
        decoder_prefix, decoder_docs, True,
    )
    edq, edbefore, edkv, edafter, encoder_prefix_terms = attend_back(
        encoder_q, encoder_da.reshape(source_rows, cols), encoder_wide, encoder_total, encoder_parts,
        encoder_prefix, encoder_docs, False,
    )
    args = (
        edbefore, edafter, halves(edq), edkv, encoder_attention, encoder_g1,
        ddbefore, ddafter, halves(ddq), ddkv, decoder_attention, decoder_g1,
        encoder_terms, encoder_prefix_terms, decoder_prefix_terms, cross_prefix_terms,
    )
    loads = whole(*args[:12])
    loads[4] = loads[10] = ((width, 3 * cols), BF16)
    prefix_sum = ((2, PREFIX, cols), F32)
    results = [*sums, prefix_sum, prefix_sum, prefix_sum]
    seq_rows = 2 * width + 512
    (
        source_gradient, target_gradient, encoder_down_gradient, encoder_up_gradient, encoder_prefix_gradient,
        decoder_prefix_gradient, cross_prefix_gradient,
    ) = exchange_call(
        partial(input_back_kernel, n_seq, (source_halo, target_halo)),
        next(ids),
        args,
        loads,
        [((2, source_half, width), F32), ((2, target_half, width), F32), *results],
        exchange_scratch(source_half, gathered_source, gathered_target, *results)
        + exchange_scratch(source_half, halo_cols, halo_cols, ((2, 2, SEGMENT, cols), BF16), "total")
        + exchange_scratch(
            target_half,
            ((2, target_halo, cols), BF16),
            ((2, target_halo, cols), BF16),
            ((2, 2, SEGMENT, cols), BF16),
            "total",
        )
        + SeqSum.scratch(n_seq, seq_rows),
        2 * ((4 if wide else 2) + 2 + 1),
        7,
        source_n,
        6 * (source_rows + target_rows) * width * cols,
    )
    source_gradient = source_gradient.reshape(source_rows, width)
    target_gradient = target_gradient.reshape(target_rows, width)

    weight_totals = (
        encoder_prefix_gradient,
        encoder_down_gradient,
        encoder_up_gradient,
        decoder_prefix_gradient,
        cross_prefix_gradient,
        decoder_down_gradient,
        decoder_up_gradient,
    )
    return (decoded.reshape(target_rows, width), source_gradient, target_gradient) + tuple(weight_totals)


def solution(mesh):
    return jax.shard_map(
        partial(on_device, mesh.shape["seq"]),
        mesh=mesh,
        in_specs=(
            P("seq", None),
            P("seq", None),
            P(),
            P(),
            P("seq", None),
            P(None, None, "tp"),
            P("tp", None),
            P(),
            P(None, "tp"),
            P("tp", None),
            P(None, None, "tp"),
            P(None, "tp"),
            P("tp", None),
            P(None, None, "tp"),
            P("tp", None),
            P(None, None, "tp"),
            P(None, "tp"),
            P(None, None, "tp"),
            P("tp", None),
            P(None, None, "tp"),
            P(),
            P(None, "tp"),
            P("tp", None),
            P(None, "tp"),
            P("tp", None),
        ),
        out_specs=(
            P("seq", None),
            P("seq", None),
            P("seq", None),
            P(None, None, "tp"),
            P(None, "tp"),
            P("tp", None),
            P(None, None, "tp"),
            P(None, None, "tp"),
            P(None, "tp"),
            P("tp", None),
        ),
        check_vma=False,
    )
```

```python
from functools import partial

import jax
import jax.numpy as jnp
from jax import lax
from jax.experimental import pallas as pl
from jax.experimental.pallas import tpu as pltpu
from jax.sharding import PartitionSpec as P

HEAD_DIM = 64
EPSILON = 1e-05
NEGATIVE = -1e30
HEADS = 4
KEY_BLOCK = 256
QUERY_BLOCK = 256
PREFIX = 30
PREFIX_ROWS = 32
SEGMENT = 64
MESH = pl.DeviceIdType.MESH
F32 = jnp.float32
BF16 = jnp.bfloat16
VMEM_BYTES = 63 * 2**20


def mm(left, right):
    return jnp.dot(left, right, preferred_element_type=F32)


def mm_nt(left, right):
    return lax.dot_general(left, right, (((1,), (1,)), ((), ())), preferred_element_type=F32)


def mm_tn(left, right):
    return lax.dot_general(left, right, (((0,), (0,)), ((), ())), preferred_element_type=F32)


def normalize(inputs, scaling):
    centered = inputs - jnp.mean(inputs, axis=-1, keepdims=True)
    spread = lax.rsqrt(jnp.mean(centered * centered, axis=-1, keepdims=True) + EPSILON)
    return scaling * (centered * spread)


def normalize_back(inputs, scaling, gradient):
    centered = inputs - jnp.mean(inputs, axis=-1, keepdims=True)
    spread = lax.rsqrt(jnp.mean(centered * centered, axis=-1, keepdims=True) + EPSILON)
    unit = centered * spread
    scaled = gradient * scaling
    first = jnp.mean(scaled, axis=-1, keepdims=True)
    second = jnp.mean(scaled * unit, axis=-1, keepdims=True)
    return spread * (scaled - first - unit * second)


def gelu_parts(inputs):
    chance = 0.5 * (1.0 + lax.erf(inputs * (0.5**0.5)))
    density = jnp.exp(-0.5 * inputs * inputs) * 0.3989422804014327
    return (inputs * chance).astype(BF16), (chance + inputs * density).astype(BF16)


def project_kernel(x_ref, w_ref, q_ref, kv_ref):
    rows = x_ref[...]
    q_ref[...] = mm(rows, w_ref[0]).astype(BF16)
    kv_ref[0] = mm(rows, w_ref[1]).astype(BF16)
    kv_ref[1] = mm(rows, w_ref[2]).astype(BF16)


def project(inputs, weights):
    rows, width = inputs.shape
    block = 256
    cols = weights.shape[2]
    return pl.pallas_call(
        project_kernel,
        grid=(rows // block,),
        in_specs=[
            pl.BlockSpec((block, width), lambda i: (i, 0)),
            pl.BlockSpec(weights.shape, lambda i: (0, 0, 0)),
        ],
        out_specs=[
            pl.BlockSpec((block, cols), lambda i: (i, 0)),
            pl.BlockSpec((2, block, cols), lambda i: (0, i, 0)),
        ],
        out_shape=[
            jax.ShapeDtypeStruct((rows, cols), BF16),
            jax.ShapeDtypeStruct((2, rows, cols), BF16),
        ],
        compiler_params=pltpu.CompilerParams(vmem_limit_bytes=VMEM_BYTES),
        cost_estimate=pl.CostEstimate(
            flops=6 * rows * width * cols, bytes_accessed=8 * rows * cols + 6 * width * cols, transcendentals=0
        ),
    )(inputs, weights)


def by_heads(rows, lane_head):
    zero = jnp.zeros_like(rows)
    return jnp.concatenate([jnp.where(lane_head == h, rows, zero) for h in range(HEADS)], axis=0)


def head_bias(kd_ref, qd_ref, start, first_query, halo, block, causal):
    key_doc = kd_ref[pl.ds(start, KEY_BLOCK), :]
    allowed = key_doc == qd_ref[0]
    if causal:
        key_place = start - halo + lax.broadcasted_iota(jnp.int32, (KEY_BLOCK, block), 0)
        query_place = first_query + lax.broadcasted_iota(jnp.int32, (KEY_BLOCK, block), 1)
        allowed = allowed & (key_place <= query_place)
    bias = jnp.where(allowed, 0.0, NEGATIVE)
    return jnp.concatenate([bias] * HEADS, axis=1)


def prefix_scores(pre_ref, stacked):
    scores = mm_nt(pre_ref[0], stacked)
    row = lax.broadcasted_iota(jnp.int32, scores.shape, 0)
    return jnp.where(row < PREFIX, scores, NEGATIVE)


def fill_window(window, parts, index):
    at = 0
    for part in parts:
        size = part.shape[1]
        window[at : at + size, :] = part[index]
        at += size


def attend_kernel(
    halo, causal, lo_ref, hi_ref, q_ref, bef_ref, own_ref, aft_ref, pre_ref, qd_ref, kd_ref,
    wide_ref, low_ref, total_ref, keys, values, blended,
):
    i = pl.program_id(0)
    block = q_ref.shape[0]
    parts = (bef_ref, own_ref, aft_ref)

    @pl.when(i == 0)
    def _():
        fill_window(keys, parts, 0)
        at = 0
        for part in parts:
            for k in range(part.shape[1] // KEY_BLOCK):
                values[at] = part[1, k * KEY_BLOCK : (k + 1) * KEY_BLOCK, :].T
                at += 1

    lane_head = lax.broadcasted_iota(jnp.int32, q_ref.shape, 1) // HEAD_DIM
    stacked = by_heads(q_ref[...] * jnp.asarray(HEAD_DIM**-0.5, BF16), lane_head)
    scores = prefix_scores(pre_ref, stacked)
    highest = jnp.max(scores, axis=0, keepdims=True)
    chances = jnp.exp(scores - highest)
    summed = jnp.sum(chances, axis=0, keepdims=True)
    low = chances.astype(BF16)
    pre_values = pre_ref[1].T
    for h in range(HEADS):
        rows = slice(h * HEAD_DIM, (h + 1) * HEAD_DIM)
        blended[rows, :] = mm(pre_values[rows, :], low[:, h * block : (h + 1) * block])

    def step(kb, carry):
        highest, summed = carry
        start = pl.multiple_of(kb * KEY_BLOCK, KEY_BLOCK)
        scores = mm_nt(keys[pl.ds(start, KEY_BLOCK), :], stacked)
        scores = scores + head_bias(kd_ref, qd_ref, start, i * block, halo, block, causal)
        top = jnp.maximum(highest, jnp.max(scores, axis=0, keepdims=True))
        fade = jnp.exp(highest - top)
        chances = jnp.exp(scores - top)
        summed = summed * fade + jnp.sum(chances, axis=0, keepdims=True)
        low = chances.astype(BF16)
        for h in range(HEADS):
            rows = slice(h * HEAD_DIM, (h + 1) * HEAD_DIM)
            cols = slice(h * block, (h + 1) * block)
            blended[rows, :] = blended[rows, :] * fade[:, cols] + mm(values[kb, rows, :], low[:, cols])
        return top, summed

    highest, summed = lax.fori_loop(lo_ref[i], hi_ref[i], step, (highest, summed))
    total_ref[0] = highest + jnp.log(summed)
    inverse = 1.0 / summed
    for h in range(HEADS):
        rows = slice(h * HEAD_DIM, (h + 1) * HEAD_DIM)
        blended[rows, :] = blended[rows, :] * inverse[:, h * block : (h + 1) * block]
    result = blended[...].T
    wide_ref[...] = result
    low_ref[...] = result.astype(BF16)


def attend(queries, parts, prefix, docs, causal):
    query_doc, key_doc, lo, hi = docs
    rows, cols = queries.shape
    count, _, block = query_doc.shape
    window = key_doc.shape[0]
    halo = parts[0].shape[1]

    def whole(array):
        return pl.BlockSpec(array.shape, lambda i, *_: (0,) * array.ndim)

    return pl.pallas_call(
        partial(attend_kernel, halo, causal),
        grid_spec=pltpu.PrefetchScalarGridSpec(
            num_scalar_prefetch=2,
            grid=(count,),
            in_specs=[
                pl.BlockSpec((block, cols), lambda i, *_: (i, 0)),
                whole(parts[0]),
                whole(parts[1]),
                whole(parts[2]),
                whole(prefix),
                pl.BlockSpec((1, 1, block), lambda i, *_: (i, 0, 0)),
                whole(key_doc),
            ],
            out_specs=[
                pl.BlockSpec((block, cols), lambda i, *_: (i, 0)),
                pl.BlockSpec((block, cols), lambda i, *_: (i, 0)),
                pl.BlockSpec((1, 1, HEADS * block), lambda i, *_: (i, 0, 0)),
            ],
            scratch_shapes=[
                pltpu.VMEM((window, cols), BF16),
                pltpu.VMEM((window // KEY_BLOCK, cols, KEY_BLOCK), BF16),
                pltpu.VMEM((cols, block), F32),
            ],
        ),
        out_shape=[
            jax.ShapeDtypeStruct((rows, cols), F32),
            jax.ShapeDtypeStruct((rows, cols), BF16),
            jax.ShapeDtypeStruct((count, 1, HEADS * block), F32),
        ],
        compiler_params=pltpu.CompilerParams(vmem_limit_bytes=VMEM_BYTES),
        cost_estimate=pl.CostEstimate(
            flops=16 * rows * 1024 * cols, bytes_accessed=8 * window * cols, transcendentals=4 * rows * 1024
        ),
    )(lo, hi, queries, *parts, prefix, query_doc, key_doc)


def attend_back_kernel(
    halo, causal, lo_ref, hi_ref, q_ref, g_ref, wide_ref, total_ref, bef_ref, own_ref, aft_ref, pre_ref,
    qd_ref, kd_ref, dq_ref, dbef_ref, down_ref, daft_ref, dpre_ref,
    keys, values, turned, key_sum, value_sum, query_sum, prefix_sum,
):
    i = pl.program_id(0)
    block = q_ref.shape[0]
    parts = (bef_ref, own_ref, aft_ref)

    @pl.when(i == 0)
    def _():
        fill_window(keys, parts, 0)
        fill_window(values, parts, 1)
        at = 0
        for part in parts:
            for k in range(part.shape[1] // KEY_BLOCK):
                turned[at] = part[0, k * KEY_BLOCK : (k + 1) * KEY_BLOCK, :].T
                at += 1
        key_sum[...] = jnp.zeros_like(key_sum)
        value_sum[...] = jnp.zeros_like(value_sum)
        prefix_sum[...] = jnp.zeros_like(prefix_sum)

    lane_head = lax.broadcasted_iota(jnp.int32, q_ref.shape, 1) // HEAD_DIM
    stacked = by_heads(q_ref[...] * jnp.asarray(HEAD_DIM**-0.5, BF16), lane_head)
    grads = by_heads(g_ref[...], lane_head)
    mixed = (g_ref[...].astype(F32) * wide_ref[...]).T
    offsets = jnp.concatenate(
        [
            jnp.sum(mixed[h * HEAD_DIM : (h + 1) * HEAD_DIM, :], axis=0, keepdims=True)
            for h in range(HEADS)
        ],
        axis=1,
    )
    total = total_ref[0]
    chances = jnp.exp(prefix_scores(pre_ref, stacked) - total)
    score_grad = (chances * (mm_nt(pre_ref[1], grads) - offsets)).astype(BF16)
    prefix_sum[0] += mm(score_grad, stacked)
    prefix_sum[1] += mm(chances.astype(BF16), grads)
    pre_keys = pre_ref[0].T
    for h in range(HEADS):
        rows = slice(h * HEAD_DIM, (h + 1) * HEAD_DIM)
        query_sum[rows, :] = mm(pre_keys[rows, :], score_grad[:, h * block : (h + 1) * block])

    def step(kb, carry):
        start = pl.multiple_of(kb * KEY_BLOCK, KEY_BLOCK)
        here = pl.ds(start, KEY_BLOCK)
        scores = mm_nt(keys[here, :], stacked)
        scores = scores + head_bias(kd_ref, qd_ref, start, i * block, halo, block, causal)
        chances = jnp.exp(scores - total)
        score_grad = (chances * (mm_nt(values[here, :], grads) - offsets)).astype(BF16)
        key_sum[here, :] += mm(score_grad, stacked)
        value_sum[here, :] += mm(chances.astype(BF16), grads)
        for h in range(HEADS):
            rows = slice(h * HEAD_DIM, (h + 1) * HEAD_DIM)
            query_sum[rows, :] += mm(turned[kb, rows, :], score_grad[:, h * block : (h + 1) * block])
        return carry

    lax.fori_loop(lo_ref[i], hi_ref[i], step, 0)
    dq_ref[...] = (query_sum[...].T * HEAD_DIM**-0.5).astype(BF16)

    @pl.when(i == pl.num_programs(0) - 1)
    def _():
        at = 0
        for part in (dbef_ref, down_ref, daft_ref):
            size = part.shape[1]
            part[0] = key_sum[at : at + size, :].astype(part.dtype)
            part[1] = value_sum[at : at + size, :].astype(part.dtype)
            at += size
        at = 0
        for k in range(2):
            for c in range(2):
                dpre_ref[at : at + PREFIX_ROWS, :] = prefix_sum[k, :, c * 128 : (c + 1) * 128].astype(BF16)
                at += PREFIX_ROWS


def attend_back(queries, grads, wide, total, parts, prefix, docs, causal):
    query_doc, key_doc, lo, hi = docs
    rows, cols = queries.shape
    count, _, block = query_doc.shape
    window = key_doc.shape[0]
    halo = parts[0].shape[1]

    def whole(shape):
        return pl.BlockSpec(shape, lambda i, *_: (0,) * len(shape))

    def blocked():
        return pl.BlockSpec((block, cols), lambda i, *_: (i, 0))

    return pl.pallas_call(
        partial(attend_back_kernel, halo, causal),
        grid_spec=pltpu.PrefetchScalarGridSpec(
            num_scalar_prefetch=2,
            grid=(count,),
            in_specs=[
                blocked(),
                blocked(),
                blocked(),
                pl.BlockSpec((1, 1, HEADS * block), lambda i, *_: (i, 0, 0)),
                whole(parts[0].shape),
                whole(parts[1].shape),
                whole(parts[2].shape),
                whole(prefix.shape),
                pl.BlockSpec((1, 1, block), lambda i, *_: (i, 0, 0)),
                whole(key_doc.shape),
            ],
            out_specs=[
                blocked(),
                whole(parts[0].shape),
                whole(parts[1].shape),
                whole(parts[2].shape),
                whole((4 * PREFIX_ROWS, 128)),
            ],
            scratch_shapes=[
                pltpu.VMEM((window, cols), BF16),
                pltpu.VMEM((window, cols), BF16),
                pltpu.VMEM((window // KEY_BLOCK, cols, KEY_BLOCK), BF16),
                pltpu.VMEM((window, cols), F32),
                pltpu.VMEM((window, cols), F32),
                pltpu.VMEM((cols, block), F32),
                pltpu.VMEM(prefix.shape, F32),
            ],
        ),
        out_shape=[
            jax.ShapeDtypeStruct((rows, cols), BF16),
            jax.ShapeDtypeStruct(parts[0].shape, BF16),
            jax.ShapeDtypeStruct(parts[1].shape, BF16),
            jax.ShapeDtypeStruct(parts[2].shape, BF16),
            jax.ShapeDtypeStruct((4 * PREFIX_ROWS, 128), BF16),
        ],
        compiler_params=pltpu.CompilerParams(vmem_limit_bytes=VMEM_BYTES),
        cost_estimate=pl.CostEstimate(
            flops=40 * rows * 1024 * cols, bytes_accessed=16 * window * cols, transcendentals=4 * rows * 1024
        ),
    )(lo, hi, queries, grads, wide, total, *parts, prefix, query_doc, key_doc)


class Place:
    def __init__(self, n_seq):
        self.n_seq = n_seq
        self.s = lax.axis_index("seq")
        self.t = lax.axis_index("tp")
        self.core = self.t % 2
        self.other = 1 - self.core
        self.y = self.t // 2
        self.twin_t = self.t + 1 - 2 * self.core
        self.across_t = (self.t + 2) % 4
        self.twin = (self.s, self.twin_t)
        self.across = (self.s, self.across_t)
        self.after = ((self.s + 1) % n_seq, self.t)
        self.before = ((self.s + n_seq - 1) % n_seq, self.t)

    def greet(self, partners, seq_sum=None):
        barrier = pltpu.get_barrier_semaphore()
        for partner in partners:
            pl.semaphore_signal(barrier, inc=1, device_id=partner, device_id_type=MESH)
        count = len(partners)
        if seq_sum is not None:
            count += seq_sum.greet(barrier)
        pl.semaphore_wait(barrier, count)


class Sems:
    def __init__(self, send, receive):
        self.send, self.receive, self.used = send, receive, 0

    def take(self):
        kind = self.used
        self.used += 1
        return kind


def remote(sems, kind, j, src, dst, device):
    return pltpu.make_async_remote_copy(
        src_ref=src,
        dst_ref=dst,
        send_sem=sems.send.at[kind, j],
        recv_sem=sems.receive.at[kind, j],
        device_id=device,
        device_id_type=MESH,
    )


def span(j):
    return pl.ds(pl.multiple_of(j * SEGMENT, SEGMENT), SEGMENT)


class Loaded:
    def __init__(self, loads, buf, *sources):
        self.buf, self.at, self.shape = buf, buf.at, buf.shape
        self.copies = []
        for source, part in sources:
            target = buf if part is None else buf.at[part]
            self.copies.append(pltpu.make_async_copy(source, target, loads.send.at[loads.take()]))
        for copy in self.copies:
            copy.start()

    def wait(self):
        for copy in self.copies:
            copy.wait()

    def __getitem__(self, index):
        return self.buf[index]


class Stored:
    def __init__(self, sems, result, buf, parts):
        self.result, self.buf, self.parts, self.sems = result, buf, parts, sems
        self.at, self.shape = buf.at, buf.shape
        self.kind = sems.take()

    def copies(self, j):
        return [
            pltpu.make_async_copy(
                self.buf.at[part], self.result.at[part], self.sems.receive.at[self.kind, 2 * j + i]
            )
            for i, part in enumerate(self.parts(j))
        ]

    def flush(self, j):
        for copy in self.copies(j):
            copy.start()

    def drain(self, j):
        for copy in self.copies(j):
            copy.wait()

    def __getitem__(self, index):
        return self.buf[index]

    def __setitem__(self, index, value):
        self.buf[index] = value


class Twins:
    def __init__(self, place, sems, buf):
        self.place, self.sems, self.buf, self.kind = place, sems, buf, sems.take()

    def copy(self, j, half):
        part = self.buf.at[half, span(j)]
        return remote(self.sems, self.kind, j, part, part, self.place.twin)

    def put(self, j, value):
        self.buf[self.place.core, span(j)] = value
        self.copy(j, self.place.core).start()

    def wait(self, j):
        self.copy(j, self.place.other).wait_recv()

    def both(self, j):
        return jnp.concatenate([self.buf[self.place.core, span(j)], self.buf[self.place.other, span(j)]], axis=0)

    def drain(self, j):
        self.copy(j, self.place.core).wait_send()


class TwinResult:
    def __init__(self, place, sems, local, result, stage):
        self.place, self.sems, self.local, self.result, self.stage = place, sems, local, result, stage
        self.kind, self.kind_local = sems.take(), local.take()

    def copies(self, j):
        rows, core = span(j), self.place.core
        return (
            remote(self.sems, self.kind, j, self.stage.at[rows], self.result.at[core, rows], self.place.twin),
            pltpu.make_async_copy(
                self.stage.at[rows], self.result.at[core, rows], self.local.receive.at[self.kind_local, 2 * j]
            ),
        )

    def put(self, j, value):
        self.stage[span(j)] = value
        for copy in self.copies(j):
            copy.start()

    def drain(self, j):
        out, local = self.copies(j)
        out.wait_send()
        local.wait()
        part = self.result.at[self.place.other, span(j)]
        remote(self.sems, self.kind, j, part, part, self.place.twin).wait_recv()


class Total:
    SHAPES = staticmethod(
        lambda half: [
            pltpu.VMEM((half, 1024), F32),
            pltpu.VMEM((half, 1024), BF16),
            pltpu.VMEM((half, 1024), BF16),
            pltpu.VMEM((half, 1024), BF16),
            pltpu.VMEM((half, 1024), BF16),
        ]
    )

    def __init__(self, place, sems, refs):
        self.place, self.sems = place, sems
        self.mine, self.away, self.came, self.chip, self.far = refs
        self.kind_twin, self.kind_across = sems.take(), sems.take()

    def twin_copy(self, j):
        rows = span(j)
        return remote(self.sems, self.kind_twin, j, self.away.at[rows], self.came.at[rows], self.place.twin)

    def across_copy(self, j):
        rows = span(j)
        return remote(self.sems, self.kind_across, j, self.chip.at[rows], self.far.at[rows], self.place.across)

    def put(self, j, value):
        self.mine[span(j)] = value[:SEGMENT]
        self.away[span(j)] = value[SEGMENT:].astype(BF16)
        self.twin_copy(j).start()

    def middle(self, j):
        self.twin_copy(j).wait_recv()
        self.chip[span(j)] = (self.mine[span(j)] + self.came[span(j)].astype(F32)).astype(BF16)
        self.across_copy(j).start()

    def get(self, j):
        self.across_copy(j).wait_recv()
        return self.chip[span(j)].astype(F32) + self.far[span(j)].astype(F32)

    def drain(self, j):
        self.twin_copy(j).wait_send()
        self.across_copy(j).wait_send()


class SeqSum:
    @staticmethod
    def scratch(n_seq, rows):
        dma = pltpu.SemaphoreType.DMA
        group = n_seq // 2
        return [
            pltpu.VMEM((rows, 128), BF16),
            pltpu.VMEM((group, rows // group, 128), BF16),
            pltpu.VMEM((2, rows // group, 128), BF16),
            pltpu.VMEM((rows, 128), BF16),
            dma((2, group)),
            dma((2, group)),
        ]

    def __init__(self, place, refs):
        self.place = place
        self.terms, self.landing, self.pair, self.total, self.sent, self.came = refs
        self.group, self.size = self.landing.shape[:2]
        self.parity, self.rank = place.s % 2, place.s // 2
        self.partner = (place.s + 1 - 2 * self.parity, place.t)

    def member(self, k):
        return (self.rank + k) % self.group

    def piece(self, rank):
        return pl.ds(pl.multiple_of(rank * self.size, self.size), self.size)

    def copy(self, phase, k, src, dst, device):
        return pltpu.make_async_remote_copy(
            src_ref=src,
            dst_ref=dst,
            send_sem=self.sent.at[phase, k],
            recv_sem=self.came.at[phase, k],
            device_id=device,
            device_id_type=MESH,
        )

    def device(self, k):
        return (self.member(k) * 2 + self.parity, self.place.t)

    def greet(self, barrier):
        def signal(k, carry):
            pl.semaphore_signal(barrier, inc=1, device_id=self.device(k), device_id_type=MESH)
            return carry

        lax.fori_loop(1, self.group, signal, 0)
        return self.group - 1

    def term_copy(self, k):
        return self.copy(0, k, self.terms.at[self.piece(self.member(k))], self.landing.at[k], self.device(k))

    def pair_copy(self):
        return self.copy(0, 0, self.pair.at[0], self.pair.at[1], self.partner)

    def total_copy(self, k):
        mine = self.total.at[self.piece(self.rank)]
        return self.copy(1, k, mine, mine, self.device(k))

    def total_arrival(self, k):
        theirs = self.total.at[self.piece(self.member(self.group - k))]
        return self.copy(1, k, theirs, theirs, self.device(k))

    def loop(self, action):
        def step(k, carry):
            action(k)
            return carry

        lax.fori_loop(1, self.group, step, 0)

    def some(self, j, action):
        lot = -(-(self.group - 1) // 3)

        def step(k, carry):
            action(k)
            return carry

        lax.fori_loop(1 + j * lot, jnp.minimum(1 + (j + 1) * lot, self.group), step, 0)

    def send_terms(self, j):
        self.some(j, lambda k: self.term_copy(k).start())

    def add(self, j):
        self.loop(lambda k: self.term_copy(k).wait_recv())

        def step(k, total):
            return total + self.landing[k].astype(F32)

        mine = self.terms[self.piece(self.rank)].astype(F32)
        self.pair[0] = lax.fori_loop(1, self.group, step, mine).astype(BF16)
        self.pair_copy().start()

    def join(self, j):
        self.pair_copy().wait_recv()
        total = self.pair[0].astype(F32) + self.pair[1].astype(F32)
        self.total[self.piece(self.rank)] = total.astype(BF16)

    def send_totals(self, j):
        self.some(j, lambda k: self.total_copy(k).start())

    def stages(self, delay):
        return [
            (delay, 3, self.send_terms), (delay + 5, 1, self.add), (delay + 7, 1, self.join),
            (delay + 7, 3, self.send_totals),
        ]

    def wait(self):
        self.loop(lambda k: self.total_arrival(k).wait_recv())

    def drain(self):
        self.loop(lambda k: self.term_copy(k).wait_send())
        self.pair_copy().wait_send()
        self.loop(lambda k: self.total_copy(k).wait_send())


def weight_terms(terms, rows, grad_side, side, grads):
    tall = rows.shape[0] * rows.shape[1]
    width, adapt = rows.shape[2], side.shape[2]

    def flat(ref):
        return ref[...].reshape(tall, ref.shape[2])

    down = mm_tn(flat(grad_side), flat(rows))
    up = 4.0 * mm_tn(flat(side), flat(grads))
    for i, term in enumerate((down, up)):
        for c in range(width // 128):
            at = (i * (width // 128) + c) * adapt
            terms[at : at + adapt] = term[:, c * 128 : (c + 1) * 128].astype(BF16)


def weight_sums(total, down, up):
    width, adapt = down.shape
    for c in range(width // 128):
        down[c * 128 : (c + 1) * 128, :] = total[c * adapt : (c + 1) * adapt].astype(F32).T
        at = (width // 128 + c) * adapt
        up[:, c * 128 : (c + 1) * 128] = total[at : at + adapt].astype(F32)


class Heads:
    @staticmethod
    def scratch(half, cols, width):
        return [
            pltpu.VMEM((2, half, 2 * cols), BF16),
            pltpu.VMEM((half, width), F32),
            pltpu.VMEM((half, width), BF16),
            pltpu.VMEM((half, width), BF16),
        ]

    def __init__(self, place, sems, own, refs):
        self.place, self.sems, self.own = place, sems, own
        self.both, self.mine, self.away, self.came = refs
        self.cols = own.shape[2]
        self.kind, self.kind_twin = sems.take(), sems.take()

    def part(self, j, y):
        return self.both.at[:, span(j), pl.ds(pl.multiple_of(y * self.cols, self.cols), self.cols)]

    def copy(self, j):
        src = self.own.at[:, span(j)]
        return remote(self.sems, self.kind, j, src, self.part(j, self.place.y), self.place.across)

    def arrival(self, j):
        part = self.part(j, 1 - self.place.y)
        return remote(self.sems, self.kind, j, part, part, self.place.across)

    def twin_copy(self, j):
        rows = span(j)
        return remote(self.sems, self.kind_twin, j, self.away.at[rows], self.came.at[rows], self.place.twin)

    def send(self, j):
        self.copy(j).start()
        self.part(j, self.place.y)[...] = self.own[:, span(j)]

    def mix(self, j, weight, product=mm):
        self.arrival(j).wait_recv()
        piece = product(own_first(self.place, self.both, j), weight[...])
        self.mine[span(j)] = piece[:SEGMENT]
        self.away[span(j)] = piece[SEGMENT:].astype(BF16)
        self.twin_copy(j).start()

    def get(self, j):
        self.twin_copy(j).wait_recv()
        return self.mine[span(j)] + self.came[span(j)].astype(F32)

    def drain(self, j):
        self.copy(j).wait_send()
        self.twin_copy(j).wait_send()


class Halo:
    def __init__(self, place, sems, rows, halo):
        self.place, self.sems, self.rows, self.halo = place, sems, rows, halo
        self.half = rows // 2
        self.up = [sems.take() if hh * self.half >= rows - halo else None for hh in range(2)]
        self.down = [sems.take() if hh * self.half < halo else None for hh in range(2)]

    def place_up(self, hh, j):
        return span(j + (hh * self.half - (self.rows - self.halo)) // SEGMENT)

    def place_down(self, hh, j):
        return span(j + hh * self.half // SEGMENT)

    def out_copies(self, j, own, before, after):
        copies = []
        for hh in range(2):
            src = own.at[:, self.place_down(hh, j)]
            if self.up[hh] is not None:
                dst = before.at[:, self.place_up(hh, j)]
                copies.append(remote(self.sems, self.up[hh], j, src, dst, self.place.after))
            if self.down[hh] is not None:
                dst = after.at[:, self.place_down(hh, j)]
                copies.append(remote(self.sems, self.down[hh], j, src, dst, self.place.before))
        return copies

    def back_copies(self, j, before, after, from_before, from_after):
        copies = []
        for hh in range(2):
            if self.up[hh] is not None:
                where = self.place_up(hh, j)
                copies.append(
                    remote(self.sems, self.up[hh], j, before.at[:, where], from_after.at[:, where], self.place.before)
                )
            if self.down[hh] is not None:
                where = self.place_down(hh, j)
                copies.append(
                    remote(self.sems, self.down[hh], j, after.at[:, where], from_before.at[:, where], self.place.after)
                )
        return copies

    def gathered(self, j, hh, own, from_before, from_after):
        total = own[:, self.place_down(hh, j)].astype(F32)
        if self.down[hh] is not None:
            total = total + from_before[:, self.place_down(hh, j)].astype(F32)
        if self.up[hh] is not None:
            total = total + from_after[:, self.place_up(hh, j)].astype(F32)
        return total


def pipeline(stages):
    last = max(delay + n for delay, n, _ in stages)

    def step(s, carry):
        for delay, n, stage in stages:
            pl.when((s >= delay) & (s < n + delay))(partial(stage, s - delay))
        return carry

    lax.fori_loop(0, last, step, 0)


def at_first(j, *loads):
    @pl.when(j == 0)
    def _():
        for load in loads:
            load.wait()


def each(n, *actions):
    def step(j, carry):
        for action in actions:
            action(j)
        return carry

    lax.fori_loop(0, n, step, 0)


def exchange_call(kernel, cid, args, loads, outs, scratch, kinds, local_kinds, n, flops):
    anywhere = pl.BlockSpec(memory_space=pl.ANY)
    moved = sum(a.size * a.dtype.itemsize for a in args)
    dma = pltpu.SemaphoreType.DMA
    return pl.pallas_call(
        kernel,
        in_specs=[anywhere] * len(args),
        out_specs=[anywhere] * len(outs),
        out_shape=[jax.ShapeDtypeStruct(shape, kind) for shape, kind in outs],
        scratch_shapes=[pltpu.VMEM(shape, kind) for shape, kind in loads]
        + scratch
        + [dma((3 * len(args),)), dma((max(local_kinds, 1), 2 * n)), dma((kinds, n)), dma((kinds, n))],
        compiler_params=pltpu.CompilerParams(
            collective_id=cid, has_side_effects=True, vmem_limit_bytes=VMEM_BYTES
        ),
        cost_estimate=pl.CostEstimate(flops=flops, bytes_accessed=moved, transcendentals=0),
    )(*args)


def feed_rows(rows, inner, outer, hidden):
    acts, slopes = gelu_parts(mm(rows, inner[...]))
    side = acts[:, hidden:]
    four = (4.0 * side.astype(F32)).astype(BF16)
    return mm(jnp.concatenate([acts[:, :hidden], four], axis=1), outer[...]), slopes, side


def feed_rows_back(grads, slopes, inner, outer, hidden):
    back = slopes.astype(F32) * mm_nt(grads, outer[...])
    grad_side = (4.0 * back[:, hidden:]).astype(BF16)
    back = jnp.concatenate([back[:, :hidden].astype(BF16), grad_side], axis=1)
    return mm_nt(back, inner[...]), grad_side


def rows_of(place, *_):
    return lambda j: [span(j)]


def both_rows(place):
    return lambda j: [(place.core, span(j)), (place.other, span(j))]


def own_first(place, ref, j):
    return jnp.concatenate([ref[place.core, span(j)], ref[place.other, span(j)]], axis=0)


def put_both(place, ref, j, value):
    ref[place.core, span(j)] = value[:SEGMENT]
    ref[place.other, span(j)] = value[SEGMENT:]


def forward_kernel(
    n_seq, halo_rows,
    a_, x_, gains_, wo_, w1_, w2_, wd_, wu_, wkv_, da_, dx_, dgains_, dwo_, dwq_,
    e1_, e3_, hidden_, slope_, side_, kv_, before, after, t1_, t2_, q_,
    a, x, gains, wo, inner, outer, wkv, da, dx, dgains, dwo, dwq,
    e1, e3, hidden, slope, side, kv, t1, t2, q,
    h0, h1, h2, h3, e2, s0, s1, s2, s3, s4, encoded, k0, k1, k2, k3, dhidden,
    loading, local_sems, send, receive,
):
    place, sems, local = Place(n_seq), Sems(send, receive), Sems(local_sems, local_sems)
    loads = Sems(loading, loading)
    half, dec_half = e1.shape[0], t1.shape[0]
    n, m = half // SEGMENT, dec_half // SEGMENT
    core = place.core
    width, wide_hidden, cols = w1_.shape[0], w1_.shape[1], dwq_.shape[1]
    a = Loaded(loads, a, (a_, None))
    x = Loaded(loads, x, (x_.at[core], None))
    gains = Loaded(loads, gains, (gains_, None))
    wo = Loaded(loads, wo, (wo_, None))
    inner = Loaded(
        loads, inner, (w1_, (slice(None), slice(0, wide_hidden))), (wd_, (slice(None), slice(wide_hidden, None)))
    )
    outer = Loaded(loads, outer, (w2_, slice(0, wide_hidden)), (wu_, slice(wide_hidden, None)))
    da = Loaded(loads, da, (da_, None))
    dx = Loaded(loads, dx, (dx_.at[core], None))
    dgains = Loaded(loads, dgains, (dgains_, None))
    dwo = Loaded(loads, dwo, (dwo_, None))
    dwq = Loaded(loads, dwq, (dwq_, None))
    wkv = Loaded(
        loads, wkv, (wkv_.at[0], (slice(None), slice(0, cols))), (wkv_.at[1], (slice(None), slice(cols, None)))
    )
    rows_j, both_j = rows_of(place), both_rows(place)
    e1 = Stored(local, e1_, e1, rows_j)
    e3 = Stored(local, e3_, e3, rows_j)
    hidden = Stored(local, hidden_, hidden, both_j)
    slope = Stored(local, slope_, slope, lambda j: [j])
    side = Stored(local, side_, side, both_j)
    kv = Stored(local, kv_, kv, lambda j: [(slice(None), span(j)), (slice(None), span(j + n))])
    t1 = Stored(local, t1_, t1, rows_j)
    t2 = Stored(local, t2_, t2, rows_j)
    q = Stored(local, q_, q, both_j)
    heads = Heads(place, sems, a, (h0, h1, h2, h3))
    low = Twins(place, sems, hidden)
    total = Total(place, sems, (s0, s1, s2, s3, s4))
    low_encoded = Twins(place, sems, encoded)
    halo = Halo(place, sems, 2 * half, halo_rows)
    dec_heads = Heads(place, sems, da, (k0, k1, k2, k3))
    dec_low = Twins(place, sems, dhidden)
    place.greet([place.twin, place.across, place.before, place.after])
    a.wait()
    da.wait()

    def mix(j):
        at_first(j, wo)
        heads.mix(j, wo)

    def mixed(j):
        at_first(j, x, gains)
        rows = span(j)
        first = x[rows].astype(F32) + heads.get(j)
        e1[rows] = first
        e1.flush(j)
        middle = normalize(first, gains[0:1])
        e2[rows] = middle
        low.put(j, middle.astype(BF16))

    def feed(j):
        at_first(j, inner, outer)
        low.wait(j)
        hidden.flush(j)
        piece, slopes, side_rows = feed_rows(low.both(j), inner, outer, wide_hidden)
        total.put(j, piece)
        slope[j] = slopes
        put_both(place, side, j, side_rows)
        slope.flush(j)
        side.flush(j)

    def finish(j):
        rows = span(j)
        second = e2[rows] + total.get(j)
        low_encoded.put(j, normalize(second, gains[1:2]).astype(BF16))
        e3[rows] = second
        e3.flush(j)

    def memory(j):
        at_first(j, wkv)
        low_encoded.wait(j)
        made = mm(low_encoded.both(j), wkv[...]).astype(BF16)
        for i in range(2):
            kv[i, span(j + place.core * n)] = made[:SEGMENT, i * cols : (i + 1) * cols]
            kv[i, span(j + place.other * n)] = made[SEGMENT:, i * cols : (i + 1) * cols]
        for copy in halo.out_copies(j, kv, before, after):
            copy.start()
        kv.flush(j)

    def dec_mix(j):
        at_first(j, dwo)
        dec_heads.mix(j, dwo)

    def dec_mixed(j):
        at_first(j, dx, dgains)
        rows = span(j)
        first = dx[rows].astype(F32) + dec_heads.get(j)
        t1[rows] = first
        t1.flush(j)
        middle = normalize(first, dgains[0:1])
        t2[rows] = middle
        t2.flush(j)
        dec_low.put(j, middle.astype(BF16))

    def dec_query(j):
        at_first(j, dwq)
        dec_low.wait(j)
        put_both(place, q, j, mm(dec_low.both(j), dwq[...]).astype(BF16))
        q.flush(j)

    pipeline(
        [
            (0, n, heads.send), (3, n, total.middle), (1, n, mix), (2, n, feed), (0, m, dec_heads.send),
            (2, m, dec_mix), (1, n, mixed), (3, m, dec_query), (4, n, finish), (2, m, dec_mixed), (5, n, memory),
        ]
    )

    def arrived(j):
        for copy in halo.out_copies(j, kv, before, after):
            copy.wait()

    each(
        n, heads.drain, low.drain, total.drain, low_encoded.drain, arrived, e1.drain, e3.drain, hidden.drain,
        slope.drain, side.drain, kv.drain,
    )
    each(m, dec_heads.drain, dec_low.drain, t1.drain, t2.drain, q.drain)


def decoder_chain_kernel(
    n_seq,
    a_, t2_, real_, cotangent_, gains_, wo_, w1_, w2_, wd_, wu_, mixing_,
    decoded, g2_, da_, terms_,
    a, t2, real, cotangent, gains, wo, inner, outer, mixing,
    g2, da, terms, stage,
    h0, h1, h2, h3, t3, t4, g3, hidden, low_g3, low_g2, slope, side, grad_side,
    f0, f1, f2, f3, f4, b0, b1, b2, b3, b4,
    loading, local_sems, send, receive,
):
    place, sems, local = Place(n_seq), Sems(send, receive), Sems(local_sems, local_sems)
    loads = Sems(loading, loading)
    half = t2.shape[0]
    n = half // SEGMENT
    core = place.core
    wide_hidden = w1_.shape[1]
    a = Loaded(loads, a, (a_, None))
    t2 = Loaded(loads, t2, (t2_, None))
    gains = Loaded(loads, gains, (gains_, None))
    wo = Loaded(loads, wo, (wo_, None))
    inner = Loaded(
        loads, inner, (w1_, (slice(None), slice(0, wide_hidden))), (wd_, (slice(None), slice(wide_hidden, None)))
    )
    outer = Loaded(loads, outer, (w2_, slice(0, wide_hidden)), (wu_, slice(wide_hidden, None)))
    real = Loaded(loads, real, (real_.at[core], None))
    cotangent = Loaded(loads, cotangent, (cotangent_.at[core], None))
    mixing = Loaded(loads, mixing, (mixing_, None))
    g2 = Stored(local, g2_, g2, rows_of(place))
    da = Stored(local, da_, da, both_rows(place))
    terms = Stored(local, terms_, terms, lambda j: [slice(None)])
    heads = Heads(place, sems, a, (h0, h1, h2, h3))
    low = Twins(place, sems, hidden)
    ahead = Total(place, sems, (f0, f1, f2, f3, f4))
    result = TwinResult(place, sems, local, decoded, stage)
    back3 = Twins(place, sems, low_g3)
    behind = Total(place, sems, (b0, b1, b2, b3, b4))
    back2 = Twins(place, sems, low_g2)
    place.greet([place.twin, place.across])
    a.wait()

    def mix(j):
        at_first(j, wo)
        heads.mix(j, wo)

    def mixed(j):
        at_first(j, t2, gains)
        rows = span(j)
        second = t2[rows] + heads.get(j)
        t3[rows] = second
        late = normalize(second, gains[1:2])
        t4[rows] = late
        low.put(j, late.astype(BF16))

    def feed(j):
        at_first(j, inner, outer)
        low.wait(j)
        piece, slopes, side_rows = feed_rows(low.both(j), inner, outer, wide_hidden)
        ahead.put(j, piece)
        slope[j] = slopes
        put_both(place, side, j, side_rows)

    def turn(j):
        at_first(j, real, cotangent)
        rows = span(j)
        third = t4[rows] + ahead.get(j)
        mask = real[rows]
        grad = normalize_back(third, gains[2:3], cotangent[rows].astype(F32) * mask)
        back3.put(j, grad.astype(BF16))
        g3[rows] = grad
        result.put(j, normalize(third, gains[2:3]) * mask)

    def feed_back(j):
        back3.wait(j)
        piece, side_rows = feed_rows_back(back3.both(j), slope[j], inner, outer, wide_hidden)
        behind.put(j, piece)
        put_both(place, grad_side, j, side_rows)

    def weights(j):
        weight_terms(terms, hidden, grad_side, side, low_g3)
        terms.flush(0)

    def finish(j):
        rows = span(j)
        grad = normalize_back(t3[rows], gains[1:2], g3[rows] + behind.get(j))
        back2.put(j, grad.astype(BF16))
        g2[rows] = grad
        g2.flush(j)

    def heads_back(j):
        at_first(j, mixing)
        back2.wait(j)
        put_both(place, da, j, mm_nt(back2.both(j), mixing[...]).astype(BF16))
        da.flush(j)

    pipeline(
        [
            (0, n, heads.send), (3, n, ahead.middle), (7, n, behind.middle), (1, n, mix), (2, n, feed),
            (1, n, mixed), (5, n, turn), (6, n, feed_back), (9, n, finish), (10, n, heads_back), (n + 7, 1, weights),
        ]
    )
    each(
        n, heads.drain, low.drain, ahead.drain, result.drain, back3.drain, behind.drain, back2.drain,
        g2.drain, da.drain,
    )
    terms.drain(0)


def key_rows(place, halo, j, scratch, own, from_before, from_after):
    for hh in range(2):
        scratch[hh] = halo.gathered(j, hh, own, from_before, from_after).astype(BF16)
    return jnp.concatenate(
        [
            jnp.concatenate([scratch[place.core, i], scratch[place.other, i]], axis=0) for i in range(2)
        ],
        axis=1,
    )


def backward_kernel(
    n_seq, halo_rows,
    dbefore_, dafter_, dkv_, wkv_, e3_, e1_, gains_, hidden_, slope_, side_, w1_, w2_, wd_, wu_,
    mixing_, dq_, dg2_, t1_, dgains_, dwq_, dmixing_, dterms_,
    g1_, da_, terms_, dg1_, dda_, ddown_, dup_,
    dbefore, dafter, dkv, wkv, e3, e1, gains, hidden, slope, side, inner, outer,
    mixing, dq, dg2, t1, dgains, dwq, dmixing, seq_terms,
    g1, da, terms, dg1, dda, ddown, dup,
    from_before, from_after, rounded, g2, low_g2, low_g1, grad_side,
    f0, f1, f2, f3, f4, b0, b1, b2, b3, b4, dlow_g1, d0, d1, d2, d3,
    seq_landing, seq_pair, seq_total, seq_sent, seq_came,
    loading, local_sems, send, receive,
):
    place, sems, local = Place(n_seq), Sems(send, receive), Sems(local_sems, local_sems)
    loads = Sems(loading, loading)
    half, dec_half = e1.shape[0], t1.shape[0]
    n, m = half // SEGMENT, dec_half // SEGMENT
    width, wide_hidden, cols = w1_.shape[0], w1_.shape[1], dwq_.shape[1]
    dbefore = Loaded(loads, dbefore, (dbefore_, None))
    dafter = Loaded(loads, dafter, (dafter_, None))
    dterms = Loaded(loads, seq_terms, (dterms_, None))
    seq_sum = SeqSum(place, (seq_terms, seq_landing, seq_pair, seq_total, seq_sent, seq_came))
    dq = Loaded(loads, dq, (dq_, None))
    dwq = Loaded(
        loads, dwq, *[(dwq_.at[y * width : (y + 1) * width], (slice(None), slice(y * cols, (y + 1) * cols))) for y in range(2)]
    )
    dkv = Loaded(loads, dkv, (dkv_, None))
    wkv = Loaded(
        loads, wkv, (wkv_.at[0], (slice(None), slice(0, cols))), (wkv_.at[1], (slice(None), slice(cols, None)))
    )
    e3 = Loaded(loads, e3, (e3_, None))
    gains = Loaded(loads, gains, (gains_, None))
    dg2 = Loaded(loads, dg2, (dg2_, None))
    t1 = Loaded(loads, t1, (t1_, None))
    dgains = Loaded(loads, dgains, (dgains_, None))
    dmixing = Loaded(loads, dmixing, (dmixing_, None))
    outer = Loaded(loads, outer, (w2_, slice(0, wide_hidden)), (wu_, slice(wide_hidden, None)))
    slope = Loaded(loads, slope, (slope_, None))
    inner = Loaded(
        loads, inner, (w1_, (slice(None), slice(0, wide_hidden))), (wd_, (slice(None), slice(wide_hidden, None)))
    )
    e1 = Loaded(loads, e1, (e1_, None))
    mixing = Loaded(loads, mixing, (mixing_, None))
    hidden = Loaded(loads, hidden, (hidden_, None))
    side = Loaded(loads, side, (side_, None))
    rows_j, both_j = rows_of(place), both_rows(place)
    g1 = Stored(local, g1_, g1, rows_j)
    da = Stored(local, da_, da, both_j)
    terms = Stored(local, terms_, terms, lambda j: [slice(None)])
    dg1 = Stored(local, dg1_, dg1, rows_j)
    dda = Stored(local, dda_, dda, both_j)
    ddown = Stored(local, ddown_, ddown, lambda j: [slice(None)])
    dup = Stored(local, dup_, dup, lambda j: [slice(None)])
    halo = Halo(place, sems, 2 * half, halo_rows)
    first = Total(place, sems, (f0, f1, f2, f3, f4))
    back2 = Twins(place, sems, low_g2)
    second = Total(place, sems, (b0, b1, b2, b3, b4))
    back1 = Twins(place, sems, low_g1)
    dec_heads = Heads(place, sems, dq, (d0, d1, d2, d3))
    dec_back = Twins(place, sems, dlow_g1)
    place.greet([place.twin, place.across, place.before, place.after], seq_sum)
    dbefore.wait()
    dafter.wait()

    def leave(j):
        for copy in halo.back_copies(j, dbefore, dafter, from_before, from_after):
            copy.start()

    dterms.wait()
    dq.wait()

    def start(j):
        at_first(j, dkv, wkv)
        for copy in halo.back_copies(j, dbefore, dafter, from_before, from_after):
            copy.wait_recv()
        first.put(j, mm_nt(key_rows(place, halo, j, rounded, dkv, from_before, from_after), wkv[...]))

    def turn(j):
        at_first(j, e3, gains)
        rows = span(j)
        grad = normalize_back(e3[rows], gains[1:2], first.get(j))
        g2[rows] = grad
        back2.put(j, grad.astype(BF16))

    def feed_back(j):
        at_first(j, slope, inner, outer)
        back2.wait(j)
        piece, side_rows = feed_rows_back(back2.both(j), slope[j], inner, outer, wide_hidden)
        second.put(j, piece)
        put_both(place, grad_side, j, side_rows)

    def weights(j):
        hidden.wait()
        side.wait()
        weight_terms(terms, hidden, grad_side, side, low_g2)
        terms.flush(0)

    def finish(j):
        at_first(j, e1)
        rows = span(j)
        grad = normalize_back(e1[rows], gains[0:1], g2[rows] + second.get(j))
        back1.put(j, grad.astype(BF16))
        g1[rows] = grad
        g1.flush(j)

    def heads_back(j):
        at_first(j, mixing)
        back1.wait(j)
        put_both(place, da, j, mm_nt(back1.both(j), mixing[...]).astype(BF16))
        da.flush(j)

    def dec_start(j):
        at_first(j, dwq)
        dec_heads.mix(j, dwq, mm_nt)

    def dec_finish(j):
        at_first(j, dg2, t1, dgains)
        rows = span(j)
        grad = normalize_back(t1[rows], dgains[0:1], dg2[rows] + dec_heads.get(j))
        dec_back.put(j, grad.astype(BF16))
        dg1[rows] = grad
        dg1.flush(j)

    def dec_heads_back(j):
        at_first(j, dmixing)
        dec_back.wait(j)
        put_both(place, dda, j, mm_nt(dec_back.both(j), dmixing[...]).astype(BF16))
        dda.flush(j)

    pipeline(
        [
            (0, n, leave), (0, m, dec_heads.send), (3, n, first.middle), (7, n, second.middle), (2, m, dec_start),
            (2, n, start), (5, n, turn), (6, n, feed_back), (3, m, dec_finish), (4, m, dec_heads_back),
            (9, n, finish), (10, n, heads_back), (n + 7, 1, weights), *seq_sum.stages(4),
        ]
    )
    seq_sum.wait()
    weight_sums(seq_total, ddown, dup)
    ddown.flush(0)
    dup.flush(0)
    seq_sum.drain()

    def left(j):
        for copy in halo.back_copies(j, dbefore, dafter, from_before, from_after):
            copy.wait_send()

    each(n, left, first.drain, back2.drain, second.drain, back1.drain, g1.drain, da.drain)
    each(m, dec_heads.drain, dec_back.drain, dg1.drain, dda.drain)
    terms.drain(0)
    ddown.drain(0)
    dup.drain(0)


def input_back_kernel(n_seq, halos, *refs):
    refs = list(refs)

    def take(count):
        taken = refs[:count]
        del refs[:count]
        return taken

    operands = [take(6), take(6)]
    term_operands = take(4)
    results = take(2)
    sum_results = take(5)
    buffers = [take(6), take(6)]
    stages = take(2)
    sums = take(5)
    scratch = [take(8), take(8)]
    seq_refs = take(6)
    loading, local_sems, send, receive = refs
    place, sems, local = Place(n_seq), Sems(send, receive), Sems(local_sems, local_sems)
    counter = Sems(loading, loading)
    loads = []
    for k in range(2):
        weights = operands[k][4]
        parts = [[(operand, None)] for operand in operands[k]]
        parts[4] = [
            (weights.at[i], (slice(None), slice(i * weights.shape[2], (i + 1) * weights.shape[2])))
            for i in range(3)
        ]
        loads.append([Loaded(counter, buf, *part) for part, buf in zip(parts, buffers[k])])
    seq_terms = seq_refs[0]
    seq_sum = SeqSum(place, seq_refs)
    at, term_loads = 0, []
    for term in term_operands:
        term_loads.append(Loaded(counter, seq_terms, (term, slice(at, at + term.shape[0]))))
        at += term.shape[0]
    sums = [Stored(local, result, buf, lambda j: [slice(None)]) for result, buf in zip(sum_results, sums)]
    seq_terms[at:] = jnp.zeros((seq_terms.shape[0] - at, 128), BF16)
    place.greet([place.twin, place.across, place.before, place.after], seq_sum)
    pieces, drains = [], []
    for k in range(2):
        dbefore, dafter, dq, dkv, weights, g1 = loads[k]
        from_before, from_after, rounded = scratch[k][:3]
        half = stages[k].shape[0]
        n = half // SEGMENT
        halo = Halo(place, sems, 2 * half, halos[k])
        total = Total(place, sems, scratch[k][3:])
        result = TwinResult(place, sems, local, results[k], stages[k])
        dbefore.wait()
        dafter.wait()

        def copies(j, halo=halo, refs=(dbefore, dafter, from_before, from_after)):
            return halo.back_copies(j, *refs)

        def leave(j, copies=copies):
            for copy in copies(j):
                copy.start()

        def start(j, k=k, halo=halo, total=total, copies=copies):
            dbefore, dafter, dq, dkv, weights, g1 = loads[k]
            from_before, from_after, rounded = scratch[k][:3]
            at_first(j, dq, dkv, weights)
            for copy in copies(j):
                copy.wait_recv()
            key_grads = key_rows(place, halo, j, rounded, dkv, from_before, from_after)
            grads = jnp.concatenate([own_first(place, dq, j), key_grads], axis=1)
            total.put(j, mm_nt(grads, weights[...]))

        def finish(j, g1=g1, total=total, result=result):
            at_first(j, g1)
            result.put(j, g1[span(j)] + total.get(j))

        def left(j, copies=copies):
            for copy in copies(j):
                copy.wait_send()

        pieces.append((n, leave, start, total, finish))
        drains.append((n, left, total.drain, result.drain))
    for load in term_loads:
        load.wait()
    stages_ = seq_sum.stages(1)
    for offset, (n, leave, start, total, finish) in zip((0, 0), pieces):
        stages_ += [
            (offset, n, leave), (offset + 3, n, total.middle), (offset + 2, n, start), (offset + 5, n, finish),
        ]
    pipeline(stages_)
    seq_sum.wait()
    seq_total = seq_refs[3]
    weight_sums(seq_total, sums[0], sums[1])
    at = 2 * sums[0].shape[0]
    for k in range(2, 5):
        for i in range(2):
            for c in range(2):
                part = seq_total[at : at + PREFIX_ROWS].astype(F32)
                sums[k][i, :, c * 128 : (c + 1) * 128] = part[0:PREFIX]
                at += PREFIX_ROWS
    for result in sums:
        result.flush(0)
    for n, *actions in drains:
        each(n, *actions)
    seq_sum.drain()
    for result in sums:
        result.drain(0)


def document_plan(query_docs, key_docs, query_rows, key_rows_, halo, block, causal):
    s = lax.axis_index("seq")
    own = lax.dynamic_slice_in_dim(query_docs, s * query_rows, query_rows)
    filler = jnp.full((halo,), -1, jnp.int32)
    padded = jnp.concatenate([filler, key_docs, filler])
    window = key_rows_ + 2 * halo
    keys = lax.dynamic_slice_in_dim(padded, s * key_rows_, window)
    blocks = own.reshape(-1, block)
    top = jnp.max(blocks, axis=1)
    bottom = jnp.min(jnp.where(blocks >= 0, blocks, 2**30), axis=1)
    read = (keys[None] >= bottom[:, None]) & (keys[None] <= top[:, None])
    index = jnp.arange(window, dtype=jnp.int32)[None]
    lo = jnp.min(jnp.where(read, index, window), axis=1) // KEY_BLOCK
    hi = (jnp.max(jnp.where(read, index + 1, 0), axis=1) + KEY_BLOCK - 1) // KEY_BLOCK
    if causal:
        ends = halo + block * (1 + jnp.arange(blocks.shape[0], dtype=jnp.int32))
        hi = jnp.minimum(hi, (ends + KEY_BLOCK - 1) // KEY_BLOCK)
    rows = jnp.where(blocks >= 0, blocks, -2)[:, None, :]
    return rows, keys[:, None], lo, hi


def halo_parts(kv, halo):
    size = lax.axis_size("seq")
    rows = kv.shape[1]
    up = [(i, i + 1) for i in range(size - 1)]
    down = [(i + 1, i) for i in range(size - 1)]
    before = lax.ppermute(kv[:, rows - halo :], "seq", up)
    after = lax.ppermute(kv[:, :halo], "seq", down)
    return before, kv, after


def across_y(array):
    return lax.all_gather(array, "tp", axis_index_groups=[[0, 2], [1, 3]], tiled=True)


def halves(array):
    return array.reshape((2, array.shape[0] // 2) + array.shape[1:])


def exchange_scratch(half, *kinds):
    shapes = []
    for kind in kinds:
        if kind == "total":
            shapes += Total.SHAPES(half)
        elif kind[0] == "heads":
            shapes += Heads.scratch(kind[1], 256, 1024)
        else:
            shape, dtype = kind
            shapes.append(pltpu.VMEM(shape, dtype))
    return shapes


def reaches_far(n_seq, source_document, target_document):
    source_docs = source_document.reshape(n_seq, -1)
    target_docs = target_document.reshape(n_seq, -1)

    def smallest(docs):
        return jnp.min(jnp.where(docs >= 0, docs, 2**30), axis=1)

    lows = jnp.minimum(smallest(source_docs), smallest(target_docs))
    highs = jnp.maximum(jnp.max(source_docs, axis=1), jnp.max(target_docs, axis=1))
    after_low = jnp.concatenate([lows[1:], jnp.full((1,), 2**30, jnp.int32)])[:, None]
    before_high = jnp.concatenate([jnp.full((1,), -1, jnp.int32), highs[:-1]])[:, None]
    far = False
    for docs in (source_docs, target_docs):
        half = docs.shape[1] // 2
        far = far | jnp.any(docs[:, :half] >= after_low)
        far = far | jnp.any((docs[:, half:] >= 0) & (docs[:, half:] <= before_high))
    return far


def on_device(n_seq, *args):
    far = reaches_far(n_seq, args[2], args[3])
    near = jnp.logical_not(far)
    return lax.cond(near, partial(on_device_with, n_seq, False), partial(on_device_with, n_seq, True), *args)


def on_device_with(
    n_seq,
    wide,
    source,
    target,
    source_document,
    target_document,
    cotangent,
    encoder_attention,
    encoder_mixing,
    encoder_gains,
    encoder_inner,
    encoder_outer,
    encoder_prefix,
    encoder_down,
    encoder_up,
    decoder_attention,
    decoder_mixing,
    decoder_prefix,
    cross_query,
    cross_memory,
    cross_mixing,
    cross_prefix,
    decoder_gains,
    decoder_inner,
    decoder_outer,
    decoder_down,
    decoder_up,
):
    ids = iter(range(1 + 16 * int(wide), 100))
    source_rows, width = source.shape
    target_rows = target.shape[0]
    cols = encoder_mixing.shape[0]
    hidden = encoder_inner.shape[1]
    adapt = encoder_down.shape[1]
    source_halo = source_rows if wide else source_rows // 2
    target_halo = target_rows if wide else target_rows // 2
    source_half, target_half = source_rows // 2, target_rows // 2
    source_n, target_n = source_half // SEGMENT, target_half // SEGMENT
    chunk = 2 * SEGMENT

    encoder_wo, decoder_wo, cross_wo = map(across_y, (encoder_mixing, decoder_mixing, cross_mixing))

    def padded(prefix):
        return jnp.pad(prefix, ((0, 0), (0, PREFIX_ROWS - prefix.shape[1]), (0, 0)))

    encoder_prefix, decoder_prefix, cross_prefix = map(padded, (encoder_prefix, decoder_prefix, cross_prefix))

    encoder_q, encoder_kv = project(source, encoder_attention)
    encoder_parts = halo_parts(encoder_kv, source_halo)
    decoder_q, decoder_kv = project(target, decoder_attention)
    decoder_kv, *encoder_parts = lax.optimization_barrier((decoder_kv, *encoder_parts))
    decoder_parts = halo_parts(decoder_kv, target_halo)

    encoder_docs = document_plan(
        source_document, source_document, source_rows, source_rows, source_halo, QUERY_BLOCK, False
    )
    decoder_docs = document_plan(
        target_document, target_document, target_rows, target_rows, target_halo, QUERY_BLOCK, True
    )
    cross_docs = document_plan(
        target_document, source_document, target_rows, source_rows, source_halo, QUERY_BLOCK, False
    )
    own_target = lax.dynamic_slice_in_dim(target_document, lax.axis_index("seq") * target_rows, target_rows)
    real = halves((own_target >= 0).astype(F32)[:, None])

    decoder_wide, decoder_low, decoder_total = attend(
        decoder_q, decoder_parts, decoder_prefix, decoder_docs, True
    )
    encoder_wide, encoder_low, encoder_total = attend(
        encoder_q, encoder_parts, encoder_prefix, encoder_docs, False
    )
    gathered_source = ((source_half, width), F32)
    gathered_target = ((target_half, width), F32)
    source_low = ((2, source_half, width), BF16)
    target_low = ((2, target_half, width), BF16)
    source_cols = ((2, source_half, cols), BF16)
    target_cols = ((2, target_half, cols), BF16)
    slopes = [((source_n, chunk, hidden + adapt), BF16), ((2, source_half, adapt), BF16)]
    inner_buf, outer_buf = ((width, hidden + adapt), BF16), ((hidden + adapt, width), BF16)
    mixing_buf = ((2 * cols, width), BF16)

    def whole(*arrays):
        return [(array.shape, array.dtype) for array in arrays]

    halo_cols = ((2, source_halo, cols), BF16)
    kv_cols = ((2, source_rows, cols), BF16)
    stored = [gathered_source, gathered_source, source_low, *slopes, kv_cols]
    stored_target = [gathered_target, gathered_target, target_cols]
    args = (
        halves(encoder_low), halves(source), encoder_gains, encoder_wo, encoder_inner, encoder_outer,
        encoder_down, encoder_up, cross_memory, halves(decoder_low), halves(target), decoder_gains,
        decoder_wo, cross_query,
    )
    loads = [
        *whole(args[0]), ((source_half, width), BF16), *whole(args[2]), mixing_buf, inner_buf, outer_buf,
        ((width, 2 * cols), BF16), *whole(args[9]), ((target_half, width), BF16), *whole(args[11]), mixing_buf,
        *whole(args[13]),
    ]
    (
        e1, e3, encoder_hidden, encoder_slope, encoder_side, cross_kv, cross_before, cross_after, t1, t2, cross_q,
    ) = exchange_call(
        partial(forward_kernel, n_seq, source_halo),
        next(ids),
        args,
        loads,
        [*stored, halo_cols, halo_cols, *stored_target],
        exchange_scratch(
            source_half,
            *stored,
            *stored_target,
            ("heads", source_half),
            gathered_source,
            "total",
            source_low,
            ("heads", target_half),
            target_low,
        ),
        2 + 1 + 2 + 1 + (4 if wide else 2) + 2 + 1,
        9,
        source_n,
        2 * source_rows * width * (2 * hidden + 2 * adapt + 6 * cols),
    )
    cross_query, cross_q = lax.optimization_barrier((cross_query, cross_q))
    cross_query_pair = across_y(cross_query)
    cross_parts = (cross_before, cross_kv, cross_after)
    cross_q = cross_q.reshape(target_rows, cols)
    cross_wide, cross_low, cross_total = attend(cross_q, cross_parts, cross_prefix, cross_docs, False)

    terms = ((2 * width, adapt), BF16)
    sums = [((width, adapt), F32), ((adapt, width), F32)]
    args = (
        halves(cross_low), t2, real, halves(cotangent), decoder_gains, cross_wo, decoder_inner,
        decoder_outer, decoder_down, decoder_up, cross_mixing,
    )
    loads = [
        *whole(args[0], args[1]), ((target_half, 1), F32), ((target_half, width), BF16), *whole(args[4]),
        mixing_buf, inner_buf, outer_buf, *whole(args[10]),
    ]
    stored = [gathered_target, target_cols, terms]
    decoded, g2, cross_da, decoder_terms = exchange_call(
        partial(decoder_chain_kernel, n_seq),
        next(ids),
        args,
        loads,
        [((2, target_half, width), F32), *stored],
        exchange_scratch(
            target_half,
            *stored,
            gathered_target,
            ("heads", target_half),
            gathered_target,
            gathered_target,
            gathered_target,
            target_low,
            target_low,
            target_low,
            ((target_n, chunk, hidden + adapt), BF16),
            ((2, target_half, adapt), BF16),
            ((2, target_half, adapt), BF16),
            "total",
            "total",
        ),
        2 + 1 + 2 + 1 + 1 + 2 + 1,
        4,
        target_n,
        2 * target_rows * width * (4 * hidden + 6 * adapt + 2 * cols),
    )
    cross_dq, cross_dbefore, cross_dkv, cross_dafter, cross_prefix_terms = attend_back(
        cross_q, cross_da.reshape(target_rows, cols), cross_wide, cross_total, cross_parts, cross_prefix,
        cross_docs, False,
    )
    args = (
        cross_dbefore, cross_dafter, cross_dkv, cross_memory, e3, e1, encoder_gains, encoder_hidden,
        encoder_slope, encoder_side, encoder_inner, encoder_outer, encoder_down, encoder_up,
        encoder_mixing, halves(cross_dq), g2, t1, decoder_gains, cross_query_pair, decoder_mixing,
        decoder_terms,
    )
    loads = [
        *whole(*args[:3]), ((width, 2 * cols), BF16), *whole(*args[4:10]), inner_buf, outer_buf, *whole(*args[14:19]),
        ((width, 2 * cols), BF16), *whole(*args[20:]),
    ]
    stored = [gathered_source, source_cols, terms, gathered_target, target_cols, *sums]
    (
        encoder_g1, encoder_da, encoder_terms, decoder_g1, decoder_da, decoder_down_gradient, decoder_up_gradient,
    ) = exchange_call(
        partial(backward_kernel, n_seq, source_halo),
        next(ids),
        args,
        loads,
        stored,
        exchange_scratch(
            source_half,
            *stored,
            halo_cols,
            halo_cols,
            ((2, 2, SEGMENT, cols), BF16),
            gathered_source,
            source_low,
            source_low,
            ((2, source_half, adapt), BF16),
            "total",
            "total",
            target_low,
        )
        + exchange_scratch(target_half, ("heads", target_half))
        + SeqSum.scratch(n_seq, 2 * width)[1:],
        (4 if wide else 2) + 2 + 1 + 2 + 1 + 2 + 1,
        7,
        source_n,
        2 * source_rows * width * (2 * hidden + 4 * adapt + 4 * cols),
    )
    ddq, ddbefore, ddkv, ddafter, decoder_prefix_terms = attend_back(
        decoder_q, decoder_da.reshape(target_rows, cols), decoder_wide, decoder_total, decoder_parts,
        decoder_prefix, decoder_docs, True,
    )
    edq, edbefore, edkv, edafter, encoder_prefix_terms = attend_back(
        encoder_q, encoder_da.reshape(source_rows, cols), encoder_wide, encoder_total, encoder_parts,
        encoder_prefix, encoder_docs, False,
    )
    args = (
        edbefore, edafter, halves(edq), edkv, encoder_attention, encoder_g1,
        ddbefore, ddafter, halves(ddq), ddkv, decoder_attention, decoder_g1,
        encoder_terms, encoder_prefix_terms, decoder_prefix_terms, cross_prefix_terms,
    )
    loads = whole(*args[:12])
    loads[4] = loads[10] = ((width, 3 * cols), BF16)
    prefix_sum = ((2, PREFIX, cols), F32)
    results = [*sums, prefix_sum, prefix_sum, prefix_sum]
    seq_rows = 2 * width + 512
    (
        source_gradient, target_gradient, encoder_down_gradient, encoder_up_gradient, encoder_prefix_gradient,
        decoder_prefix_gradient, cross_prefix_gradient,
    ) = exchange_call(
        partial(input_back_kernel, n_seq, (source_halo, target_halo)),
        next(ids),
        args,
        loads,
        [((2, source_half, width), F32), ((2, target_half, width), F32), *results],
        exchange_scratch(source_half, gathered_source, gathered_target, *results)
        + exchange_scratch(source_half, halo_cols, halo_cols, ((2, 2, SEGMENT, cols), BF16), "total")
        + exchange_scratch(
            target_half,
            ((2, target_halo, cols), BF16),
            ((2, target_halo, cols), BF16),
            ((2, 2, SEGMENT, cols), BF16),
            "total",
        )
        + SeqSum.scratch(n_seq, seq_rows),
        2 * ((4 if wide else 2) + 2 + 1),
        7,
        source_n,
        6 * (source_rows + target_rows) * width * cols,
    )
    source_gradient = source_gradient.reshape(source_rows, width)
    target_gradient = target_gradient.reshape(target_rows, width)

    weight_totals = (
        encoder_prefix_gradient,
        encoder_down_gradient,
        encoder_up_gradient,
        decoder_prefix_gradient,
        cross_prefix_gradient,
        decoder_down_gradient,
        decoder_up_gradient,
    )
    return (decoded.reshape(target_rows, width), source_gradient, target_gradient) + tuple(weight_totals)


def solution(mesh):
    return jax.shard_map(
        partial(on_device, mesh.shape["seq"]),
        mesh=mesh,
        in_specs=(
            P("seq", None),
            P("seq", None),
            P(),
            P(),
            P("seq", None),
            P(None, None, "tp"),
            P("tp", None),
            P(),
            P(None, "tp"),
            P("tp", None),
            P(None, None, "tp"),
            P(None, "tp"),
            P("tp", None),
            P(None, None, "tp"),
            P("tp", None),
            P(None, None, "tp"),
            P(None, "tp"),
            P(None, None, "tp"),
            P("tp", None),
            P(None, None, "tp"),
            P(),
            P(None, "tp"),
            P("tp", None),
            P(None, "tp"),
            P("tp", None),
        ),
        out_specs=(
            P("seq", None),
            P("seq", None),
            P("seq", None),
            P(None, None, "tp"),
            P(None, "tp"),
            P("tp", None),
            P(None, None, "tp"),
            P(None, None, "tp"),
            P(None, "tp"),
            P("tp", None),
        ),
        check_vma=False,
    )
```
